32 devices in a mesh: cluster: 4 (over z), member: 8 (over y, x, core).
Axes of the slice: x: 2, y: 2, z: 4, core: 2. Of those that a mesh axis runs over, the one named last changes fastest.
Arguments:
- factors: float32 [64, 1024, 1024], P(('cluster', 'member')), as said below
- panels: float32 [64, 1024, 256], P(('cluster', 'member')), may hold values from -0.09375 to 0.09375
- sizes: int32 [64], P(('cluster', 'member')), may hold values from 512 to 1024
- glue_index: int32 [64, 256], P(('cluster', 'member')), may hold values from 0 to 1023, as said below
- loads: float32 [4096, 256], P(('cluster', 'member')), may hold values from -6 to 6
Outputs:
- dual_rows: float32 [4096, 1024], P(('cluster', 'member'))
- products: float32 [4096, 256], P(('cluster', 'member'))
The draws below stay inside these ranges and needn't reach their ends.
Inputs may be any that keep to these rules, and one draw needn't show every extreme that they name: `glue_index`: the 256 entries of one subdomain are distinct; at most 64 of them lie in any one aligned block of 1024 // 8 dual rows, and every subdomain has 64 in some block. `factors`: strictly upper entries are zero; diagonal entries positive.
All inputs are finite; a program needn't handle non-finite values.
Results may differ from the reference program's by a relative error of at most 0.0003.
Values sent between devices are 32-bit elements; how exact they have to be, the bound alone decides.
No kernel may reach another device: no remote copies, remote signals or barrier semaphores. Data moves between devices by JAX's collectives and lax.ppermute only.
A program may use at most 192 MiB of HBM per device.

```python
import math
import jax
import jax.numpy as jnp
from jax import lax

ORDER = 1024
PANEL = 256
NDUAL = 1024
IFACE = 8
SUB_DEV = 2
NRHS = 256
SUBS = 64
ALLDUAL = 4096
N_CLUSTER = 4
N_MEMBER = 8


def draw_factors(key, part):
    key_diag, key_lower = jax.random.split(key)
    diagonal = jax.random.uniform(key_diag, (SUBS, ORDER), jnp.float32, 1.0, 2.0)
    lower_part = 0.4 * jax.random.normal(key_lower, (SUBS, ORDER, ORDER), jnp.float32) / math.sqrt(ORDER)
    strict = jnp.tril(lower_part, -1)
    return strict + diagonal[:, :, None] * jnp.eye(ORDER, dtype=jnp.float32)


def draw_glue_index(key, part):
    row_share = NDUAL // N_MEMBER
    capacity = 2 * PANEL // N_MEMBER
    pair_count = N_MEMBER // 2
    key_split, key_order, key_rank, key_pick = jax.random.split(jax.random.fold_in(key, 7), 4)
    first_share = jax.random.randint(key_split, (SUBS, pair_count), 0, capacity + 1)
    first_share = first_share.at[:, 0].set(capacity)
    paired = jnp.stack([first_share, capacity - first_share], axis=-1).reshape(SUBS, N_MEMBER)
    order_keys = jax.random.split(key_order, SUBS)
    block_order = jax.vmap(lambda one_key: jax.random.permutation(one_key, N_MEMBER))(order_keys).astype(jnp.int32)
    inverse = jnp.argsort(block_order, axis=1).astype(jnp.int32)
    counts = jnp.take_along_axis(paired, inverse, axis=1)
    scores = jax.random.randint(key_rank, (SUBS, N_MEMBER, row_share), 0, 2 ** 20) * row_share
    scores = scores + lax.broadcasted_iota(jnp.int32, (SUBS, N_MEMBER, row_share), 2)
    ranks = jnp.argsort(jnp.argsort(scores, axis=2), axis=2).astype(jnp.int32)
    chosen = (ranks < counts[:, :, None]).reshape(SUBS, NDUAL)
    picking = jax.random.randint(key_pick, (SUBS, NDUAL), 0, 2 ** 19) * NDUAL
    picking = picking + lax.broadcasted_iota(jnp.int32, (SUBS, NDUAL), 1)
    ordering = jnp.where(chosen, 0, 2 ** 30).astype(jnp.int32) + picking
    return jnp.argsort(ordering, axis=1)[:, :PANEL].astype(jnp.int32)


def touch_ends(drawn, rng, smallest, high):
    longest = drawn.shape.index(max(drawn.shape))
    spots = []
    for shift in (0, 1):
        where = [jax.random.randint(jax.random.fold_in(rng, axis), (), 0, length) for axis, length in enumerate(drawn.shape)]
        where[longest] = (where[longest] + shift) % drawn.shape[longest]
        spots.append(tuple(where))
    return drawn.at[spots[0]].set(smallest).at[spots[1]].set(high)


def shard_levels(stream_key, extent, pieces, least, largest):
    loudness = 1.0
    for dim, blocks in pieces:
        draws = jax.random.uniform(jax.random.fold_in(jax.random.fold_in(stream_key, 6), dim), (blocks,), jnp.float32, least / len(pieces), largest / len(pieces))
        loudness = loudness * jnp.repeat(jnp.exp(draws), extent[dim] // blocks).reshape((-1,) + (1,) * (len(extent) - 1 - dim))
    return loudness


def bell_draw(stream_key, extent, deviation, limit, shards=(), held_as=jnp.bfloat16):
    values = jax.random.normal(stream_key, extent, jnp.float32) * deviation
    if len(shards) > 0:
        values = shard_levels(stream_key, extent, shards, -0.22, 0.18) * values
    return jnp.clip(values, min=-limit, max=limit).astype(held_as)


def setup_inputs(seed: int = 0) -> dict:
    key_of = jax.random.split(jax.random.key(seed), 6)
    return {
        "factors": draw_factors(jax.random.fold_in(key_of[5], 71), 0),
        "panels": bell_draw(key_of[1], (SUBS, ORDER, PANEL), (ORDER * SUB_DEV * N_MEMBER * PANEL // NDUAL) ** -0.5, 0.09375, ((0, 32),), jnp.float32),
        "sizes": touch_ends(jax.random.randint(key_of[2], (SUBS,), ORDER // 2, ORDER + 1), jax.random.fold_in(key_of[2], 1), ORDER // 2, ORDER).astype(jnp.int32),
        "glue_index": draw_glue_index(jax.random.fold_in(key_of[5], 71), 0),
        "loads": bell_draw(key_of[4], (ALLDUAL, NRHS), 1.0, 6.0, ((0, 32),), jnp.float32),
    }


def one_subdomain(items):
    factor, gluing, live_size = items
    factor_order = factor.shape[0]
    row_ids = lax.broadcasted_iota(jnp.int32, (factor_order, factor_order), 0)
    col_ids = lax.broadcasted_iota(jnp.int32, (factor_order, factor_order), 1)
    keeping = (row_ids < live_size) & (col_ids < live_size) & (col_ids <= row_ids)
    live_factor = jnp.where(keeping, factor, (row_ids == col_ids).astype(jnp.float32))
    panel_rows = lax.broadcasted_iota(jnp.int32, gluing.shape, 0)
    live_panel = jnp.where(panel_rows < live_size, gluing, jnp.zeros_like(gluing))
    solved = lax.linalg.triangular_solve(live_factor, live_panel, left_side=True, lower=True)
    return lax.dot_general(solved.astype(jnp.float32), solved.astype(jnp.float32), (((0,), (0,)), ((), ())), precision=lax.Precision.HIGHEST, preferred_element_type=jnp.float32)

def reference(factors, panels, sizes, glue_index, loads):
    local_dual = lax.map(one_subdomain, (factors, panels, sizes))
    per_cluster = SUB_DEV * N_MEMBER
    cluster_of = (jnp.arange(SUBS, dtype=jnp.int32) // per_cluster).astype(jnp.int32)
    assembled = jnp.zeros((N_CLUSTER, NDUAL, NDUAL), jnp.float32)
    assembled = assembled.at[cluster_of[:, None, None], glue_index[:, :, None], glue_index[:, None, :]].add(local_dual)
    dual_rows = assembled.reshape(N_CLUSTER * NDUAL, NDUAL)
    raw = jnp.einsum('cij,cjr->cir', assembled, loads.reshape(N_CLUSTER, NDUAL, NRHS), precision=lax.Precision.HIGHEST)
    row_share = NDUAL // N_MEMBER
    blocked = raw.reshape(N_CLUSTER, N_MEMBER, row_share, NRHS)
    previous_rows = jnp.roll(blocked, 1, axis=0)[:, :, row_share - IFACE:, :]
    next_rows = jnp.roll(blocked, -1, axis=0)[:, :, :IFACE, :]
    between = jnp.zeros((N_CLUSTER, N_MEMBER, row_share - 2 * IFACE, NRHS), jnp.float32)
    products = blocked + jnp.concatenate([previous_rows, between, next_rows], axis=2)
    return (dual_rows, products.reshape(N_CLUSTER * NDUAL, NRHS))
```

```python
import functools
import jax, jax.numpy as jnp
from jax import lax
from jax.experimental import pallas as pl
from jax.experimental.pallas import tpu as pltpu
F32, BF = jnp.float32, jnp.bfloat16
from jax.sharding import PartitionSpec as P

STRIDE, BASE = 128, 32
NDUAL, IFACE = 1024, 8

def split(v):
    hi = v.astype(BF)
    return hi, (v - hi.astype(F32)).astype(BF)

def mm(a, b, dims=(((1,), (0,)), ((), ()))):
    return lax.dot_general(a, b, dims, preferred_element_type=F32)

def mm3(a, b):
    ah, al = a
    bh, bl = b
    return mm(ah, bh) + (mm(al, bh) + mm(ah, bl))

def iota(shape, dim):
    return lax.broadcasted_iota(jnp.int32, shape, dim)

def invert_blocks(blocks):
    count = len(blocks)
    slabs = STRIDE // BASE
    lane = iota((BASE, STRIDE), 1)
    row = iota((BASE, STRIDE), 0)
    group, local = lane // BASE, lane % BASE
    compact = []
    for block in blocks:
        packed = block[:BASE]
        for q in range(1, slabs):
            packed = jnp.where(group == q, block[q * BASE:(q + 1) * BASE], packed)
        compact.append(packed)
    scaled, recips = [], []
    for packed in compact:
        diag = jnp.sum(jnp.where(row == local, packed, 0.0), axis=0, keepdims=True)
        recip = 1.0 / diag
        recips.append(recip)
        scaled.append(jnp.where(row > local, packed * recip, 0.0))
    parts = BASE // 8
    eye = (row == local).astype(F32)
    lane8 = iota((8, STRIDE), 1)
    base8 = (lane8 // BASE) * BASE
    row8 = iota((8, STRIDE), 0)
    out = []
    for k in range(count):
        work = [eye[g * 8:(g + 1) * 8] for g in range(parts)]
        for j in range(BASE - 1):
            pivot = work[j // 8][j % 8:j % 8 + 1]
            for g in range(j // 8, parts):
                column = jnp.take_along_axis(scaled[k][g * 8:(g + 1) * 8], base8 + j, axis=1, mode="promise_in_bounds")
                work[g] = work[g] - column * pivot
        for g in range(parts):
            rec = jnp.take_along_axis(jnp.broadcast_to(recips[k], (8, STRIDE)), base8 + row8 + g * 8, axis=1, mode="promise_in_bounds")
            work[g] = work[g] * rec
        out.append(jnp.concatenate(work, axis=0))
    full_lane = iota((STRIDE, STRIDE), 1)
    full_row = iota((STRIDE, STRIDE), 0)
    result = []
    for block, packed in zip(blocks, out):
        inverse = jnp.concatenate([jnp.where(group == q, packed, 0.0) for q in range(slabs)], axis=0)
        size = BASE
        while size < STRIDE:
            pick = ((full_row // size) % 2 == 1) & (full_lane // size == full_row // size - 1)
            below = jnp.where(pick, block, 0.0)
            inv2 = split(inverse)
            inverse = inverse - mm3(inv2, split(mm3(split(below), inv2)))
            size *= 2
        result.append(inverse)
    return result

def solve_kernel(members, sizes_ref, glue_ref, f_ref, p_ref, out_ref, rest, solved_hi, solved_lo):
    subs, order, width = p_ref.shape
    steps = order // STRIDE
    row = iota((STRIDE, STRIDE), 0)
    col = iota((STRIDE, STRIDE), 1)
    prow = iota((STRIDE, width), 0)
    inverses = []
    for s in range(subs):
        blocks = []
        for j in range(steps):
            a = j * STRIDE
            d = f_ref[s, a:a + STRIDE, a:a + STRIDE]
            keep = (row + a < sizes_ref[s]) & (col <= row)
            blocks.append(jnp.where(keep, d, (row == col).astype(F32)))
        inverses.append([split(v) for v in invert_blocks(blocks)])
    for j in range(steps):
        a = j * STRIDE
        for s in range(subs):
            now = (p_ref if j == 0 else rest)[s, a:a + STRIDE]
            now = jnp.where(prow + a < sizes_ref[s], now, 0.0)
            x = split(mm3(inverses[s][j], split(now)))
            solved_hi[s, a:a + STRIDE] = x[0]
            solved_lo[s, a:a + STRIDE] = x[1]
            for i in range(j + 1, steps):
                b = i * STRIDE
                before = (p_ref if j == 0 else rest)[s, b:b + STRIDE]
                rest[s, b:b + STRIDE] = before - mm3(split(f_ref[s, b:b + STRIDE, a:a + STRIDE]), x)
    capacity = 2 * width // members
    share = out_ref.shape[1]
    glue = glue_ref[...]
    dims = (((0,), (0,)), ((), ()))
    before = (iota((width, width), 0) < iota((width, width), 1)).astype(BF)
    dual_order = NDUAL
    for s in range(subs):
        hi, lo = solved_hi[s], solved_lo[s]
        cross = mm(hi, lo, dims)
        dual = mm(hi, hi, dims) + (cross + cross.T)
        dh, dl = split(dual)
        line = glue[s:s + 1]
        owner = line // (dual_order // members)
        owners = (iota((members, width), 0) == owner)
        ranks = mm(owners.astype(BF), before)
        rank = jnp.sum(jnp.where(owners, ranks, 0.0), axis=0, keepdims=True).astype(jnp.int32)
        target = owner * capacity + rank
        dispatch = (iota((members * capacity, width), 0) == target).astype(BF)
        values = mm(dispatch, dh) + mm(dispatch, dl)
        for k in range(members):
            out_ref[k, s * capacity:(s + 1) * capacity] = values[k * capacity:(k + 1) * capacity]

def solve(factors, panels, sizes, glue, members):
    subs, order, width = panels.shape
    capacity = 2 * width // members
    vm = pl.BlockSpec(memory_space=pltpu.VMEM)
    return pl.pallas_call(
        functools.partial(solve_kernel, members),
        out_shape=jax.ShapeDtypeStruct((members, subs * capacity, width), F32),
        in_specs=[pl.BlockSpec(memory_space=pltpu.SMEM), vm, vm, vm],
        out_specs=vm,
        scratch_shapes=[pltpu.VMEM((subs, order, width), F32), pltpu.VMEM((subs, order, width), BF), pltpu.VMEM((subs, order, width), BF)],
        compiler_params=pltpu.CompilerParams(vmem_limit_bytes=48 << 20),
        cost_estimate=pl.CostEstimate(flops=20_000_000_000, bytes_accessed=12 << 20, transcendentals=0),
        name="solve",
    )(sizes, glue, factors, panels)


def routes_kernel(subs, place_ref, got_ref, line_ref, rows_ref, high_ref, low_ref):
    members, block, nrhs = got_ref.shape
    share = NDUAL // members
    slots = rows_ref.shape[2]
    width = nrhs
    capacity = slots // subs
    loads = jnp.concatenate([got_ref[k, :share] for k in range(members)], axis=0)
    loads_high, loads_low = split(loads)
    lines = jnp.concatenate([got_ref[k, share:share + subs] for k in range(members)], axis=0)
    line_ref[...] = lines.astype(jnp.int32)
    glue = lines.astype(jnp.int32)
    standing = lines.T.astype(jnp.int32)
    first = place_ref[0] * share
    mine = ((glue >= first) & (glue < first + share))
    before = (iota((width, width), 0) < iota((width, width), 1)).astype(BF)
    ranks = mm(mine.astype(BF), before).astype(jnp.int32)
    ranks = jnp.where(mine, ranks, -1)
    for k in range(members):
        for s in range(subs):
            i = k * subs + s
            at_row = (iota((share, width), 0) + first == glue[i:i + 1]).astype(BF)
            rank = jnp.where(ranks[i:i + 1] >= 0, ranks[i:i + 1] + s * capacity, -1)
            at_slot = (iota((slots, width), 0) == rank).astype(BF)
            rows_ref[k, s * share:(s + 1) * share] = mm(at_row, at_slot, (((1,), (1,)), ((), ()))).astype(BF)
            spread = (iota((width, NDUAL), 1) == standing[:, i:i + 1]).astype(BF)
            high_ref[i] = mm(spread, loads_high).astype(BF)
            low_ref[i] = mm(spread, loads_low).astype(BF)


def raw_kernel(subs, values_ref, rows_ref, high_ref, low_ref, raw_ref, first_ref, last_ref, wide_high, wide_low):
    members, slots, width = values_ref.shape
    share, nrhs = raw_ref.shape
    total = jnp.zeros((share, nrhs), F32)
    for k in range(members):
        vh, vl = split(values_ref[k])
        rows = rows_ref[k]
        wh = mm(rows, vh).astype(BF)
        wl = mm(rows, vl).astype(BF)
        for s in range(subs):
            i = k * subs + s
            part = (wh[s * share:(s + 1) * share], wl[s * share:(s + 1) * share])
            wide_high[i] = part[0]
            wide_low[i] = part[1]
            total = total + mm3(part, (high_ref[i], low_ref[i]))
    raw_ref[...] = total
    first_ref[...] = total[:IFACE]
    last_ref[...] = total[share - IFACE:]


def place_kernel(line_ref, wide_high, wide_low, dual_ref):
    count, share, width = wide_high.shape
    total = jnp.zeros(dual_ref.shape, F32)
    for i in range(count):
        columns = (iota((NDUAL, width), 0) == line_ref[i:i + 1]).astype(BF)
        dims = (((1,), (1,)), ((), ()))
        total = total + (mm(wide_high[i], columns, dims) + mm(wide_low[i], columns, dims))
    dual_ref[...] = total


def call(kernel, outs, args, flops, name, smem=0):
    vm = pl.BlockSpec(memory_space=pltpu.VMEM)
    specs = [pl.BlockSpec(memory_space=pltpu.SMEM)] * smem + [vm] * (len(args) - smem)
    return pl.pallas_call(
        kernel,
        out_shape=outs,
        in_specs=specs,
        out_specs=jax.tree.map(lambda _: vm, outs),
        compiler_params=pltpu.CompilerParams(vmem_limit_bytes=48 << 20),
        cost_estimate=pl.CostEstimate(flops=flops, bytes_accessed=4 << 20, transcendentals=0),
        name=name,
    )(*args)


def on_device(factors, panels, sizes, glue_index, loads):
    members = lax.axis_size("member")
    subs, order, width = panels.shape
    share, nrhs = loads.shape
    capacity = 2 * width // members
    slots = subs * capacity
    count = members * subs
    shape = jax.ShapeDtypeStruct
    padding = jnp.zeros((-subs % 8, width), F32)
    mine = jnp.concatenate([loads, glue_index.astype(F32), padding], axis=0)
    everyone = jnp.broadcast_to(mine[None], (members,) + mine.shape)
    got = lax.all_to_all(everyone, "member", split_axis=0, concat_axis=0, tiled=True)
    values = solve(factors, panels, sizes, glue_index, members)
    place = lax.axis_index("member").astype(jnp.int32).reshape(1)
    lines, rows, high, low = call(
        functools.partial(routes_kernel, subs),
        (
            shape((count, width), jnp.int32),
            shape((members, subs * share, slots), BF),
            shape((count, width, nrhs), BF),
            shape((count, width, nrhs), BF),
        ),
        (place, got),
        6_000_000_000,
        "routes",
        smem=1,
    )
    values = lax.all_to_all(values, "member", split_axis=0, concat_axis=0, tiled=True)
    raw, first, last, wide_high, wide_low = call(
        functools.partial(raw_kernel, subs),
        (
            shape((share, nrhs), F32),
            shape((IFACE, nrhs), F32),
            shape((IFACE, nrhs), F32),
            shape((count, share, width), BF),
            shape((count, share, width), BF),
        ),
        (values, rows, high, low),
        2_000_000_000,
        "raw",
    )
    peers = lax.axis_size("cluster")
    up = [(i, (i + 1) % peers) for i in range(peers)]
    down = [(j, i) for i, j in up]
    before = lax.ppermute(last, "cluster", up)
    after = lax.ppermute(first, "cluster", down)
    dual_rows = call(
        place_kernel, shape((share, NDUAL), F32), (lines, wide_high, wide_low), 4_000_000_000, "place"
    )
    between = jnp.zeros((share - 2 * IFACE, nrhs), F32)
    products = raw + jnp.concatenate([before, between, after], axis=0)
    return (dual_rows, products)


def solution(mesh):
    shards = ("cluster", "member")
    return jax.shard_map(
        on_device,
        mesh=mesh,
        in_specs=(P(shards, None, None), P(shards, None, None), P(shards), P(shards, None), P(shards, None)),
        out_specs=(P(shards, None), P(shards, None)),
        check_vma=False,
    )
```

```python
import functools
import jax, jax.numpy as jnp
from jax import lax
from jax.experimental import pallas as pl
from jax.experimental.pallas import tpu as pltpu
F32, BF = jnp.float32, jnp.bfloat16
from jax.sharding import PartitionSpec as P

STRIDE, BASE = 128, 16
NDUAL, IFACE = 1024, 8

def split(v):
    hi = v.astype(BF)
    return hi, (v - hi.astype(F32)).astype(BF)

def mm(a, b, dims=(((1,), (0,)), ((), ()))):
    return lax.dot_general(a, b, dims, preferred_element_type=F32)

def mm3(a, b):
    ah, al = a
    bh, bl = b
    return mm(ah, bh) + (mm(al, bh) + mm(ah, bl))

def iota(shape, dim):
    return lax.broadcasted_iota(jnp.int32, shape, dim)

def mmk(a, b):
    ah, al = a
    bh, bl = b
    return mm(jnp.concatenate([ah, al], axis=1), jnp.concatenate([bh, bh], axis=0)) + mm(ah, bl)


def turn(v, by):
    return pltpu.roll(v, by, 1)


def split32(v):
    hi = v.astype(BF).astype(F32)
    return hi, v - hi


def eliminate(packs):
    lane = iota((BASE, STRIDE), 1)
    row = iota((BASE, STRIDE), 0)
    local = lane % BASE
    parts = BASE // 8
    start = (iota((8, STRIDE), 1) // BASE) * BASE
    row8 = iota((8, STRIDE), 0)
    eye = (row == local).astype(F32)
    recips, works, pieces = [], [], []
    for packed in packs:
        diag = jnp.sum(jnp.where(row == local, packed, 0.0), axis=0, keepdims=True)
        recip = 1.0 / diag
        scaled = jnp.where(row > local, packed * recip, 0.0)
        recips.append(jnp.broadcast_to(recip, (8, STRIDE)))
        works.append([eye[g * 8:(g + 1) * 8] for g in range(parts)])
        pieces.append([scaled[g * 8:(g + 1) * 8] for g in range(parts)])
    for j in range(BASE - 1):
        for work, piece in zip(works, pieces):
            pivot = work[j // 8][j % 8:j % 8 + 1]
            for g in range((j + 1) // 8, parts):
                column = jnp.take_along_axis(piece[g], start + j, axis=1, mode="promise_in_bounds")
                work[g] = work[g] - column * pivot
    for work, recip in zip(works, recips):
        for g in range(parts):
            work[g] = work[g] * jnp.take_along_axis(recip, start + (row8 + g * 8), axis=1, mode="promise_in_bounds")
    return [jnp.concatenate(work, axis=0) for work in works]


def slabs_of(v, size):
    return [v[r:r + size] for r in range(0, v.shape[0], size)]


def invert_blocks(blocks):
    lane = iota((BASE, STRIDE), 1)
    packs = []
    for block in blocks:
        packed = block[:BASE]
        for q, slab in enumerate(slabs_of(block, BASE)):
            packed = jnp.where(lane // BASE == q, slab, packed) if q else packed
        packs.append(packed)
    inners = eliminate(packs)
    states = [[jnp.where(lane // BASE == q, inner, 0.0) for q in range(STRIDE // BASE)] for inner in inners]
    size = BASE
    while size < STRIDE:
        half = iota((STRIDE // 2, STRIDE), 1) // size
        even = half % 2 == 0
        pair = (half // 2 == iota((STRIDE // 2, STRIDE), 0) // size) & even
        products = []
        for block, slabs in zip(blocks, states):
            ch, cl = split32(jnp.where(pair, jnp.concatenate(slabs_of(block, size)[1::2], axis=0), 0.0))
            a = jnp.concatenate([ch + turn(cl, size), ch], axis=1).astype(BF)
            tops = [split(v) for v in slabs[0::2]]
            w = [v[0] for v in tops for _ in range(2)] + [v[1] for v in tops for _ in range(2)]
            products.append(mm(a, jnp.concatenate(w, axis=0)))
        belows = []
        for product, slabs in zip(products, states):
            xh, xl = split32(jnp.concatenate(slabs[1::2], axis=0))
            a = jnp.concatenate([xh + turn(xl, STRIDE - size), xh], axis=1).astype(BF)
            th, tl = split(product)
            w = [v for v in slabs_of(th, size) for _ in range(2)] + [v for v in slabs_of(tl, size) for _ in range(2)]
            belows.append(slabs_of(mm(a, jnp.concatenate(w, axis=0)), size))
        states = [
            [jnp.concatenate([top, low - add], axis=0) for top, low, add in zip(slabs[0::2], slabs[1::2], below)]
            for slabs, below in zip(states, belows)
        ]
        size *= 2
    return [slabs[0] for slabs in states]


BATCH = 16


def solve_kernel(members, sizes_ref, glue_ref, far_ref, p_ref, out_ref, rest, f_ref, corner_sems, strip_sems):
    subs, order, width = p_ref.shape
    wide = 2 * STRIDE
    corner_copies, strip_copies = [], {}
    for s in range(subs):
        for step, a in enumerate(range(0, order, wide)):
            square = (s, pl.ds(a, wide), pl.ds(a, wide))
            corner_copies.append(pltpu.make_async_copy(far_ref.at[square], f_ref.at[square], corner_sems.at[s, step]))
    for step, a in enumerate(range(0, order - wide, wide)):
        for s in range(subs):
            strip = (s, pl.ds(a + wide, order - a - wide), pl.ds(a, wide))
            strip_copies[s, a] = pltpu.make_async_copy(far_ref.at[strip], f_ref.at[strip], strip_sems.at[s, step])
    for copy in corner_copies:
        copy.start()
    for copy in strip_copies.values():
        copy.start()
    for copy in corner_copies:
        copy.wait()
    row = iota((STRIDE, STRIDE), 0)
    col = iota((STRIDE, STRIDE), 1)
    prow = iota((wide, width), 0)
    dims = (((0,), (0,)), ((), ()))
    squares = [jnp.zeros((width, width), F32)] * subs
    crosses = [jnp.zeros((width, width), F32)] * subs
    places = [(s, a) for a in range(0, order, STRIDE) for s in range(subs)]
    small = {}
    for first in range(0, len(places), BATCH):
        batch = places[first:first + BATCH]
        blocks = []
        for s, a in batch:
            d = f_ref[s, a:a + STRIDE, a:a + STRIDE]
            keep = (row + a < sizes_ref[s]) & (col <= row)
            blocks.append(jnp.where(keep, d, (row == col).astype(F32)))
        for place, inverse in zip(batch, invert_blocks(blocks)):
            small[place] = split(inverse)
    heads = [(s, a) for a in range(0, order, wide) for s in range(subs)]
    corners = []
    for s, a in heads:
        b = a + STRIDE
        corner = jnp.where(row + b < sizes_ref[s], f_ref[s, b:b + STRIDE, a:b], 0.0)
        corners.append(split(mmk(split(corner), small[s, a])))
    inverses = {}
    for (s, a), corner in zip(heads, corners):
        above, below = small[s, a], small[s, a + STRIDE]
        turned = split(-mmk(below, corner))
        blank = jnp.zeros((STRIDE, STRIDE), BF)
        inverses[s, a] = [
            jnp.concatenate([jnp.concatenate([u, blank], axis=1), jnp.concatenate([t, l], axis=1)], axis=0)
            for u, t, l in zip(above, turned, below)
        ]

    def source(a):
        return p_ref if a < wide else rest

    for a in range(0, order, wide):
        solved = []
        for s in range(subs):
            now = jnp.where(prow + a < sizes_ref[s], source(a)[s, a:a + wide], 0.0)
            solved.append(split(mm3(inverses[s, a], split(now))))
        if a + wide < order:
            for s in range(subs):
                strip_copies[s, a].wait()
        for c in range(a + wide, order, wide):
            for s in range(subs):
                rest[s, c:c + wide] = source(a)[s, c:c + wide] - mm3(split(f_ref[s, c:c + wide, a:a + wide]), solved[s])
        for s in range(subs):
            hi, lo = solved[s]
            squares[s] = squares[s] + mm(hi, hi, dims)
            crosses[s] = crosses[s] + mm(hi, lo, dims)
    capacity = 2 * width // members
    glue = glue_ref[...]
    before = (iota((width, width), 0) < iota((width, width), 1)).astype(BF)
    dual_order = NDUAL
    for s in range(subs):
        dh, dl = split(squares[s] + (crosses[s] + crosses[s].T))
        line = glue[s:s + 1]
        owner = line // (dual_order // members)
        owners = (iota((members, width), 0) == owner)
        ranks = mm(owners.astype(BF), before)
        rank = jnp.sum(jnp.where(owners, ranks, 0.0), axis=0, keepdims=True).astype(jnp.int32)
        target = owner * capacity + rank
        dispatch = (iota((members * capacity, width), 0) == target).astype(BF)
        values = mm(dispatch, dh) + mm(dispatch, dl)
        for k in range(members):
            out_ref[k, s * capacity:(s + 1) * capacity] = values[k * capacity:(k + 1) * capacity]

def solve(factors, panels, sizes, glue, members):
    subs, order, width = panels.shape
    capacity = 2 * width // members
    vm = pl.BlockSpec(memory_space=pltpu.VMEM)
    return pl.pallas_call(
        functools.partial(solve_kernel, members),
        out_shape=jax.ShapeDtypeStruct((members, subs * capacity, width), F32),
        in_specs=[pl.BlockSpec(memory_space=pltpu.SMEM), vm, pl.BlockSpec(memory_space=pltpu.HBM), vm],
        out_specs=vm,
        scratch_shapes=[
            pltpu.VMEM((subs, order, width), F32),
            pltpu.VMEM((subs, order, order), F32),
            pltpu.SemaphoreType.DMA((subs, order // (2 * STRIDE))),
            pltpu.SemaphoreType.DMA((subs, order // (2 * STRIDE))),
        ],
        compiler_params=pltpu.CompilerParams(vmem_limit_bytes=54 << 20),
        cost_estimate=pl.CostEstimate(flops=10_000_000_000, bytes_accessed=12 << 20, transcendentals=0),
        name="solve",
    )(sizes, glue, factors, panels)


def pack_kernel(loads_ref, glue_ref, out_ref):
    members, rows, nrhs = out_ref.shape
    half, lines = loads_ref.shape[0] // 2, glue_ref.shape[0] // 2
    blank = jnp.zeros((rows - half - lines, nrhs), F32)
    for k in range(members):
        part = k % 2
        out_ref[k, :half] = loads_ref[part * half:(part + 1) * half]
        line = glue_ref[part * lines:(part + 1) * lines].astype(F32)
        out_ref[k, half:] = jnp.concatenate([line, blank], axis=0)


def routes_kernel(subs, place_ref, own_ref, twin_ref, stand_ref, rows_ref, high_ref, low_ref):
    members, block, width = own_ref.shape
    share = NDUAL // members
    half, lines = share // 2, subs // 2
    slots = rows_ref.shape[2]
    capacity = slots // subs
    first_core = place_ref[0] % 2 == 0
    halves = (
        jnp.where(first_core, own_ref[...], twin_ref[...]),
        jnp.where(first_core, twin_ref[...], own_ref[...]),
    )
    glue = []
    for k in range(members):
        for part in range(2):
            row = k * share + part * half
            load = split(halves[part][k, :half])
            high_ref[row:row + half] = load[0]
            low_ref[row:row + half] = load[1]
            glue.append(halves[part][k, half:half + lines])
    glue = jnp.concatenate(glue, axis=0)
    stand_ref[...] = glue.T.astype(jnp.int32)
    glue = glue.astype(jnp.int32)
    first = place_ref[0] * share
    mine = (glue >= first) & (glue < first + share)
    before = (iota((width, width), 0) < iota((width, width), 1)).astype(BF)
    ranks = mm(mine.astype(BF), before).astype(jnp.int32)
    for k in range(members):
        for s in range(subs):
            i = k * subs + s
            at_row = (iota((share, width), 0) + first == glue[i:i + 1]).astype(BF)
            rank = jnp.where(mine[i:i + 1], ranks[i:i + 1] + s * capacity, -1)
            at_slot = (iota((slots, width), 0) == rank).astype(BF)
            rows_ref[k, s * share:(s + 1) * share] = mm(at_row, at_slot, (((1,), (1,)), ((), ()))).astype(BF)


def finish_kernel(subs, values_ref, rows_ref, stand_ref, high_ref, low_ref, dual_ref, raw_ref, first_ref, last_ref):
    members, slots, width = values_ref.shape
    share, nrhs = raw_ref.shape
    total = jnp.zeros((2 * share, NDUAL), F32)
    for k in range(members):
        moved = mm(rows_ref[k], jnp.concatenate(split(values_ref[k]), axis=1)).astype(BF)
        for s in range(subs):
            i = k * subs + s
            part = moved[s * share:(s + 1) * share]
            columns = (iota((width, NDUAL), 1) == stand_ref[:, i:i + 1]).astype(BF)
            total = total + mm(jnp.concatenate([part[:, :width], part[:, width:]], axis=0), columns)
    dual = total[:share] + total[share:]
    dual_ref[...] = dual
    raw = mm3(split(dual), (high_ref[...], low_ref[...]))
    raw_ref[...] = raw
    first_ref[...] = raw[:IFACE]
    last_ref[...] = raw[share - IFACE:]


def call(kernel, outs, args, flops, name, smem=0):
    vm = pl.BlockSpec(memory_space=pltpu.VMEM)
    specs = [pl.BlockSpec(memory_space=pltpu.SMEM)] * smem + [vm] * (len(args) - smem)
    return pl.pallas_call(
        kernel,
        out_shape=outs,
        in_specs=specs,
        out_specs=jax.tree.map(lambda _: vm, outs),
        compiler_params=pltpu.CompilerParams(vmem_limit_bytes=16 << 20),
        cost_estimate=pl.CostEstimate(flops=flops, bytes_accessed=4 << 20, transcendentals=0),
        name=name,
    )(*args)


def on_device(factors, panels, sizes, glue_index, loads):
    members = lax.axis_size("member")
    subs, order, width = panels.shape
    share, nrhs = loads.shape
    capacity = 2 * width // members
    slots = subs * capacity
    count = members * subs
    shape = jax.ShapeDtypeStruct
    packed = call(pack_kernel, shape((members, share // 2 + 8 * (-(-subs // 16)), nrhs), F32), (loads, glue_index), 1_000_000, "pack")
    own = lax.all_to_all(packed, "member", split_axis=0, concat_axis=0, tiled=True)
    values = solve(factors, panels, sizes, glue_index, members)
    twin = lax.ppermute(own, "member", [(i, i ^ 1) for i in range(members)])
    place = lax.axis_index("member").astype(jnp.int32).reshape(1)
    stand, rows, high, low = call(
        functools.partial(routes_kernel, subs),
        (
            shape((width, count), jnp.int32),
            shape((members, subs * share, slots), BF),
            shape((NDUAL, nrhs), BF),
            shape((NDUAL, nrhs), BF),
        ),
        (place, own, twin),
        2_000_000_000,
        "routes",
        smem=1,
    )
    values = lax.all_to_all(values, "member", split_axis=0, concat_axis=0, tiled=True)
    dual_rows, raw, first, last = call(
        functools.partial(finish_kernel, subs),
        (
            shape((share, NDUAL), F32),
            shape((share, nrhs), F32),
            shape((IFACE, nrhs), F32),
            shape((IFACE, nrhs), F32),
        ),
        (values, rows, stand, high, low),
        5_000_000_000,
        "finish",
    )
    peers = lax.axis_size("cluster")
    up = [(i, (i + 1) % peers) for i in range(peers)]
    down = [(j, i) for i, j in up]
    before = lax.ppermute(last, "cluster", up)
    after = lax.ppermute(first, "cluster", down)
    between = jnp.zeros((share - 2 * IFACE, nrhs), F32)
    products = raw + jnp.concatenate([before, between, after], axis=0)
    return (dual_rows, products)


def solution(mesh):
    shards = ("cluster", "member")
    return jax.shard_map(
        on_device,
        mesh=mesh,
        in_specs=(P(shards, None, None), P(shards, None, None), P(shards), P(shards, None), P(shards, None)),
        out_specs=(P(shards, None), P(shards, None)),
        check_vma=False,
    )
```

```python
import functools
import jax, jax.numpy as jnp
from jax import lax
from jax.experimental import pallas as pl
from jax.experimental.pallas import tpu as pltpu
F32, BF = jnp.float32, jnp.bfloat16
from jax.sharding import PartitionSpec as P

STRIDE, BASE = 128, 16
NDUAL, IFACE = 1024, 8

def split(v):
    hi = v.astype(BF)
    return hi, (v - hi.astype(F32)).astype(BF)

def mm(a, b, dims=(((1,), (0,)), ((), ()))):
    return lax.dot_general(a, b, dims, preferred_element_type=F32)

def mm3(a, b):
    ah, al = a
    bh, bl = b
    return mm(ah, bh) + (mm(al, bh) + mm(ah, bl))

def iota(shape, dim):
    return lax.broadcasted_iota(jnp.int32, shape, dim)

def mmk(a, b):
    ah, al = a
    bh, bl = b
    return mm(jnp.concatenate([ah, al], axis=1), jnp.concatenate([bh, bh], axis=0)) + mm(ah, bl)


def turn(v, by):
    return pltpu.roll(v, by, 1)


def split32(v):
    hi = v.astype(BF).astype(F32)
    return hi, v - hi


def eliminate(packs):
    lane = iota((BASE, STRIDE), 1)
    row = iota((BASE, STRIDE), 0)
    local = lane % BASE
    parts = BASE // 8
    start = (iota((8, STRIDE), 1) // BASE) * BASE
    row8 = iota((8, STRIDE), 0)
    eye = (row == local).astype(F32)
    recips, works, pieces = [], [], []
    for packed in packs:
        diag = jnp.sum(jnp.where(row == local, packed, 0.0), axis=0, keepdims=True)
        recip = 1.0 / diag
        scaled = jnp.where(row > local, packed * recip, 0.0)
        recips.append(jnp.broadcast_to(recip, (8, STRIDE)))
        works.append([eye[g * 8:(g + 1) * 8] for g in range(parts)])
        pieces.append([scaled[g * 8:(g + 1) * 8] for g in range(parts)])
    for j in range(BASE - 1):
        for work, piece in zip(works, pieces):
            pivot = work[j // 8][j % 8:j % 8 + 1]
            for g in range((j + 1) // 8, parts):
                column = jnp.take_along_axis(piece[g], start + j, axis=1, mode="promise_in_bounds")
                work[g] = work[g] - column * pivot
    for work, recip in zip(works, recips):
        for g in range(parts):
            work[g] = work[g] * jnp.take_along_axis(recip, start + (row8 + g * 8), axis=1, mode="promise_in_bounds")
    return [jnp.concatenate(work, axis=0) for work in works]


def slabs_of(v, size):
    return [v[r:r + size] for r in range(0, v.shape[0], size)]


def invert_blocks(blocks):
    lane = iota((BASE, STRIDE), 1)
    packs = []
    for block in blocks:
        packed = block[:BASE]
        for q, slab in enumerate(slabs_of(block, BASE)):
            packed = jnp.where(lane // BASE == q, slab, packed) if q else packed
        packs.append(packed)
    inners = eliminate(packs)
    states = [[jnp.where(lane // BASE == q, inner, 0.0) for q in range(STRIDE // BASE)] for inner in inners]
    size = BASE
    while size < STRIDE:
        half = iota((STRIDE // 2, STRIDE), 1) // size
        even = half % 2 == 0
        pair = (half // 2 == iota((STRIDE // 2, STRIDE), 0) // size) & even
        products = []
        for block, slabs in zip(blocks, states):
            ch, cl = split32(jnp.where(pair, jnp.concatenate(slabs_of(block, size)[1::2], axis=0), 0.0))
            a = jnp.concatenate([ch + turn(cl, size), ch], axis=1).astype(BF)
            tops = [split(v) for v in slabs[0::2]]
            w = [v[0] for v in tops for _ in range(2)] + [v[1] for v in tops for _ in range(2)]
            products.append(mm(a, jnp.concatenate(w, axis=0)))
        belows = []
        for product, slabs in zip(products, states):
            xh, xl = split32(jnp.concatenate(slabs[1::2], axis=0))
            a = jnp.concatenate([xh + turn(xl, STRIDE - size), xh], axis=1).astype(BF)
            th, tl = split(product)
            w = [v for v in slabs_of(th, size) for _ in range(2)] + [v for v in slabs_of(tl, size) for _ in range(2)]
            belows.append(slabs_of(mm(a, jnp.concatenate(w, axis=0)), size))
        states = [
            [jnp.concatenate([top, low - add], axis=0) for top, low, add in zip(slabs[0::2], slabs[1::2], below)]
            for slabs, below in zip(states, belows)
        ]
        size *= 2
    return [slabs[0] for slabs in states]


BATCH = 16


def solve_kernel(members, sizes_ref, glue_ref, far_ref, p_ref, out_ref, rest, f_ref, square_sems, corner_sems, strip_sems, panel_sem):
    subs, order, width = p_ref.shape
    wide = 2 * STRIDE
    square_copies, corner_copies, strip_copies = {}, {}, {}

    def fetch(s, rows, columns, sem):
        part = (s, rows, columns)
        copy = pltpu.make_async_copy(far_ref.at[part], f_ref.at[part], sem)
        copy.start()
        return copy

    for step, a in enumerate(range(0, order, STRIDE)):
        for s in range(subs):
            square_copies[s, a] = fetch(s, pl.ds(a, STRIDE), pl.ds(a, STRIDE), square_sems.at[s, step])
    for step, a in enumerate(range(0, order, wide)):
        for s in range(subs):
            corner_copies[s, a] = fetch(s, pl.ds(a + STRIDE, STRIDE), pl.ds(a, STRIDE), corner_sems.at[s, step])
    panel_copy = pltpu.make_async_copy(p_ref, rest, panel_sem)
    panel_copy.start()
    for step, a in enumerate(range(0, order - wide, wide)):
        for s in range(subs):
            strip_copies[s, a] = fetch(s, pl.ds(a + wide, order - a - wide), pl.ds(a, wide), strip_sems.at[s, step])
    row = iota((STRIDE, STRIDE), 0)
    col = iota((STRIDE, STRIDE), 1)
    prow = iota((wide, width), 0)
    dims = (((0,), (0,)), ((), ()))
    squares = [jnp.zeros((width, width), F32)] * subs
    crosses = [jnp.zeros((width, width), F32)] * subs
    places = [(s, a) for a in range(0, order, STRIDE) for s in range(subs)]
    small = {}
    for first in range(0, len(places), BATCH):
        batch = places[first:first + BATCH]
        blocks = []
        for s, a in batch:
            square_copies[s, a].wait()
            d = f_ref[s, a:a + STRIDE, a:a + STRIDE]
            keep = (row + a < sizes_ref[s]) & (col <= row)
            blocks.append(jnp.where(keep, d, (row == col).astype(F32)))
        for place, inverse in zip(batch, invert_blocks(blocks)):
            small[place] = split(inverse)
    heads = [(s, a) for a in range(0, order, wide) for s in range(subs)]
    corners = []
    for s, a in heads:
        b = a + STRIDE
        corner_copies[s, a].wait()
        corner = jnp.where(row + b < sizes_ref[s], f_ref[s, b:b + STRIDE, a:b], 0.0)
        corners.append(split(mmk(split(corner), small[s, a])))
    inverses = {}
    for (s, a), corner in zip(heads, corners):
        above, below = small[s, a], small[s, a + STRIDE]
        turned = split(-mmk(below, corner))
        blank = jnp.zeros((STRIDE, STRIDE), BF)
        inverses[s, a] = [
            jnp.concatenate([jnp.concatenate([u, blank], axis=1), jnp.concatenate([t, l], axis=1)], axis=0)
            for u, t, l in zip(above, turned, below)
        ]

    panel_copy.wait()
    for a in range(0, order, wide):
        solved = []
        for s in range(subs):
            now = jnp.where(prow + a < sizes_ref[s], rest[s, a:a + wide], 0.0)
            solved.append(split(mm3(inverses[s, a], split(now))))
        if a + wide < order:
            for s in range(subs):
                strip_copies[s, a].wait()
        for c in range(a + wide, order, wide):
            for s in range(subs):
                rest[s, c:c + wide] = rest[s, c:c + wide] - mm3(split(f_ref[s, c:c + wide, a:a + wide]), solved[s])
        for s in range(subs):
            hi, lo = solved[s]
            squares[s] = squares[s] + mm(hi, hi, dims)
            crosses[s] = crosses[s] + mm(hi, lo, dims)
    capacity = 2 * width // members
    glue = glue_ref[...]
    before = (iota((width, width), 0) < iota((width, width), 1)).astype(BF)
    dual_order = NDUAL
    for s in range(subs):
        dh, dl = split(squares[s] + (crosses[s] + crosses[s].T))
        line = glue[s:s + 1]
        owner = line // (dual_order // members)
        owners = (iota((members, width), 0) == owner)
        ranks = mm(owners.astype(BF), before)
        rank = jnp.sum(jnp.where(owners, ranks, 0.0), axis=0, keepdims=True).astype(jnp.int32)
        target = owner * capacity + rank
        dispatch = (iota((members * capacity, width), 0) == target).astype(BF)
        values = mm(dispatch, dh) + mm(dispatch, dl)
        for k in range(members):
            out_ref[k, s * capacity:(s + 1) * capacity] = values[k * capacity:(k + 1) * capacity]

def solve(factors, panels, sizes, glue, members):
    subs, order, width = panels.shape
    capacity = 2 * width // members
    vm = pl.BlockSpec(memory_space=pltpu.VMEM)
    far = pl.BlockSpec(memory_space=pltpu.HBM)
    return pl.pallas_call(
        functools.partial(solve_kernel, members),
        out_shape=jax.ShapeDtypeStruct((members, subs * capacity, width), F32),
        in_specs=[pl.BlockSpec(memory_space=pltpu.SMEM), vm, far, far],
        out_specs=vm,
        scratch_shapes=[
            pltpu.VMEM((subs, order, width), F32),
            pltpu.VMEM((subs, order, order), F32),
            pltpu.SemaphoreType.DMA((subs, order // STRIDE)),
            pltpu.SemaphoreType.DMA((subs, order // (2 * STRIDE))),
            pltpu.SemaphoreType.DMA((subs, order // (2 * STRIDE))),
            pltpu.SemaphoreType.DMA,
        ],
        compiler_params=pltpu.CompilerParams(vmem_limit_bytes=54 << 20),
        cost_estimate=pl.CostEstimate(flops=10_000_000_000, bytes_accessed=12 << 20, transcendentals=0),
        name="solve",
    )(sizes, glue, factors, panels)


def pack_kernel(loads_ref, glue_ref, out_ref):
    members, rows, nrhs = out_ref.shape
    half, lines = loads_ref.shape[0] // 2, glue_ref.shape[0] // 2
    blank = jnp.zeros((rows - half - lines, nrhs), F32)
    for k in range(members):
        part = k % 2
        out_ref[k, :half] = loads_ref[part * half:(part + 1) * half]
        line = glue_ref[part * lines:(part + 1) * lines].astype(F32)
        out_ref[k, half:] = jnp.concatenate([line, blank], axis=0)


def routes_kernel(subs, place_ref, own_ref, twin_ref, stand_ref, label_ref, high_ref, low_ref):
    members, block, width = own_ref.shape
    share = NDUAL // members
    half, lines = share // 2, subs // 2
    slots = label_ref.shape[1]
    capacity = slots // subs
    first_core = place_ref[0] % 2 == 0
    halves = (
        jnp.where(first_core, own_ref[...], twin_ref[...]),
        jnp.where(first_core, twin_ref[...], own_ref[...]),
    )
    glue = []
    for k in range(members):
        for part in range(2):
            row = k * share + part * half
            load = split(halves[part][k, :half])
            high_ref[row:row + half] = load[0]
            low_ref[row:row + half] = load[1]
            glue.append(halves[part][k, half:half + lines])
    glue = jnp.concatenate(glue, axis=0)
    stand_ref[...] = glue.T.astype(jnp.int32)
    glue = glue.astype(jnp.int32)
    first = place_ref[0] * share
    mine = (glue >= first) & (glue < first + share)
    before = (iota((width, width), 0) < iota((width, width), 1)).astype(BF)
    ranks = mm(mine.astype(BF), before).astype(jnp.int32)
    local = jnp.where(mine, glue - first + 1, 0).astype(F32).astype(BF)
    labels = []
    for k in range(members):
        found = jnp.full((1, slots), -1.0, F32)
        for s in range(subs):
            i = k * subs + s
            rank = jnp.where(mine[i:i + 1], ranks[i:i + 1] + s * capacity, -1)
            at_slot = (iota((slots, width), 0) == rank).astype(BF)
            line = mm(local[i:i + 1], at_slot, (((1,), (1,)), ((), ())))
            found = jnp.where(line > 0.5, line + (s * share - 1), found)
        labels.append(found)
    label_ref[...] = jnp.concatenate(labels, axis=0).astype(jnp.int32)


def finish_kernel(subs, values_ref, label_ref, stand_ref, high_ref, low_ref, dual_ref, raw_ref, first_ref, last_ref):
    members, slots, width = values_ref.shape
    share, nrhs = raw_ref.shape
    total = jnp.zeros((2 * share, NDUAL), F32)
    for k in range(members):
        rows = (iota((subs * share, slots), 0) == label_ref[k:k + 1]).astype(BF)
        moved = mm(rows, jnp.concatenate(split(values_ref[k]), axis=1)).astype(BF)
        for s in range(subs):
            i = k * subs + s
            part = moved[s * share:(s + 1) * share]
            columns = (iota((width, NDUAL), 1) == stand_ref[:, i:i + 1]).astype(BF)
            total = total + mm(jnp.concatenate([part[:, :width], part[:, width:]], axis=0), columns)
    dual = total[:share] + total[share:]
    dual_ref[...] = dual
    raw = mm3(split(dual), (high_ref[...], low_ref[...]))
    raw_ref[...] = raw
    first_ref[...] = raw[:IFACE]
    last_ref[...] = raw[share - IFACE:]


def call(kernel, outs, args, flops, name, smem=0, grant=16):
    vm = pl.BlockSpec(memory_space=pltpu.VMEM)
    specs = [pl.BlockSpec(memory_space=pltpu.SMEM)] * smem + [vm] * (len(args) - smem)
    return pl.pallas_call(
        kernel,
        out_shape=outs,
        in_specs=specs,
        out_specs=jax.tree.map(lambda _: vm, outs),
        compiler_params=pltpu.CompilerParams(vmem_limit_bytes=grant << 20),
        cost_estimate=pl.CostEstimate(flops=flops, bytes_accessed=4 << 20, transcendentals=0),
        name=name,
    )(*args)


def on_device(factors, panels, sizes, glue_index, loads):
    members = lax.axis_size("member")
    subs, order, width = panels.shape
    share, nrhs = loads.shape
    capacity = 2 * width // members
    slots = subs * capacity
    count = members * subs
    shape = jax.ShapeDtypeStruct
    packed = call(pack_kernel, shape((members, share // 2 + 8 * (-(-subs // 16)), nrhs), F32), (loads, glue_index), 1_000_000, "pack", grant=58)
    own = lax.all_to_all(packed, "member", split_axis=0, concat_axis=0, tiled=True)
    values = solve(factors, panels, sizes, glue_index, members)
    twin = lax.ppermute(own, "member", [(i, i ^ 1) for i in range(members)])
    place = lax.axis_index("member").astype(jnp.int32).reshape(1)
    stand, labels, high, low = call(
        functools.partial(routes_kernel, subs),
        (
            shape((width, count), jnp.int32),
            shape((members, slots), jnp.int32),
            shape((NDUAL, nrhs), BF),
            shape((NDUAL, nrhs), BF),
        ),
        (place, own, twin),
        2_000_000_000,
        "routes",
        smem=1,
    )
    values = lax.all_to_all(values, "member", split_axis=0, concat_axis=0, tiled=True)
    dual_rows, raw, first, last = call(
        functools.partial(finish_kernel, subs),
        (
            shape((share, NDUAL), F32),
            shape((share, nrhs), F32),
            shape((IFACE, nrhs), F32),
            shape((IFACE, nrhs), F32),
        ),
        (values, labels, stand, high, low),
        5_000_000_000,
        "finish",
    )
    peers = lax.axis_size("cluster")
    up = [(i, (i + 1) % peers) for i in range(peers)]
    down = [(j, i) for i, j in up]
    before = lax.ppermute(last, "cluster", up)
    after = lax.ppermute(first, "cluster", down)
    between = jnp.zeros((share - 2 * IFACE, nrhs), F32)
    products = raw + jnp.concatenate([before, between, after], axis=0)
    return (dual_rows, products)


def solution(mesh):
    shards = ("cluster", "member")
    return jax.shard_map(
        on_device,
        mesh=mesh,
        in_specs=(P(shards, None, None), P(shards, None, None), P(shards), P(shards, None), P(shards, None)),
        out_specs=(P(shards, None), P(shards, None)),
        check_vma=False,
    )
```

```python
import functools
import jax, jax.numpy as jnp
from jax import lax
from jax.experimental import pallas as pl
from jax.experimental.pallas import tpu as pltpu
F32, BF = jnp.float32, jnp.bfloat16
from jax.sharding import PartitionSpec as P

STRIDE, BASE = 128, 16
NDUAL, IFACE = 1024, 8

def split(v):
    hi = v.astype(BF)
    return hi, (v - hi.astype(F32)).astype(BF)

def mm(a, b, dims=(((1,), (0,)), ((), ()))):
    return lax.dot_general(a, b, dims, preferred_element_type=F32)

def mm3(a, b):
    ah, al = a
    bh, bl = b
    return mm(ah, bh) + (mm(al, bh) + mm(ah, bl))

def iota(shape, dim):
    return lax.broadcasted_iota(jnp.int32, shape, dim)

def mmk(a, b):
    ah, al = a
    bh, bl = b
    return mm(jnp.concatenate([ah, al], axis=1), jnp.concatenate([bh, bh], axis=0)) + mm(ah, bl)


def turn(v, by):
    return pltpu.roll(v, by, 1)


def split32(v):
    hi = v.astype(BF).astype(F32)
    return hi, v - hi


def eliminate(packs):
    lane = iota((BASE, STRIDE), 1)
    row = iota((BASE, STRIDE), 0)
    local = lane % BASE
    parts = BASE // 8
    start = (iota((8, STRIDE), 1) // BASE) * BASE
    row8 = iota((8, STRIDE), 0)
    eye = (row == local).astype(F32)
    recips, works, pieces = [], [], []
    for packed in packs:
        diag = jnp.sum(jnp.where(row == local, packed, 0.0), axis=0, keepdims=True)
        recip = 1.0 / diag
        scaled = jnp.where(row > local, packed * recip, 0.0)
        recips.append(jnp.broadcast_to(recip, (8, STRIDE)))
        works.append([eye[g * 8:(g + 1) * 8] for g in range(parts)])
        pieces.append([scaled[g * 8:(g + 1) * 8] for g in range(parts)])
    for j in range(BASE - 1):
        for work, piece in zip(works, pieces):
            pivot = work[j // 8][j % 8:j % 8 + 1]
            for g in range((j + 1) // 8, parts):
                column = jnp.take_along_axis(piece[g], start + j, axis=1, mode="promise_in_bounds")
                work[g] = work[g] - column * pivot
    for work, recip in zip(works, recips):
        for g in range(parts):
            work[g] = work[g] * jnp.take_along_axis(recip, start + (row8 + g * 8), axis=1, mode="promise_in_bounds")
    return [jnp.concatenate(work, axis=0) for work in works]


def slabs_of(v, size):
    return [v[r:r + size] for r in range(0, v.shape[0], size)]


def invert_blocks(blocks):
    lane = iota((BASE, STRIDE), 1)
    packs = []
    for block in blocks:
        packed = block[:BASE]
        for q, slab in enumerate(slabs_of(block, BASE)):
            packed = jnp.where(lane // BASE == q, slab, packed) if q else packed
        packs.append(packed)
    inners = eliminate(packs)
    states = [[jnp.where(lane // BASE == q, inner, 0.0) for q in range(STRIDE // BASE)] for inner in inners]
    size = BASE
    while size < STRIDE:
        half = iota((STRIDE // 2, STRIDE), 1) // size
        even = half % 2 == 0
        pair = (half // 2 == iota((STRIDE // 2, STRIDE), 0) // size) & even
        products = []
        for block, slabs in zip(blocks, states):
            ch, cl = split32(jnp.where(pair, jnp.concatenate(slabs_of(block, size)[1::2], axis=0), 0.0))
            a = jnp.concatenate([ch + turn(cl, size), ch], axis=1).astype(BF)
            tops = [split(v) for v in slabs[0::2]]
            w = [v[0] for v in tops for _ in range(2)] + [v[1] for v in tops for _ in range(2)]
            products.append(mm(a, jnp.concatenate(w, axis=0)))
        belows = []
        for product, slabs in zip(products, states):
            xh, xl = split32(jnp.concatenate(slabs[1::2], axis=0))
            a = jnp.concatenate([xh + turn(xl, STRIDE - size), xh], axis=1).astype(BF)
            th, tl = split(product)
            w = [v for v in slabs_of(th, size) for _ in range(2)] + [v for v in slabs_of(tl, size) for _ in range(2)]
            belows.append(slabs_of(mm(a, jnp.concatenate(w, axis=0)), size))
        states = [
            [jnp.concatenate([top, low - add], axis=0) for top, low, add in zip(slabs[0::2], slabs[1::2], below)]
            for slabs, below in zip(states, belows)
        ]
        size *= 2
    return [slabs[0] for slabs in states]


BATCH = 16


def solve_kernel(members, place_ref, sizes_ref, glue_ref, square_ref, far_ref, p_ref, *refs):
    out_refs = refs[:members]
    rest, f_ref, corner_sems, strip_sems, panel_sem = refs[members:]
    subs, order, width = p_ref.shape
    wide = 2 * STRIDE
    corner_copies, strip_copies = {}, {}

    def fetch(s, rows, columns, sem):
        part = (s, rows, columns)
        copy = pltpu.make_async_copy(far_ref.at[part], f_ref.at[part], sem)
        copy.start()
        return copy

    for step, a in enumerate(range(0, order, wide)):
        for s in range(subs):
            corner_copies[s, a] = fetch(s, pl.ds(a + STRIDE, STRIDE), pl.ds(a, STRIDE), corner_sems.at[s, step])
    panel_copy = pltpu.make_async_copy(p_ref, rest, panel_sem)
    panel_copy.start()
    for step, a in enumerate(range(0, order - wide, wide)):
        for s in range(subs):
            strip_copies[s, a] = fetch(s, pl.ds(a + wide, order - a - wide), pl.ds(a, wide), strip_sems.at[s, step])
    row = iota((STRIDE, STRIDE), 0)
    col = iota((STRIDE, STRIDE), 1)
    prow = iota((wide, width), 0)
    dims = (((0,), (0,)), ((), ()))
    squares = [jnp.zeros((width, width), F32)] * subs
    crosses = [jnp.zeros((width, width), F32)] * subs
    places = [(s, a) for a in range(0, order, STRIDE) for s in range(subs)]
    small = {}
    for first in range(0, len(places), BATCH):
        batch = places[first:first + BATCH]
        blocks = []
        for s, a in batch:
            d = square_ref[s, a // STRIDE]
            keep = (row + a < sizes_ref[s]) & (col <= row)
            blocks.append(jnp.where(keep, d, (row == col).astype(F32)))
        for place, inverse in zip(batch, invert_blocks(blocks)):
            small[place] = split(inverse)
    heads = [(s, a) for a in range(0, order, wide) for s in range(subs)]
    corners = []
    for s, a in heads:
        b = a + STRIDE
        corner_copies[s, a].wait()
        corner = jnp.where(row + b < sizes_ref[s], f_ref[s, b:b + STRIDE, a:b], 0.0)
        corners.append(split(mmk(split(corner), small[s, a])))
    inverses = {}
    for (s, a), corner in zip(heads, corners):
        above, below = small[s, a], small[s, a + STRIDE]
        turned = split(-mmk(below, corner))
        blank = jnp.zeros((STRIDE, STRIDE), BF)
        inverses[s, a] = [
            jnp.concatenate([jnp.concatenate([u, blank], axis=1), jnp.concatenate([t, l], axis=1)], axis=0)
            for u, t, l in zip(above, turned, below)
        ]

    panel_copy.wait()
    for a in range(0, order, wide):
        solved = []
        for s in range(subs):
            now = jnp.where(prow + a < sizes_ref[s], rest[s, a:a + wide], 0.0)
            solved.append(split(mm3(inverses[s, a], split(now))))
        if a + wide < order:
            for s in range(subs):
                strip_copies[s, a].wait()
        for c in range(a + wide, order, wide):
            for s in range(subs):
                rest[s, c:c + wide] = rest[s, c:c + wide] - mm3(split(f_ref[s, c:c + wide, a:a + wide]), solved[s])
        for s in range(subs):
            hi, lo = solved[s]
            squares[s] = squares[s] + mm(hi, hi, dims)
            crosses[s] = crosses[s] + mm(hi, lo, dims)
    capacity = 2 * width // members
    glue = glue_ref[...]
    before = (iota((width, width), 0) < iota((width, width), 1)).astype(BF)
    dual_order = NDUAL
    for s in range(subs):
        dh, dl = split(squares[s] + (crosses[s] + crosses[s].T))
        line = glue[s:s + 1]
        owner = line // (dual_order // members)
        owners = (iota((members, width), 0) == owner)
        ranks = mm(owners.astype(BF), before)
        rank = jnp.sum(jnp.where(owners, ranks, 0.0), axis=0, keepdims=True).astype(jnp.int32)
        target = (owner ^ place_ref[0]) * capacity + rank
        dispatch = (iota((members * capacity, width), 0) == target).astype(BF)
        values = mm(dispatch, dh) + mm(dispatch, dl)
        for k in range(members):
            out_refs[k][s * capacity:(s + 1) * capacity] = values[k * capacity:(k + 1) * capacity]

def solve(place, sizes, glue, squares, factors, panels, members):
    subs, order, width = panels.shape
    capacity = 2 * width // members
    vm = pl.BlockSpec(memory_space=pltpu.VMEM)
    sm = pl.BlockSpec(memory_space=pltpu.SMEM)
    far = pl.BlockSpec(memory_space=pltpu.HBM)
    return pl.pallas_call(
        functools.partial(solve_kernel, members),
        out_shape=[jax.ShapeDtypeStruct((subs * capacity, width), F32)] * members,
        in_specs=[sm, sm, vm, vm, far, far],
        out_specs=[vm] * members,
        scratch_shapes=[
            pltpu.VMEM((subs, order, width), F32),
            pltpu.VMEM((subs, order, order), F32),
            pltpu.SemaphoreType.DMA((subs, order // (2 * STRIDE))),
            pltpu.SemaphoreType.DMA((subs, order // (2 * STRIDE))),
            pltpu.SemaphoreType.DMA,
        ],
        compiler_params=pltpu.CompilerParams(vmem_limit_bytes=54 << 20),
        cost_estimate=pl.CostEstimate(flops=10_000_000_000, bytes_accessed=8 << 20, transcendentals=0),
        name="solve",
    )(place, sizes, glue, squares, factors, panels)


def pack_kernel(loads_ref, far_ref, glue_ref, out_ref, square_ref, tail, load_sems, tail_sems, square_sems):
    members, rows, nrhs = out_ref.shape
    half, lines = loads_ref.shape[0] // 2, glue_ref.shape[0] // 2
    subs, blocks = square_ref.shape[:2]
    copies = []
    for k in range(members):
        rows_of = loads_ref.at[pl.ds(k % 2 * half, half)]
        copies.append(pltpu.make_async_copy(rows_of, out_ref.at[k, pl.ds(0, half)], load_sems.at[k]))
    for s in range(subs):
        for j in range(blocks):
            block = far_ref.at[s, pl.ds(j * STRIDE, STRIDE), pl.ds(j * STRIDE, STRIDE)]
            copies.append(pltpu.make_async_copy(block, square_ref.at[s, j], square_sems.at[s, j]))
    for copy in copies:
        copy.start()
    blank = jnp.zeros((rows - half - lines, nrhs), F32)
    for part in range(2):
        line = glue_ref[part * lines:(part + 1) * lines].astype(F32)
        tail[part] = jnp.concatenate([line, blank], axis=0)
    for k in range(members):
        copy = pltpu.make_async_copy(tail.at[k % 2], out_ref.at[k, pl.ds(half, rows - half)], tail_sems.at[k])
        copy.start()
        copies.append(copy)
    for copy in copies:
        copy.wait()


def pack(loads, factors, glue, members):
    subs, order, _ = factors.shape
    share, nrhs = loads.shape
    rows = share // 2 + 8 * (-(-subs // 16))
    vm = pl.BlockSpec(memory_space=pltpu.VMEM)
    far = pl.BlockSpec(memory_space=pltpu.HBM)
    return pl.pallas_call(
        pack_kernel,
        out_shape=[
            jax.ShapeDtypeStruct((members, rows, nrhs), F32),
            jax.ShapeDtypeStruct((subs, order // STRIDE, STRIDE, STRIDE), F32),
        ],
        in_specs=[far, far, vm],
        out_specs=[far, vm],
        scratch_shapes=[
            pltpu.VMEM((2, rows - share // 2, nrhs), F32),
            pltpu.SemaphoreType.DMA((members,)),
            pltpu.SemaphoreType.DMA((members,)),
            pltpu.SemaphoreType.DMA((subs, order // STRIDE)),
        ],
        compiler_params=pltpu.CompilerParams(vmem_limit_bytes=58 << 20),
        cost_estimate=pl.CostEstimate(flops=1_000_000, bytes_accessed=3 << 20, transcendentals=0),
        name="pack",
    )(loads, factors, glue)


def routes_kernel(subs, place_ref, own_ref, twin_ref, stand_ref, label_ref, high_ref, low_ref):
    members, block, width = own_ref.shape
    share = NDUAL // members
    half, lines = share // 2, subs // 2
    slots = label_ref.shape[1]
    capacity = slots // subs
    first_core = place_ref[0] % 2 == 0
    glue = []
    for k in range(members):
        source = place_ref[0] ^ k
        pair = own_ref[source], twin_ref[source]
        for part in range(2):
            got = jnp.where(first_core, pair[part], pair[1 - part])
            row = pl.ds(pl.multiple_of(source * share + part * half, half), half)
            high_ref[row], low_ref[row] = split(got[:half])
            glue.append(got[half:half + lines])
    glue = jnp.concatenate(glue, axis=0)
    stand_ref[...] = glue.T.astype(jnp.int32)
    glue = glue.astype(jnp.int32)
    first = place_ref[0] * share
    mine = (glue >= first) & (glue < first + share)
    before = (iota((width, width), 0) < iota((width, width), 1)).astype(BF)
    ranks = mm(mine.astype(BF), before).astype(jnp.int32)
    local = jnp.where(mine, glue - first + 1, 0).astype(F32).astype(BF)
    labels = []
    for k in range(members):
        found = jnp.full((1, slots), -1.0, F32)
        for s in range(subs):
            i = k * subs + s
            rank = jnp.where(mine[i:i + 1], ranks[i:i + 1] + s * capacity, -1)
            at_slot = (iota((slots, width), 0) == rank).astype(BF)
            line = mm(local[i:i + 1], at_slot, (((1,), (1,)), ((), ())))
            found = jnp.where(line > 0.5, line + (s * share - 1), found)
        labels.append(found)
    label_ref[...] = jnp.concatenate(labels, axis=0).astype(jnp.int32)


def finish_kernel(subs, order, label_ref, stand_ref, high_ref, low_ref, *refs):
    values, (dual_ref, raw_ref, first_ref, last_ref) = refs[:-4], refs[-4:]
    members = len(values)
    slots, width = values[0].shape
    share, nrhs = raw_ref.shape
    total = jnp.zeros((2 * share, NDUAL), F32)
    for k, value in zip(order, values):
        rows = (iota((subs * share, slots), 0) == label_ref[k:k + 1]).astype(BF)
        moved = mm(rows, jnp.concatenate(split(value[...]), axis=1)).astype(BF)
        for s in range(subs):
            i = k * subs + s
            part = moved[s * share:(s + 1) * share]
            columns = (iota((width, NDUAL), 1) == stand_ref[:, i:i + 1]).astype(BF)
            total = total + mm(jnp.concatenate([part[:, :width], part[:, width:]], axis=0), columns)
    dual = total[:share] + total[share:]
    dual_ref[...] = dual
    raw = mm3(split(dual), (high_ref[...], low_ref[...]))
    raw_ref[...] = raw
    first_ref[...] = raw[:IFACE]
    last_ref[...] = raw[share - IFACE:]


def call(kernel, outs, args, flops, name, smem=0, grant=16):
    vm = pl.BlockSpec(memory_space=pltpu.VMEM)
    specs = [pl.BlockSpec(memory_space=pltpu.SMEM)] * smem + [vm] * (len(args) - smem)
    return pl.pallas_call(
        kernel,
        out_shape=outs,
        in_specs=specs,
        out_specs=jax.tree.map(lambda _: vm, outs),
        compiler_params=pltpu.CompilerParams(vmem_limit_bytes=grant << 20),
        cost_estimate=pl.CostEstimate(flops=flops, bytes_accessed=4 << 20, transcendentals=0),
        name=name,
    )(*args)


def on_device(factors, panels, sizes, glue_index, loads):
    members = lax.axis_size("member")
    subs, order, width = panels.shape
    share, nrhs = loads.shape
    capacity = 2 * width // members
    slots = subs * capacity
    count = members * subs
    shape = jax.ShapeDtypeStruct
    place = lax.axis_index("member").astype(jnp.int32).reshape(1)

    def across(value, distance):
        return lax.ppermute(value, "member", [(i, i ^ distance) for i in range(members)])

    packed, squares = pack(loads, factors, glue_index, members)
    own = lax.all_to_all(packed, "member", split_axis=0, concat_axis=0, tiled=True)
    values = solve(place, sizes, glue_index, squares, factors, panels, members)
    own, *values = lax.optimization_barrier((own, *values))
    arrivals = (0, *range(2, members, 2), *range(3, members, 2), 1)
    arrived = [across(values[k], k) if k else values[k] for k in arrivals]
    twin = across(own, 1)
    stand, labels, high, low = call(
        functools.partial(routes_kernel, subs),
        (
            shape((width, count), jnp.int32),
            shape((members, slots), jnp.int32),
            shape((NDUAL, nrhs), BF),
            shape((NDUAL, nrhs), BF),
        ),
        (place, own, twin),
        2_000_000_000,
        "routes",
        smem=1,
    )
    dual_rows, raw, first, last = call(
        functools.partial(finish_kernel, subs, arrivals),
        (
            shape((share, NDUAL), F32),
            shape((share, nrhs), F32),
            shape((IFACE, nrhs), F32),
            shape((IFACE, nrhs), F32),
        ),
        (labels, stand, high, low, *arrived),
        5_000_000_000,
        "finish",
    )
    peers = lax.axis_size("cluster")
    up = [(i, (i + 1) % peers) for i in range(peers)]
    down = [(j, i) for i, j in up]
    before = lax.ppermute(last, "cluster", up)
    after = lax.ppermute(first, "cluster", down)
    between = jnp.zeros((share - 2 * IFACE, nrhs), F32)
    products = raw + jnp.concatenate([before, between, after], axis=0)
    return (dual_rows, products)


def solution(mesh):
    shards = ("cluster", "member")
    return jax.shard_map(
        on_device,
        mesh=mesh,
        in_specs=(P(shards, None, None), P(shards, None, None), P(shards), P(shards, None), P(shards, None)),
        out_specs=(P(shards, None), P(shards, None)),
        check_vma=False,
    )
```

```python
import functools
import jax, jax.numpy as jnp
from jax import lax
from jax.experimental import pallas as pl
from jax.experimental.pallas import tpu as pltpu
F32, BF = jnp.float32, jnp.bfloat16
from jax.sharding import PartitionSpec as P

STRIDE, BASE = 128, 16
NDUAL, IFACE = 1024, 8

def split(v):
    hi = v.astype(BF)
    return hi, (v - hi.astype(F32)).astype(BF)

def mm(a, b, dims=(((1,), (0,)), ((), ()))):
    return lax.dot_general(a, b, dims, preferred_element_type=F32)

def mm3(a, b):
    ah, al = a
    bh, bl = b
    return mm(ah, bh) + (mm(al, bh) + mm(ah, bl))

def iota(shape, dim):
    return lax.broadcasted_iota(jnp.int32, shape, dim)

def mmk(a, b):
    ah, al = a
    bh, bl = b
    return mm(jnp.concatenate([ah, al], axis=1), jnp.concatenate([bh, bh], axis=0)) + mm(ah, bl)


def turn(v, by):
    return pltpu.roll(v, by, 1)


def split32(v):
    hi = v.astype(BF).astype(F32)
    return hi, v - hi


def eliminate(packs):
    lane = iota((BASE, STRIDE), 1)
    row = iota((BASE, STRIDE), 0)
    local = lane % BASE
    parts = BASE // 8
    start = (iota((8, STRIDE), 1) // BASE) * BASE
    row8 = iota((8, STRIDE), 0)
    eye = (row == local).astype(F32)
    recips, works, pieces = [], [], []
    for packed in packs:
        diag = jnp.sum(jnp.where(row == local, packed, 0.0), axis=0, keepdims=True)
        recip = 1.0 / diag
        scaled = jnp.where(row > local, packed * recip, 0.0)
        recips.append(jnp.broadcast_to(recip, (8, STRIDE)))
        works.append([eye[g * 8:(g + 1) * 8] for g in range(parts)])
        pieces.append([scaled[g * 8:(g + 1) * 8] for g in range(parts)])
    for j in range(BASE - 1):
        for work, piece in zip(works, pieces):
            pivot = work[j // 8][j % 8:j % 8 + 1]
            for g in range((j + 1) // 8, parts):
                column = jnp.take_along_axis(piece[g], start + j, axis=1, mode="promise_in_bounds")
                work[g] = work[g] - column * pivot
    for work, recip in zip(works, recips):
        for g in range(parts):
            work[g] = work[g] * jnp.take_along_axis(recip, start + (row8 + g * 8), axis=1, mode="promise_in_bounds")
    return [jnp.concatenate(work, axis=0) for work in works]


def slabs_of(v, size):
    return [v[r:r + size] for r in range(0, v.shape[0], size)]


def invert_blocks(blocks):
    lane = iota((BASE, STRIDE), 1)
    packs = []
    for block in blocks:
        packed = block[:BASE]
        for q, slab in enumerate(slabs_of(block, BASE)):
            packed = jnp.where(lane // BASE == q, slab, packed) if q else packed
        packs.append(packed)
    inners = eliminate(packs)
    states = [[jnp.where(lane // BASE == q, inner, 0.0) for q in range(STRIDE // BASE)] for inner in inners]
    size = BASE
    while size < STRIDE:
        half = iota((STRIDE // 2, STRIDE), 1) // size
        even = half % 2 == 0
        pair = (half // 2 == iota((STRIDE // 2, STRIDE), 0) // size) & even
        products = []
        for block, slabs in zip(blocks, states):
            ch, cl = split32(jnp.where(pair, jnp.concatenate(slabs_of(block, size)[1::2], axis=0), 0.0))
            a = jnp.concatenate([ch + turn(cl, size), ch], axis=1).astype(BF)
            tops = [split(v) for v in slabs[0::2]]
            w = [v[0] for v in tops for _ in range(2)] + [v[1] for v in tops for _ in range(2)]
            products.append(mm(a, jnp.concatenate(w, axis=0)))
        belows = []
        for product, slabs in zip(products, states):
            xh, xl = split32(jnp.concatenate(slabs[1::2], axis=0))
            a = jnp.concatenate([xh + turn(xl, STRIDE - size), xh], axis=1).astype(BF)
            th, tl = split(product)
            w = [v for v in slabs_of(th, size) for _ in range(2)] + [v for v in slabs_of(tl, size) for _ in range(2)]
            belows.append(slabs_of(mm(a, jnp.concatenate(w, axis=0)), size))
        states = [
            [jnp.concatenate([top, low - add], axis=0) for top, low, add in zip(slabs[0::2], slabs[1::2], below)]
            for slabs, below in zip(states, belows)
        ]
        size *= 2
    return [slabs[0] for slabs in states]


BATCH = 16


def solve_kernel(members, place_ref, sizes_ref, glue_ref, far_ref, p_ref, *refs):
    out_refs = refs[:members]
    rest, f_ref, square_sems, corner_sems, strip_sems, panel_sem = refs[members:]
    subs, order, width = p_ref.shape
    wide = 2 * STRIDE
    square_copies, corner_copies, strip_copies = {}, {}, {}

    def fetch(s, rows, columns, sem):
        part = (s, rows, columns)
        copy = pltpu.make_async_copy(far_ref.at[part], f_ref.at[part], sem)
        copy.start()
        return copy

    for step, a in enumerate(range(0, order, STRIDE)):
        for s in range(subs):
            square_copies[s, a] = fetch(s, pl.ds(a, STRIDE), pl.ds(a, STRIDE), square_sems.at[s, step])
    for step, a in enumerate(range(0, order, wide)):
        for s in range(subs):
            corner_copies[s, a] = fetch(s, pl.ds(a + STRIDE, STRIDE), pl.ds(a, STRIDE), corner_sems.at[s, step])
    panel_copy = pltpu.make_async_copy(p_ref, rest, panel_sem)
    panel_copy.start()
    for step, a in enumerate(range(0, order - wide, wide)):
        for s in range(subs):
            strip_copies[s, a] = fetch(s, pl.ds(a + wide, order - a - wide), pl.ds(a, wide), strip_sems.at[s, step])
    row = iota((STRIDE, STRIDE), 0)
    col = iota((STRIDE, STRIDE), 1)
    prow = iota((wide, width), 0)
    dims = (((0,), (0,)), ((), ()))
    squares = [jnp.zeros((width, width), F32)] * subs
    crosses = [jnp.zeros((width, width), F32)] * subs
    places = [(s, a) for a in range(0, order, STRIDE) for s in range(subs)]
    small = {}
    for first in range(0, len(places), BATCH):
        batch = places[first:first + BATCH]
        blocks = []
        for s, a in batch:
            square_copies[s, a].wait()
            d = f_ref[s, a:a + STRIDE, a:a + STRIDE]
            keep = (row + a < sizes_ref[s]) & (col <= row)
            blocks.append(jnp.where(keep, d, (row == col).astype(F32)))
        for place, inverse in zip(batch, invert_blocks(blocks)):
            small[place] = split(inverse)
    heads = [(s, a) for a in range(0, order, wide) for s in range(subs)]
    corners = []
    for s, a in heads:
        b = a + STRIDE
        corner_copies[s, a].wait()
        corner = jnp.where(row + b < sizes_ref[s], f_ref[s, b:b + STRIDE, a:b], 0.0)
        corners.append(split(mmk(split(corner), small[s, a])))
    inverses = {}
    for (s, a), corner in zip(heads, corners):
        above, below = small[s, a], small[s, a + STRIDE]
        turned = split(-mmk(below, corner))
        blank = jnp.zeros((STRIDE, STRIDE), BF)
        inverses[s, a] = [
            jnp.concatenate([jnp.concatenate([u, blank], axis=1), jnp.concatenate([t, l], axis=1)], axis=0)
            for u, t, l in zip(above, turned, below)
        ]

    panel_copy.wait()
    for a in range(0, order, wide):
        solved = []
        for s in range(subs):
            now = jnp.where(prow + a < sizes_ref[s], rest[s, a:a + wide], 0.0)
            solved.append(split(mm3(inverses[s, a], split(now))))
        if a + wide < order:
            for s in range(subs):
                strip_copies[s, a].wait()
        for c in range(a + wide, order, wide):
            for s in range(subs):
                rest[s, c:c + wide] = rest[s, c:c + wide] - mm3(split(f_ref[s, c:c + wide, a:a + wide]), solved[s])
        for s in range(subs):
            hi, lo = solved[s]
            squares[s] = squares[s] + mm(hi, hi, dims)
            crosses[s] = crosses[s] + mm(hi, lo, dims)
    capacity = 2 * width // members
    glue = glue_ref[...]
    before = (iota((width, width), 0) < iota((width, width), 1)).astype(BF)
    dual_order = NDUAL
    for s in range(subs):
        dh, dl = split(squares[s] + (crosses[s] + crosses[s].T))
        line = glue[s:s + 1]
        owner = line // (dual_order // members)
        owners = (iota((members, width), 0) == owner)
        ranks = mm(owners.astype(BF), before)
        rank = jnp.sum(jnp.where(owners, ranks, 0.0), axis=0, keepdims=True).astype(jnp.int32)
        target = (owner ^ place_ref[0]) * capacity + rank
        dispatch = (iota((members * capacity, width), 0) == target).astype(BF)
        values = mm(dispatch, dh) + mm(dispatch, dl)
        for k in range(members):
            out_refs[k][s * capacity:(s + 1) * capacity] = values[k * capacity:(k + 1) * capacity]

def solve(place, sizes, glue, factors, panels, members):
    subs, order, width = panels.shape
    capacity = 2 * width // members
    vm = pl.BlockSpec(memory_space=pltpu.VMEM)
    sm = pl.BlockSpec(memory_space=pltpu.SMEM)
    far = pl.BlockSpec(memory_space=pltpu.HBM)
    return pl.pallas_call(
        functools.partial(solve_kernel, members),
        out_shape=[jax.ShapeDtypeStruct((subs * capacity, width), F32)] * members,
        in_specs=[sm, sm, vm, far, far],
        out_specs=[vm] * members,
        scratch_shapes=[
            pltpu.VMEM((subs, order, width), F32),
            pltpu.VMEM((subs, order, order), F32),
            pltpu.SemaphoreType.DMA((subs, order // STRIDE)),
            pltpu.SemaphoreType.DMA((subs, order // (2 * STRIDE))),
            pltpu.SemaphoreType.DMA((subs, order // (2 * STRIDE))),
            pltpu.SemaphoreType.DMA,
        ],
        compiler_params=pltpu.CompilerParams(vmem_limit_bytes=54 << 20),
        cost_estimate=pl.CostEstimate(flops=10_000_000_000, bytes_accessed=8 << 20, transcendentals=0),
        name="solve",
    )(place, sizes, glue, factors, panels)


def pack_kernel(loads_ref, glue_ref, out_ref):
    members, rows, nrhs = out_ref.shape
    half, lines = loads_ref.shape[0] // 2, glue_ref.shape[0] // 2
    blank = jnp.zeros((rows - half - lines, nrhs), F32)
    for k in range(members):
        part = k % 2
        out_ref[k, :half] = loads_ref[part * half:(part + 1) * half]
        line = glue_ref[part * lines:(part + 1) * lines].astype(F32)
        out_ref[k, half:] = jnp.concatenate([line, blank], axis=0)


def routes_kernel(subs, place_ref, own_ref, twin_ref, stand_ref, label_ref, high_ref, low_ref):
    members, block, width = own_ref.shape
    share = NDUAL // members
    half, lines = share // 2, subs // 2
    slots = label_ref.shape[1]
    capacity = slots // subs
    first_core = place_ref[0] % 2 == 0
    glue = []
    for k in range(members):
        source = place_ref[0] ^ k
        pair = own_ref[source], twin_ref[source]
        for part in range(2):
            got = jnp.where(first_core, pair[part], pair[1 - part])
            row = pl.ds(pl.multiple_of(source * share + part * half, half), half)
            high_ref[row], low_ref[row] = split(got[:half])
            glue.append(got[half:half + lines])
    glue = jnp.concatenate(glue, axis=0)
    stand_ref[...] = glue.T.astype(jnp.int32)
    glue = glue.astype(jnp.int32)
    first = place_ref[0] * share
    mine = (glue >= first) & (glue < first + share)
    before = (iota((width, width), 0) < iota((width, width), 1)).astype(BF)
    ranks = mm(mine.astype(BF), before).astype(jnp.int32)
    local = jnp.where(mine, glue - first + 1, 0).astype(F32).astype(BF)
    labels = []
    for k in range(members):
        found = jnp.full((1, slots), -1.0, F32)
        for s in range(subs):
            i = k * subs + s
            rank = jnp.where(mine[i:i + 1], ranks[i:i + 1] + s * capacity, -1)
            at_slot = (iota((slots, width), 0) == rank).astype(BF)
            line = mm(local[i:i + 1], at_slot, (((1,), (1,)), ((), ())))
            found = jnp.where(line > 0.5, line + (s * share - 1), found)
        labels.append(found)
    label_ref[...] = jnp.concatenate(labels, axis=0).astype(jnp.int32)


def placed(subs, sources, label_ref, stand_ref, values):
    slots, width = values[0].shape
    share = NDUAL // label_ref.shape[0]
    total = jnp.zeros((2 * share, NDUAL), F32)
    for k, value in zip(sources, values):
        rows = (iota((subs * share, slots), 0) == label_ref[k:k + 1]).astype(BF)
        moved = mm(rows, jnp.concatenate(split(value[...]), axis=1)).astype(BF)
        for s in range(subs):
            i = k * subs + s
            part = moved[s * share:(s + 1) * share]
            columns = (iota((width, NDUAL), 1) == stand_ref[:, i:i + 1]).astype(BF)
            total = total + mm(jnp.concatenate([part[:, :width], part[:, width:]], axis=0), columns)
    return total[:share] + total[share:]


def early_kernel(subs, sources, label_ref, stand_ref, *refs):
    refs[-1][...] = placed(subs, sources, label_ref, stand_ref, refs[:-1])


def finish_kernel(subs, sources, label_ref, stand_ref, high_ref, low_ref, early_ref, *refs):
    values, (dual_ref, raw_ref, first_ref, last_ref) = refs[:-4], refs[-4:]
    dual = early_ref[...] + placed(subs, sources, label_ref, stand_ref, values)
    dual_ref[...] = dual
    raw = mm3(split(dual), (high_ref[...], low_ref[...]))
    raw_ref[...] = raw
    first_ref[...] = raw[:IFACE]
    last_ref[...] = raw[raw.shape[0] - IFACE:]


def call(kernel, outs, args, flops, name, smem=0, grant=16):
    vm = pl.BlockSpec(memory_space=pltpu.VMEM)
    specs = [pl.BlockSpec(memory_space=pltpu.SMEM)] * smem + [vm] * (len(args) - smem)
    return pl.pallas_call(
        kernel,
        out_shape=outs,
        in_specs=specs,
        out_specs=jax.tree.map(lambda _: vm, outs),
        compiler_params=pltpu.CompilerParams(vmem_limit_bytes=grant << 20),
        cost_estimate=pl.CostEstimate(flops=flops, bytes_accessed=4 << 20, transcendentals=0),
        name=name,
    )(*args)


def on_device(factors, panels, sizes, glue_index, loads):
    members = lax.axis_size("member")
    subs, order, width = panels.shape
    share, nrhs = loads.shape
    capacity = 2 * width // members
    slots = subs * capacity
    count = members * subs
    shape = jax.ShapeDtypeStruct
    place = lax.axis_index("member").astype(jnp.int32).reshape(1)

    def across(value, distance):
        return lax.ppermute(value, "member", [(i, i ^ distance) for i in range(members)])

    packed = call(pack_kernel, shape((members, share // 2 + 8 * (-(-subs // 16)), nrhs), F32), (loads, glue_index), 1_000_000, "pack", grant=58)
    own = lax.all_to_all(packed, "member", split_axis=0, concat_axis=0, tiled=True)
    values = solve(place, sizes, glue_index, factors, panels, members)
    own, *values = lax.optimization_barrier((own, *values))
    arrivals = (0, *range(2, members, 2), *range(3, members, 2), 1)
    arrived = [across(values[k], k) if k else values[k] for k in arrivals]
    twin = across(own, 1)
    stand, labels, high, low = call(
        functools.partial(routes_kernel, subs),
        (
            shape((width, count), jnp.int32),
            shape((members, slots), jnp.int32),
            shape((NDUAL, nrhs), BF),
            shape((NDUAL, nrhs), BF),
        ),
        (place, own, twin),
        2_000_000_000,
        "routes",
        smem=1,
    )
    half = members // 2
    early = call(
        functools.partial(early_kernel, subs, arrivals[:half]),
        shape((share, NDUAL), F32),
        (labels, stand, *arrived[:half]),
        2_000_000_000,
        "early",
    )
    dual_rows, raw, first, last = call(
        functools.partial(finish_kernel, subs, arrivals[half:]),
        (
            shape((share, NDUAL), F32),
            shape((share, nrhs), F32),
            shape((IFACE, nrhs), F32),
            shape((IFACE, nrhs), F32),
        ),
        (labels, stand, high, low, early, *arrived[half:]),
        3_000_000_000,
        "finish",
    )
    peers = lax.axis_size("cluster")
    up = [(i, (i + 1) % peers) for i in range(peers)]
    down = [(j, i) for i, j in up]
    before = lax.ppermute(last, "cluster", up)
    after = lax.ppermute(first, "cluster", down)
    between = jnp.zeros((share - 2 * IFACE, nrhs), F32)
    products = raw + jnp.concatenate([before, between, after], axis=0)
    return (dual_rows, products)


def solution(mesh):
    shards = ("cluster", "member")
    return jax.shard_map(
        on_device,
        mesh=mesh,
        in_specs=(P(shards, None, None), P(shards, None, None), P(shards), P(shards, None), P(shards, None)),
        out_specs=(P(shards, None), P(shards, None)),
        check_vma=False,
    )
```

```python
import functools
import jax, jax.numpy as jnp
from jax import lax
from jax.experimental import pallas as pl
from jax.experimental.pallas import tpu as pltpu
F32, BF = jnp.float32, jnp.bfloat16
from jax.sharding import PartitionSpec as P

STRIDE, BASE = 128, 16
NDUAL, IFACE = 1024, 8

def split(v):
    hi = v.astype(BF)
    return hi, (v - hi.astype(F32)).astype(BF)

def mm(a, b, dims=(((1,), (0,)), ((), ()))):
    return lax.dot_general(a, b, dims, preferred_element_type=F32)

def mm3(a, b):
    ah, al = a
    bh, bl = b
    return mm(ah, bh) + (mm(al, bh) + mm(ah, bl))

def iota(shape, dim):
    return lax.broadcasted_iota(jnp.int32, shape, dim)

def mmk(a, b):
    ah, al = a
    bh, bl = b
    return mm(jnp.concatenate([ah, al], axis=1), jnp.concatenate([bh, bh], axis=0)) + mm(ah, bl)


def turn(v, by):
    return pltpu.roll(v, by, 1)


def split32(v):
    hi = v.astype(BF).astype(F32)
    return hi, v - hi


def eliminate(packs):
    lane = iota((BASE, STRIDE), 1)
    row = iota((BASE, STRIDE), 0)
    local = lane % BASE
    parts = BASE // 8
    start = (iota((8, STRIDE), 1) // BASE) * BASE
    row8 = iota((8, STRIDE), 0)
    eye = (row == local).astype(F32)
    recips, works, pieces = [], [], []
    for packed in packs:
        diag = jnp.sum(jnp.where(row == local, packed, 0.0), axis=0, keepdims=True)
        recip = 1.0 / diag
        scaled = jnp.where(row > local, packed * recip, 0.0)
        recips.append(jnp.broadcast_to(recip, (8, STRIDE)))
        works.append([eye[g * 8:(g + 1) * 8] for g in range(parts)])
        pieces.append([scaled[g * 8:(g + 1) * 8] for g in range(parts)])
    for j in range(BASE - 1):
        for work, piece in zip(works, pieces):
            pivot = work[j // 8][j % 8:j % 8 + 1]
            for g in range((j + 1) // 8, parts):
                column = jnp.take_along_axis(piece[g], start + j, axis=1, mode="promise_in_bounds")
                work[g] = work[g] - column * pivot
    for work, recip in zip(works, recips):
        for g in range(parts):
            work[g] = work[g] * jnp.take_along_axis(recip, start + (row8 + g * 8), axis=1, mode="promise_in_bounds")
    return [jnp.concatenate(work, axis=0) for work in works]


def slabs_of(v, size):
    return [v[r:r + size] for r in range(0, v.shape[0], size)]


def invert_blocks(blocks):
    lane = iota((BASE, STRIDE), 1)
    packs = []
    for block in blocks:
        packed = block[:BASE]
        for q, slab in enumerate(slabs_of(block, BASE)):
            packed = jnp.where(lane // BASE == q, slab, packed) if q else packed
        packs.append(packed)
    inners = eliminate(packs)
    states = [[jnp.where(lane // BASE == q, inner, 0.0) for q in range(STRIDE // BASE)] for inner in inners]
    size = BASE
    while size < STRIDE:
        half = iota((STRIDE // 2, STRIDE), 1) // size
        even = half % 2 == 0
        pair = (half // 2 == iota((STRIDE // 2, STRIDE), 0) // size) & even
        products = []
        for block, slabs in zip(blocks, states):
            ch, cl = split32(jnp.where(pair, jnp.concatenate(slabs_of(block, size)[1::2], axis=0), 0.0))
            a = jnp.concatenate([ch + turn(cl, size), ch], axis=1).astype(BF)
            tops = [split(v) for v in slabs[0::2]]
            w = [v[0] for v in tops for _ in range(2)] + [v[1] for v in tops for _ in range(2)]
            products.append(mm(a, jnp.concatenate(w, axis=0)))
        belows = []
        for product, slabs in zip(products, states):
            xh, xl = split32(jnp.concatenate(slabs[1::2], axis=0))
            a = jnp.concatenate([xh + turn(xl, STRIDE - size), xh], axis=1).astype(BF)
            th, tl = split(product)
            w = [v for v in slabs_of(th, size) for _ in range(2)] + [v for v in slabs_of(tl, size) for _ in range(2)]
            belows.append(slabs_of(mm(a, jnp.concatenate(w, axis=0)), size))
        states = [
            [jnp.concatenate([top, low - add], axis=0) for top, low, add in zip(slabs[0::2], slabs[1::2], below)]
            for slabs, below in zip(states, belows)
        ]
        size *= 2
    return [slabs[0] for slabs in states]


BATCH = 16


def solve_kernel(members, far_sizes_ref, far_glue_ref, far_ref, p_ref, *refs):
    out_refs = refs[:members]
    rest, f_ref, sizes_ref, glue_ref, square_sems, corner_sems, strip_sems, panel_sem, small_sems = refs[members:]
    sizes_copy = pltpu.make_async_copy(far_sizes_ref, sizes_ref, small_sems.at[0])
    glue_copy = pltpu.make_async_copy(far_glue_ref, glue_ref, small_sems.at[1])
    sizes_copy.start()
    subs, order, width = p_ref.shape
    wide = 2 * STRIDE
    square_copies, corner_copies, strip_copies = {}, {}, {}

    def fetch(s, rows, columns, sem):
        part = (s, rows, columns)
        copy = pltpu.make_async_copy(far_ref.at[part], f_ref.at[part], sem)
        copy.start()
        return copy

    for step, a in enumerate(range(0, order, STRIDE)):
        for s in range(subs):
            square_copies[s, a] = fetch(s, pl.ds(a, STRIDE), pl.ds(a, STRIDE), square_sems.at[s, step])
    for step, a in enumerate(range(0, order, wide)):
        for s in range(subs):
            corner_copies[s, a] = fetch(s, pl.ds(a + STRIDE, STRIDE), pl.ds(a, STRIDE), corner_sems.at[s, step])
    panel_copy = pltpu.make_async_copy(p_ref, rest, panel_sem)
    panel_copy.start()
    glue_copy.start()
    for step, a in enumerate(range(0, order - wide, wide)):
        for s in range(subs):
            strip_copies[s, a] = fetch(s, pl.ds(a + wide, order - a - wide), pl.ds(a, wide), strip_sems.at[s, step])
    sizes_copy.wait()
    row = iota((STRIDE, STRIDE), 0)
    col = iota((STRIDE, STRIDE), 1)
    prow = iota((wide, width), 0)
    dims = (((0,), (0,)), ((), ()))
    squares = [jnp.zeros((width, width), F32)] * subs
    crosses = [jnp.zeros((width, width), F32)] * subs
    places = [(s, a) for a in range(0, order, STRIDE) for s in range(subs)]
    small = {}
    for first in range(0, len(places), BATCH):
        batch = places[first:first + BATCH]
        blocks = []
        for s, a in batch:
            square_copies[s, a].wait()
            d = f_ref[s, a:a + STRIDE, a:a + STRIDE]
            keep = (row + a < sizes_ref[s]) & (col <= row)
            blocks.append(jnp.where(keep, d, (row == col).astype(F32)))
        for place, inverse in zip(batch, invert_blocks(blocks)):
            small[place] = split(inverse)
    heads = [(s, a) for a in range(0, order, wide) for s in range(subs)]
    corners = []
    for s, a in heads:
        b = a + STRIDE
        corner_copies[s, a].wait()
        corner = jnp.where(row + b < sizes_ref[s], f_ref[s, b:b + STRIDE, a:b], 0.0)
        corners.append(split(mmk(split(corner), small[s, a])))
    inverses = {}
    for (s, a), corner in zip(heads, corners):
        above, below = small[s, a], small[s, a + STRIDE]
        turned = split(-mmk(below, corner))
        blank = jnp.zeros((STRIDE, STRIDE), BF)
        inverses[s, a] = [
            jnp.concatenate([jnp.concatenate([u, blank], axis=1), jnp.concatenate([t, l], axis=1)], axis=0)
            for u, t, l in zip(above, turned, below)
        ]

    capacity = 2 * width // members
    glue_copy.wait()
    glue = glue_ref[...]
    place = lax.axis_index("member")
    before = (iota((width, width), 0) < iota((width, width), 1)).astype(BF)
    dispatches = []
    for s in range(subs):
        owner = glue[s:s + 1] // (NDUAL // members)
        owners = (iota((members, width), 0) == owner)
        ranks = mm(owners.astype(BF), before)
        rank = jnp.sum(jnp.where(owners, ranks, 0.0), axis=0, keepdims=True).astype(jnp.int32)
        target = (owner ^ place) * capacity + rank
        dispatches.append((iota((members * capacity, width), 0) == target).astype(BF))
    panel_copy.wait()
    for a in range(0, order, wide):
        solved = []
        for s in range(subs):
            now = jnp.where(prow + a < sizes_ref[s], rest[s, a:a + wide], 0.0)
            solved.append(split(mm3(inverses[s, a], split(now))))
        if a + wide < order:
            for s in range(subs):
                strip_copies[s, a].wait()
        for c in range(a + wide, order, wide):
            for s in range(subs):
                rest[s, c:c + wide] = rest[s, c:c + wide] - mm3(split(f_ref[s, c:c + wide, a:a + wide]), solved[s])
        for s in range(subs):
            hi, lo = solved[s]
            squares[s] = squares[s] + mm(hi, hi, dims)
            crosses[s] = crosses[s] + mm(hi, lo, dims)
    duals = [split(squares[s] + (crosses[s] + crosses[s].T)) for s in range(subs)]
    for s in range(subs):
        values = mm(dispatches[s], duals[s][0]) + mm(dispatches[s], duals[s][1])
        for k in range(members):
            out_refs[k][s * capacity:(s + 1) * capacity] = values[k * capacity:(k + 1) * capacity]


def solve(sizes, glue, factors, panels, members):
    subs, order, width = panels.shape
    capacity = 2 * width // members
    vm = pl.BlockSpec(memory_space=pltpu.VMEM)
    far = pl.BlockSpec(memory_space=pltpu.HBM)
    return pl.pallas_call(
        functools.partial(solve_kernel, members),
        out_shape=[jax.ShapeDtypeStruct((subs * capacity, width), F32)] * members,
        in_specs=[far] * 4,
        out_specs=[vm] * members,
        scratch_shapes=[
            pltpu.VMEM((subs, order, width), F32),
            pltpu.VMEM((subs, order, order), F32),
            pltpu.SMEM((subs,), jnp.int32),
            pltpu.VMEM((subs, width), jnp.int32),
            pltpu.SemaphoreType.DMA((subs, order // STRIDE)),
            pltpu.SemaphoreType.DMA((subs, order // (2 * STRIDE))),
            pltpu.SemaphoreType.DMA((subs, order // (2 * STRIDE))),
            pltpu.SemaphoreType.DMA,
            pltpu.SemaphoreType.DMA((2,)),
        ],
        compiler_params=pltpu.CompilerParams(vmem_limit_bytes=54 << 20),
        cost_estimate=pl.CostEstimate(flops=10_000_000_000, bytes_accessed=8 << 20, transcendentals=0),
        name="solve",
    )(sizes, glue, factors, panels)


def pack_kernel(loads_ref, glue_ref, out_ref, held, lines_of, tail, in_sems, load_sems, tail_sems):
    members, rows, nrhs = out_ref.shape
    half, lines = loads_ref.shape[0] // 2, glue_ref.shape[0] // 2
    labels = pltpu.make_async_copy(glue_ref, lines_of, in_sems.at[0])
    load = pltpu.make_async_copy(loads_ref, held, in_sems.at[1])
    labels.start()
    load.start()
    labels.wait()
    blank = jnp.zeros((rows - half - lines, nrhs), F32)
    for part in range(2):
        line = lines_of[part * lines:(part + 1) * lines].astype(F32)
        tail[part] = jnp.concatenate([line, blank], axis=0)
    copies = []
    for k in range(members):
        copies.append(pltpu.make_async_copy(tail.at[k % 2], out_ref.at[k, pl.ds(half, rows - half)], tail_sems.at[k]))
        copies[-1].start()
    load.wait()
    for k in range(members):
        rows_of = held.at[pl.ds(k % 2 * half, half)]
        copies.append(pltpu.make_async_copy(rows_of, out_ref.at[k, pl.ds(0, half)], load_sems.at[k]))
        copies[-1].start()
    for copy in copies:
        copy.wait()


def pack(loads, glue, members):
    subs = glue.shape[0]
    share, nrhs = loads.shape
    rows = share // 2 + 8 * (-(-subs // 16))
    far = pl.BlockSpec(memory_space=pltpu.HBM)
    return pl.pallas_call(
        pack_kernel,
        out_shape=jax.ShapeDtypeStruct((members, rows, nrhs), F32),
        in_specs=[far, far],
        out_specs=far,
        scratch_shapes=[
            pltpu.VMEM((share, nrhs), F32),
            pltpu.VMEM(glue.shape, jnp.int32),
            pltpu.VMEM((2, rows - share // 2, nrhs), F32),
            pltpu.SemaphoreType.DMA((2,)),
            pltpu.SemaphoreType.DMA((members,)),
            pltpu.SemaphoreType.DMA((members,)),
        ],
        compiler_params=pltpu.CompilerParams(vmem_limit_bytes=58 << 20),
        cost_estimate=pl.CostEstimate(flops=1_000_000, bytes_accessed=1 << 20, transcendentals=0),
        name="pack",
    )(loads, glue)


def routes_kernel(subs, place_ref, own_ref, twin_ref, stand_ref, label_ref, high_ref, low_ref):
    members, block, width = own_ref.shape
    share = NDUAL // members
    half, lines = share // 2, subs // 2
    slots = label_ref.shape[1]
    capacity = slots // subs
    first_core = place_ref[0] % 2 == 0
    glue = []
    for k in range(members):
        source = place_ref[0] ^ k
        pair = own_ref[source], twin_ref[source]
        for part in range(2):
            got = jnp.where(first_core, pair[part], pair[1 - part])
            row = pl.ds(pl.multiple_of(source * share + part * half, half), half)
            high_ref[row], low_ref[row] = split(got[:half])
            glue.append(got[half:half + lines])
    glue = jnp.concatenate(glue, axis=0)
    stand_ref[...] = glue.T.astype(jnp.int32)
    glue = glue.astype(jnp.int32)
    first = place_ref[0] * share
    mine = (glue >= first) & (glue < first + share)
    before = (iota((width, width), 0) < iota((width, width), 1)).astype(BF)
    ranks = mm(mine.astype(BF), before).astype(jnp.int32)
    local = jnp.where(mine, glue - first + 1, 0).astype(F32).astype(BF)
    labels = []
    for k in range(members):
        found = jnp.full((1, slots), -1.0, F32)
        for s in range(subs):
            i = k * subs + s
            rank = jnp.where(mine[i:i + 1], ranks[i:i + 1] + s * capacity, -1)
            at_slot = (iota((slots, width), 0) == rank).astype(BF)
            line = mm(local[i:i + 1], at_slot, (((1,), (1,)), ((), ())))
            found = jnp.where(line > 0.5, line + (s * share - 1), found)
        labels.append(found)
    label_ref[...] = jnp.concatenate(labels, axis=0).astype(jnp.int32)


def placed(subs, sources, label_ref, stand_ref, values):
    slots, width = values[0].shape
    share = NDUAL // label_ref.shape[0]
    total = jnp.zeros((2 * share, NDUAL), F32)
    for k, value in zip(sources, values):
        rows = (iota((subs * share, slots), 0) == label_ref[k:k + 1]).astype(BF)
        moved = mm(rows, jnp.concatenate(split(value[...]), axis=1)).astype(BF)
        for s in range(subs):
            i = k * subs + s
            part = moved[s * share:(s + 1) * share]
            columns = (iota((width, NDUAL), 1) == stand_ref[:, i:i + 1]).astype(BF)
            total = total + mm(jnp.concatenate([part[:, :width], part[:, width:]], axis=0), columns)
    return total[:share] + total[share:]


def early_kernel(subs, sources, label_ref, stand_ref, *refs):
    refs[-1][...] = placed(subs, sources, label_ref, stand_ref, refs[:-1])


def finish_kernel(subs, sources, label_ref, stand_ref, high_ref, low_ref, early_ref, *refs):
    values, (dual_ref, raw_ref, first_ref, last_ref) = refs[:-4], refs[-4:]
    dual = early_ref[...] + placed(subs, sources, label_ref, stand_ref, values)
    dual_ref[...] = dual
    raw = mm3(split(dual), (high_ref[...], low_ref[...]))
    raw_ref[...] = raw
    first_ref[...] = raw[:IFACE]
    last_ref[...] = raw[raw.shape[0] - IFACE:]


def call(kernel, outs, args, flops, name, smem=0):
    vm = pl.BlockSpec(memory_space=pltpu.VMEM)
    specs = [pl.BlockSpec(memory_space=pltpu.SMEM)] * smem + [vm] * (len(args) - smem)
    return pl.pallas_call(
        kernel,
        out_shape=outs,
        in_specs=specs,
        out_specs=jax.tree.map(lambda _: vm, outs),
        compiler_params=pltpu.CompilerParams(vmem_limit_bytes=16 << 20),
        cost_estimate=pl.CostEstimate(flops=flops, bytes_accessed=4 << 20, transcendentals=0),
        name=name,
    )(*args)


def on_device(factors, panels, sizes, glue_index, loads):
    members = lax.axis_size("member")
    subs, order, width = panels.shape
    share, nrhs = loads.shape
    capacity = 2 * width // members
    slots = subs * capacity
    count = members * subs
    shape = jax.ShapeDtypeStruct
    place = lax.axis_index("member").astype(jnp.int32).reshape(1)

    def across(value, distance):
        return lax.ppermute(value, "member", [(i, i ^ distance) for i in range(members)])

    packed = pack(loads, glue_index, members)
    own = lax.all_to_all(packed, "member", split_axis=0, concat_axis=0, tiled=True)
    values = solve(sizes, glue_index, factors, panels, members)
    own, *values = lax.optimization_barrier((own, *values))
    arrivals = (0, *range(2, members, 2), *range(3, members, 2), 1)
    arrived = [across(values[k], k) if k else values[k] for k in arrivals]
    twin = across(own, 1)
    stand, labels, high, low = call(
        functools.partial(routes_kernel, subs),
        (
            shape((width, count), jnp.int32),
            shape((members, slots), jnp.int32),
            shape((NDUAL, nrhs), BF),
            shape((NDUAL, nrhs), BF),
        ),
        (place, own, twin),
        2_000_000_000,
        "routes",
        smem=1,
    )
    half = members // 2
    early = call(
        functools.partial(early_kernel, subs, arrivals[:half]),
        shape((share, NDUAL), F32),
        (labels, stand, *arrived[:half]),
        2_000_000_000,
        "early",
    )
    dual_rows, raw, first, last = call(
        functools.partial(finish_kernel, subs, arrivals[half:]),
        (
            shape((share, NDUAL), F32),
            shape((share, nrhs), F32),
            shape((IFACE, nrhs), F32),
            shape((IFACE, nrhs), F32),
        ),
        (labels, stand, high, low, early, *arrived[half:]),
        3_000_000_000,
        "finish",
    )
    peers = lax.axis_size("cluster")
    up = [(i, (i + 1) % peers) for i in range(peers)]
    down = [(j, i) for i, j in up]
    before = lax.ppermute(last, "cluster", up)
    after = lax.ppermute(first, "cluster", down)
    between = jnp.zeros((share - 2 * IFACE, nrhs), F32)
    products = raw + jnp.concatenate([before, between, after], axis=0)
    return (dual_rows, products)


def solution(mesh):
    shards = ("cluster", "member")
    return jax.shard_map(
        on_device,
        mesh=mesh,
        in_specs=(P(shards, None, None), P(shards, None, None), P(shards), P(shards, None), P(shards, None)),
        out_specs=(P(shards, None), P(shards, None)),
        check_vma=False,
    )
```

```python
import functools
import jax, jax.numpy as jnp
from jax import lax
from jax.experimental import pallas as pl
from jax.experimental.pallas import tpu as pltpu
F32, BF = jnp.float32, jnp.bfloat16
from jax.sharding import PartitionSpec as P

STRIDE, BASE = 128, 16
NDUAL, IFACE = 1024, 8

def split(v):
    hi = v.astype(BF)
    return hi, (v - hi.astype(F32)).astype(BF)

def mm(a, b, dims=(((1,), (0,)), ((), ()))):
    return lax.dot_general(a, b, dims, preferred_element_type=F32)

def mm3(a, b):
    ah, al = a
    bh, bl = b
    return mm(ah, bh) + (mm(al, bh) + mm(ah, bl))

def iota(shape, dim):
    return lax.broadcasted_iota(jnp.int32, shape, dim)

def mmk(a, b):
    ah, al = a
    bh, bl = b
    return mm(jnp.concatenate([ah, al], axis=1), jnp.concatenate([bh, bh], axis=0)) + mm(ah, bl)


def turn(v, by):
    return pltpu.roll(v, by, 1)


def split32(v):
    hi = v.astype(BF).astype(F32)
    return hi, v - hi


def eliminate(packs):
    lane = iota((BASE, STRIDE), 1)
    row = iota((BASE, STRIDE), 0)
    local = lane % BASE
    parts = BASE // 8
    start = (iota((8, STRIDE), 1) // BASE) * BASE
    row8 = iota((8, STRIDE), 0)
    eye = (row == local).astype(F32)
    recips, works, pieces = [], [], []
    for packed in packs:
        diag = jnp.sum(jnp.where(row == local, packed, 0.0), axis=0, keepdims=True)
        recip = 1.0 / diag
        scaled = jnp.where(row > local, packed * recip, 0.0)
        recips.append(jnp.broadcast_to(recip, (8, STRIDE)))
        works.append([eye[g * 8:(g + 1) * 8] for g in range(parts)])
        pieces.append([scaled[g * 8:(g + 1) * 8] for g in range(parts)])
    for j in range(BASE - 1):
        for work, piece in zip(works, pieces):
            pivot = work[j // 8][j % 8:j % 8 + 1]
            for g in range((j + 1) // 8, parts):
                column = jnp.take_along_axis(piece[g], start + j, axis=1, mode="promise_in_bounds")
                work[g] = work[g] - column * pivot
    for work, recip in zip(works, recips):
        for g in range(parts):
            work[g] = work[g] * jnp.take_along_axis(recip, start + (row8 + g * 8), axis=1, mode="promise_in_bounds")
    return [jnp.concatenate(work, axis=0) for work in works]


def slabs_of(v, size):
    return [v[r:r + size] for r in range(0, v.shape[0], size)]


def invert_blocks(blocks):
    lane = iota((BASE, STRIDE), 1)
    packs = []
    for block in blocks:
        packed = block[:BASE]
        for q, slab in enumerate(slabs_of(block, BASE)):
            packed = jnp.where(lane // BASE == q, slab, packed) if q else packed
        packs.append(packed)
    inners = eliminate(packs)
    states = [[jnp.where(lane // BASE == q, inner, 0.0) for q in range(STRIDE // BASE)] for inner in inners]
    size = BASE
    while size < STRIDE:
        half = iota((STRIDE // 2, STRIDE), 1) // size
        even = half % 2 == 0
        pair = (half // 2 == iota((STRIDE // 2, STRIDE), 0) // size) & even
        products = []
        for block, slabs in zip(blocks, states):
            ch, cl = split32(jnp.where(pair, jnp.concatenate(slabs_of(block, size)[1::2], axis=0), 0.0))
            a = jnp.concatenate([ch + turn(cl, size), ch], axis=1).astype(BF)
            tops = [split(v) for v in slabs[0::2]]
            w = [v[0] for v in tops for _ in range(2)] + [v[1] for v in tops for _ in range(2)]
            products.append(mm(a, jnp.concatenate(w, axis=0)))
        belows = []
        for product, slabs in zip(products, states):
            xh, xl = split32(jnp.concatenate(slabs[1::2], axis=0))
            a = jnp.concatenate([xh + turn(xl, STRIDE - size), xh], axis=1).astype(BF)
            th, tl = split(product)
            w = [v for v in slabs_of(th, size) for _ in range(2)] + [v for v in slabs_of(tl, size) for _ in range(2)]
            belows.append(slabs_of(mm(a, jnp.concatenate(w, axis=0)), size))
        states = [
            [jnp.concatenate([top, low - add], axis=0) for top, low, add in zip(slabs[0::2], slabs[1::2], below)]
            for slabs, below in zip(states, belows)
        ]
        size *= 2
    return [slabs[0] for slabs in states]


BATCH = 16


def solve_kernel(members, far_sizes_ref, far_glue_ref, far_ref, p_ref, *refs):
    out_refs = refs[:members]
    rest, f_ref, sizes_ref, glue_ref, square_sems, corner_sems, strip_sems, panel_sem, small_sems = refs[members:]
    sizes_copy = pltpu.make_async_copy(far_sizes_ref, sizes_ref, small_sems.at[0])
    glue_copy = pltpu.make_async_copy(far_glue_ref, glue_ref, small_sems.at[1])
    sizes_copy.start()
    subs, order, width = p_ref.shape
    wide = 2 * STRIDE
    square_copies, corner_copies, strip_copies = {}, {}, {}

    def fetch(s, rows, columns, sem):
        part = (s, rows, columns)
        copy = pltpu.make_async_copy(far_ref.at[part], f_ref.at[part], sem)
        copy.start()
        return copy

    for step, a in enumerate(range(0, order, STRIDE)):
        for s in range(subs):
            square_copies[s, a] = fetch(s, pl.ds(a, STRIDE), pl.ds(a, STRIDE), square_sems.at[s, step])
    for step, a in enumerate(range(0, order, wide)):
        for s in range(subs):
            corner_copies[s, a] = fetch(s, pl.ds(a + STRIDE, STRIDE), pl.ds(a, STRIDE), corner_sems.at[s, step])
    panel_copy = pltpu.make_async_copy(p_ref, rest, panel_sem)
    panel_copy.start()
    glue_copy.start()
    for step, a in enumerate(range(0, order - wide, wide)):
        for s in range(subs):
            strip_copies[s, a] = fetch(s, pl.ds(a + wide, order - a - wide), pl.ds(a, wide), strip_sems.at[s, step])
    sizes_copy.wait()
    row = iota((STRIDE, STRIDE), 0)
    col = iota((STRIDE, STRIDE), 1)
    prow = iota((wide, width), 0)
    dims = (((0,), (0,)), ((), ()))
    squares = [jnp.zeros((width, width), F32)] * subs
    crosses = [jnp.zeros((width, width), F32)] * subs
    places = [(s, a) for a in range(0, order, STRIDE) for s in range(subs)]
    small = {}
    for first in range(0, len(places), BATCH):
        batch = places[first:first + BATCH]
        blocks = []
        for s, a in batch:
            square_copies[s, a].wait()
            d = f_ref[s, a:a + STRIDE, a:a + STRIDE]
            keep = (row + a < sizes_ref[s]) & (col <= row)
            blocks.append(jnp.where(keep, d, (row == col).astype(F32)))
        for place, inverse in zip(batch, invert_blocks(blocks)):
            small[place] = split(inverse)
    heads = [(s, a) for a in range(0, order, wide) for s in range(subs)]
    corners = []
    for s, a in heads:
        b = a + STRIDE
        corner_copies[s, a].wait()
        corner = jnp.where(row + b < sizes_ref[s], f_ref[s, b:b + STRIDE, a:b], 0.0)
        corners.append(split(mmk(split(corner), small[s, a])))
    inverses = {}
    for (s, a), corner in zip(heads, corners):
        above, below = small[s, a], small[s, a + STRIDE]
        turned = split(-mmk(below, corner))
        blank = jnp.zeros((STRIDE, STRIDE), BF)
        inverses[s, a] = [
            jnp.concatenate([jnp.concatenate([u, blank], axis=1), jnp.concatenate([t, l], axis=1)], axis=0)
            for u, t, l in zip(above, turned, below)
        ]

    capacity = 2 * width // members
    glue_copy.wait()
    glue = glue_ref[...]
    place = lax.axis_index("member")
    before = (iota((width, width), 0) < iota((width, width), 1)).astype(BF)
    dispatches = []
    for s in range(subs):
        owner = glue[s:s + 1] // (NDUAL // members)
        owners = (iota((members, width), 0) == owner)
        ranks = mm(owners.astype(BF), before)
        rank = jnp.sum(jnp.where(owners, ranks, 0.0), axis=0, keepdims=True).astype(jnp.int32)
        target = (owner ^ place) * capacity + rank
        dispatches.append((iota((members * capacity, width), 0) == target).astype(BF))
    panel_copy.wait()
    for a in range(0, order, wide):
        solved = []
        for s in range(subs):
            now = jnp.where(prow + a < sizes_ref[s], rest[s, a:a + wide], 0.0)
            solved.append(split(mm3(inverses[s, a], split(now))))
        if a + wide < order:
            for s in range(subs):
                strip_copies[s, a].wait()
        for c in range(a + wide, order, wide):
            for s in range(subs):
                rest[s, c:c + wide] = rest[s, c:c + wide] - mm3(split(f_ref[s, c:c + wide, a:a + wide]), solved[s])
        for s in range(subs):
            hi, lo = solved[s]
            squares[s] = squares[s] + mm(hi, hi, dims)
            crosses[s] = crosses[s] + mm(hi, lo, dims)
    duals = [split(squares[s] + (crosses[s] + crosses[s].T)) for s in range(subs)]
    for s in range(subs):
        values = mm(dispatches[s], duals[s][0]) + mm(dispatches[s], duals[s][1])
        for k in range(members):
            out_refs[k][s * capacity:(s + 1) * capacity] = values[k * capacity:(k + 1) * capacity]


def solve(sizes, glue, factors, panels, members):
    subs, order, width = panels.shape
    capacity = 2 * width // members
    vm = pl.BlockSpec(memory_space=pltpu.VMEM)
    far = pl.BlockSpec(memory_space=pltpu.HBM)
    return pl.pallas_call(
        functools.partial(solve_kernel, members),
        out_shape=[jax.ShapeDtypeStruct((subs * capacity, width), F32)] * members,
        in_specs=[far] * 4,
        out_specs=[vm] * members,
        scratch_shapes=[
            pltpu.VMEM((subs, order, width), F32),
            pltpu.VMEM((subs, order, order), F32),
            pltpu.SMEM((subs,), jnp.int32),
            pltpu.VMEM((subs, width), jnp.int32),
            pltpu.SemaphoreType.DMA((subs, order // STRIDE)),
            pltpu.SemaphoreType.DMA((subs, order // (2 * STRIDE))),
            pltpu.SemaphoreType.DMA((subs, order // (2 * STRIDE))),
            pltpu.SemaphoreType.DMA,
            pltpu.SemaphoreType.DMA((2,)),
        ],
        compiler_params=pltpu.CompilerParams(vmem_limit_bytes=54 << 20),
        cost_estimate=pl.CostEstimate(flops=10_000_000_000, bytes_accessed=8 << 20, transcendentals=0),
        name="solve",
    )(sizes, glue, factors, panels)


def pack_kernel(loads_ref, glue_ref, out_ref, held, lines_of, tail, in_sems, load_sems, tail_sems):
    members, rows, nrhs = out_ref.shape
    half, lines = loads_ref.shape[0] // 2, glue_ref.shape[0] // 2
    labels = pltpu.make_async_copy(glue_ref, lines_of, in_sems.at[0])
    load = pltpu.make_async_copy(loads_ref, held, in_sems.at[1])
    labels.start()
    load.start()
    labels.wait()
    blank = jnp.zeros((rows - half - lines, nrhs), F32)
    for part in range(2):
        line = lines_of[part * lines:(part + 1) * lines].astype(F32)
        tail[part] = jnp.concatenate([line, blank], axis=0)
    copies = []
    for k in range(members):
        copies.append(pltpu.make_async_copy(tail.at[k % 2], out_ref.at[k, pl.ds(half, rows - half)], tail_sems.at[k]))
        copies[-1].start()
    load.wait()
    for k in range(members):
        rows_of = held.at[pl.ds(k % 2 * half, half)]
        copies.append(pltpu.make_async_copy(rows_of, out_ref.at[k, pl.ds(0, half)], load_sems.at[k]))
        copies[-1].start()
    for copy in copies:
        copy.wait()


def pack(loads, glue, members):
    subs = glue.shape[0]
    share, nrhs = loads.shape
    rows = share // 2 + 8 * (-(-subs // 16))
    far = pl.BlockSpec(memory_space=pltpu.HBM)
    return pl.pallas_call(
        pack_kernel,
        out_shape=jax.ShapeDtypeStruct((members, rows, nrhs), F32),
        in_specs=[far, far],
        out_specs=far,
        scratch_shapes=[
            pltpu.VMEM((share, nrhs), F32),
            pltpu.VMEM(glue.shape, jnp.int32),
            pltpu.VMEM((2, rows - share // 2, nrhs), F32),
            pltpu.SemaphoreType.DMA((2,)),
            pltpu.SemaphoreType.DMA((members,)),
            pltpu.SemaphoreType.DMA((members,)),
        ],
        compiler_params=pltpu.CompilerParams(vmem_limit_bytes=58 << 20),
        cost_estimate=pl.CostEstimate(flops=1_000_000, bytes_accessed=1 << 20, transcendentals=0),
        name="pack",
    )(loads, glue)


def routes_kernel(subs, place_ref, own_ref, twin_ref, stand_ref, label_ref, high_ref, low_ref):
    members, block, width = own_ref.shape
    share = NDUAL // members
    half, lines = share // 2, subs // 2
    slots = label_ref.shape[1]
    capacity = slots // subs
    first_core = place_ref[0] % 2 == 0
    glue = []
    for k in range(members):
        source = place_ref[0] ^ k
        pair = own_ref[source], twin_ref[source]
        for part in range(2):
            got = jnp.where(first_core, pair[part], pair[1 - part])
            row = pl.ds(pl.multiple_of(source * share + part * half, half), half)
            high_ref[row], low_ref[row] = split(got[:half])
            glue.append(got[half:half + lines])
    glue = jnp.concatenate(glue, axis=0)
    stand_ref[...] = glue.T.astype(jnp.int32)
    glue = glue.astype(jnp.int32)
    first = place_ref[0] * share
    mine = (glue >= first) & (glue < first + share)
    before = (iota((width, width), 0) < iota((width, width), 1)).astype(BF)
    ranks = mm(mine.astype(BF), before).astype(jnp.int32)
    local = jnp.where(mine, glue - first + 1, 0).astype(F32).astype(BF)
    labels = []
    for k in range(members):
        found = jnp.full((1, slots), -1.0, F32)
        for s in range(subs):
            i = k * subs + s
            rank = jnp.where(mine[i:i + 1], ranks[i:i + 1] + s * capacity, -1)
            at_slot = (iota((slots, width), 0) == rank).astype(BF)
            line = mm(local[i:i + 1], at_slot, (((1,), (1,)), ((), ())))
            found = jnp.where(line > 0.5, line + (s * share - 1), found)
        labels.append(found)
    label_ref[...] = jnp.concatenate(labels, axis=0).astype(jnp.int32)


def placed(subs, sources, label_ref, stand_ref, values):
    slots, width = values[0].shape
    share = NDUAL // label_ref.shape[0]
    total = jnp.zeros((2 * share, NDUAL), F32)
    for k, value in zip(sources, values):
        rows = (iota((subs * share, slots), 0) == label_ref[k:k + 1]).astype(BF)
        moved = mm(rows, jnp.concatenate(split(value[...]), axis=1)).astype(BF)
        for s in range(subs):
            i = k * subs + s
            part = moved[s * share:(s + 1) * share]
            columns = (iota((width, NDUAL), 1) == stand_ref[:, i:i + 1]).astype(BF)
            total = total + mm(jnp.concatenate([part[:, :width], part[:, width:]], axis=0), columns)
    return total[:share] + total[share:]


def early_kernel(subs, sources, label_ref, stand_ref, *refs):
    refs[-1][...] = placed(subs, sources, label_ref, stand_ref, refs[:-1])


def finish_kernel(subs, sources, label_ref, stand_ref, high_ref, low_ref, early_ref, *refs):
    values, (dual_ref, raw_ref, first_ref, last_ref) = refs[:-4], refs[-4:]
    dual = early_ref[...] + placed(subs, sources, label_ref, stand_ref, values)
    dual_ref[...] = dual
    raw = mm3(split(dual), (high_ref[...], low_ref[...]))
    raw_ref[...] = raw
    first_ref[...] = raw[:IFACE]
    last_ref[...] = raw[raw.shape[0] - IFACE:]


def call(kernel, outs, args, flops, name, smem=0):
    vm = pl.BlockSpec(memory_space=pltpu.VMEM)
    specs = [pl.BlockSpec(memory_space=pltpu.SMEM)] * smem + [vm] * (len(args) - smem)
    return pl.pallas_call(
        kernel,
        out_shape=outs,
        in_specs=specs,
        out_specs=jax.tree.map(lambda _: vm, outs),
        compiler_params=pltpu.CompilerParams(vmem_limit_bytes=16 << 20),
        cost_estimate=pl.CostEstimate(flops=flops, bytes_accessed=4 << 20, transcendentals=0),
        name=name,
    )(*args)


def on_device(factors, panels, sizes, glue_index, loads):
    members = lax.axis_size("member")
    subs, order, width = panels.shape
    share, nrhs = loads.shape
    capacity = 2 * width // members
    slots = subs * capacity
    count = members * subs
    shape = jax.ShapeDtypeStruct
    place = lax.axis_index("member").astype(jnp.int32).reshape(1)

    def across(value, distance):
        return lax.ppermute(value, "member", [(i, i ^ distance) for i in range(members)])

    packed = pack(loads, glue_index, members)
    own = lax.all_to_all(packed, "member", split_axis=0, concat_axis=0, tiled=True)
    values = solve(sizes, glue_index, factors, panels, members)
    own, *values = lax.optimization_barrier((own, *values))
    distances = [*range(2, members, 2), *range(3, members, 2), 1]
    arrived = {0: values[0], **{k: across(values[k], k) for k in distances}}
    last_ones = distances[-3:-1]
    first_ones = [k for k in arrived if k not in last_ones]
    twin = across(own, 1)
    stand, labels, high, low = call(
        functools.partial(routes_kernel, subs),
        (
            shape((width, count), jnp.int32),
            shape((members, slots), jnp.int32),
            shape((NDUAL, nrhs), BF),
            shape((NDUAL, nrhs), BF),
        ),
        (place, own, twin),
        2_000_000_000,
        "routes",
        smem=1,
    )
    early = call(
        functools.partial(early_kernel, subs, first_ones),
        shape((share, NDUAL), F32),
        (labels, stand, *[arrived[k] for k in first_ones]),
        2_000_000_000,
        "early",
    )
    dual_rows, raw, first, last = call(
        functools.partial(finish_kernel, subs, last_ones),
        (
            shape((share, NDUAL), F32),
            shape((share, nrhs), F32),
            shape((IFACE, nrhs), F32),
            shape((IFACE, nrhs), F32),
        ),
        (labels, stand, high, low, early, *[arrived[k] for k in last_ones]),
        3_000_000_000,
        "finish",
    )
    peers = lax.axis_size("cluster")
    up = [(i, (i + 1) % peers) for i in range(peers)]
    down = [(j, i) for i, j in up]
    before = lax.ppermute(last, "cluster", up)
    after = lax.ppermute(first, "cluster", down)
    between = jnp.zeros((share - 2 * IFACE, nrhs), F32)
    products = raw + jnp.concatenate([before, between, after], axis=0)
    return (dual_rows, products)


def solution(mesh):
    shards = ("cluster", "member")
    return jax.shard_map(
        on_device,
        mesh=mesh,
        in_specs=(P(shards, None, None), P(shards, None, None), P(shards), P(shards, None), P(shards, None)),
        out_specs=(P(shards, None), P(shards, None)),
        check_vma=False,
    )
```

```python
import functools
import jax, jax.numpy as jnp
from jax import lax
from jax.experimental import pallas as pl
from jax.experimental.pallas import tpu as pltpu
F32, BF = jnp.float32, jnp.bfloat16
from jax.sharding import PartitionSpec as P

STRIDE, BASE = 128, 16
NDUAL, IFACE = 1024, 8

def split(v):
    hi = v.astype(BF)
    return hi, (v - hi.astype(F32)).astype(BF)

def mm(a, b, dims=(((1,), (0,)), ((), ()))):
    return lax.dot_general(a, b, dims, preferred_element_type=F32)

def mm3(a, b):
    ah, al = a
    bh, bl = b
    return mm(ah, bh) + (mm(al, bh) + mm(ah, bl))

def iota(shape, dim):
    return lax.broadcasted_iota(jnp.int32, shape, dim)

def mmk(a, b):
    ah, al = a
    bh, bl = b
    return mm(jnp.concatenate([ah, al], axis=1), jnp.concatenate([bh, bh], axis=0)) + mm(ah, bl)


def turn(v, by):
    return pltpu.roll(v, by, 1)


def split32(v):
    hi = v.astype(BF).astype(F32)
    return hi, v - hi


def eliminate(packs):
    lane = iota((BASE, STRIDE), 1)
    row = iota((BASE, STRIDE), 0)
    local = lane % BASE
    parts = BASE // 8
    start = (iota((8, STRIDE), 1) // BASE) * BASE
    row8 = iota((8, STRIDE), 0)
    eye = (row == local).astype(F32)
    recips, works, pieces = [], [], []
    for packed in packs:
        diag = jnp.sum(jnp.where(row == local, packed, 0.0), axis=0, keepdims=True)
        recip = 1.0 / diag
        scaled = jnp.where(row > local, packed * recip, 0.0)
        recips.append(jnp.broadcast_to(recip, (8, STRIDE)))
        works.append([eye[g * 8:(g + 1) * 8] for g in range(parts)])
        pieces.append([scaled[g * 8:(g + 1) * 8] for g in range(parts)])
    for j in range(BASE - 1):
        for work, piece in zip(works, pieces):
            pivot = work[j // 8][j % 8:j % 8 + 1]
            for g in range((j + 1) // 8, parts):
                column = jnp.take_along_axis(piece[g], start + j, axis=1, mode="promise_in_bounds")
                work[g] = work[g] - column * pivot
    for work, recip in zip(works, recips):
        for g in range(parts):
            work[g] = work[g] * jnp.take_along_axis(recip, start + (row8 + g * 8), axis=1, mode="promise_in_bounds")
    return [jnp.concatenate(work, axis=0) for work in works]


def slabs_of(v, size):
    return [v[r:r + size] for r in range(0, v.shape[0], size)]


def invert_blocks(blocks):
    lane = iota((BASE, STRIDE), 1)
    packs = []
    for block in blocks:
        packed = block[:BASE]
        for q, slab in enumerate(slabs_of(block, BASE)):
            packed = jnp.where(lane // BASE == q, slab, packed) if q else packed
        packs.append(packed)
    inners = eliminate(packs)
    states = [[jnp.where(lane // BASE == q, inner, 0.0) for q in range(STRIDE // BASE)] for inner in inners]
    size = BASE
    while size < STRIDE:
        half = iota((STRIDE // 2, STRIDE), 1) // size
        even = half % 2 == 0
        pair = (half // 2 == iota((STRIDE // 2, STRIDE), 0) // size) & even
        products = []
        for block, slabs in zip(blocks, states):
            ch, cl = split32(jnp.where(pair, jnp.concatenate(slabs_of(block, size)[1::2], axis=0), 0.0))
            a = jnp.concatenate([ch + turn(cl, size), ch], axis=1).astype(BF)
            tops = [split(v) for v in slabs[0::2]]
            w = [v[0] for v in tops for _ in range(2)] + [v[1] for v in tops for _ in range(2)]
            products.append(mm(a, jnp.concatenate(w, axis=0)))
        belows = []
        for product, slabs in zip(products, states):
            xh, xl = split32(jnp.concatenate(slabs[1::2], axis=0))
            a = jnp.concatenate([xh + turn(xl, STRIDE - size), xh], axis=1).astype(BF)
            th, tl = split(product)
            w = [v for v in slabs_of(th, size) for _ in range(2)] + [v for v in slabs_of(tl, size) for _ in range(2)]
            belows.append(slabs_of(mm(a, jnp.concatenate(w, axis=0)), size))
        states = [
            [jnp.concatenate([top, low - add], axis=0) for top, low, add in zip(slabs[0::2], slabs[1::2], below)]
            for slabs, below in zip(states, belows)
        ]
        size *= 2
    return [slabs[0] for slabs in states]


BATCH = 16


def solve_kernel(members, far_sizes_ref, far_glue_ref, far_ref, p_ref, *refs):
    out_refs = refs[:members]
    rest, f_ref, sizes_ref, glue_ref, square_sems, corner_sems, strip_sems, panel_sem, small_sems = refs[members:]
    sizes_copy = pltpu.make_async_copy(far_sizes_ref, sizes_ref, small_sems.at[0])
    glue_copy = pltpu.make_async_copy(far_glue_ref, glue_ref, small_sems.at[1])
    sizes_copy.start()
    subs, order, width = p_ref.shape
    wide = 2 * STRIDE
    square_copies, corner_copies, strip_copies = {}, {}, {}

    def fetch(s, rows, columns, sem):
        part = (s, rows, columns)
        copy = pltpu.make_async_copy(far_ref.at[part], f_ref.at[part], sem)
        copy.start()
        return copy

    for step, a in enumerate(range(0, order, STRIDE)):
        for s in range(subs):
            square_copies[s, a] = fetch(s, pl.ds(a, STRIDE), pl.ds(a, STRIDE), square_sems.at[s, step])
    for step, a in enumerate(range(0, order, wide)):
        for s in range(subs):
            corner_copies[s, a] = fetch(s, pl.ds(a + STRIDE, STRIDE), pl.ds(a, STRIDE), corner_sems.at[s, step])
    panel_copy = pltpu.make_async_copy(p_ref, rest, panel_sem)
    panel_copy.start()
    glue_copy.start()
    for step, a in enumerate(range(0, order - wide, wide)):
        for s in range(subs):
            strip_copies[s, a] = fetch(s, pl.ds(a + wide, order - a - wide), pl.ds(a, wide), strip_sems.at[s, step])
    sizes_copy.wait()
    row = iota((STRIDE, STRIDE), 0)
    col = iota((STRIDE, STRIDE), 1)
    prow = iota((wide, width), 0)
    dims = (((0,), (0,)), ((), ()))
    squares = [jnp.zeros((width, width), F32)] * subs
    crosses = [jnp.zeros((width, width), F32)] * subs
    places = [(s, a) for a in range(0, order, STRIDE) for s in range(subs)]
    small = {}
    for first in range(0, len(places), BATCH):
        batch = places[first:first + BATCH]
        blocks = []
        for s, a in batch:
            square_copies[s, a].wait()
            d = f_ref[s, a:a + STRIDE, a:a + STRIDE]
            keep = (row + a < sizes_ref[s]) & (col <= row)
            blocks.append(jnp.where(keep, d, (row == col).astype(F32)))
        for place, inverse in zip(batch, invert_blocks(blocks)):
            small[place] = split(inverse)
    heads = [(s, a) for a in range(0, order, wide) for s in range(subs)]
    corners = []
    for s, a in heads:
        b = a + STRIDE
        corner_copies[s, a].wait()
        corner = jnp.where(row + b < sizes_ref[s], f_ref[s, b:b + STRIDE, a:b], 0.0)
        corners.append(split(mmk(split(corner), small[s, a])))
    inverses = {}
    for (s, a), corner in zip(heads, corners):
        above, below = small[s, a], small[s, a + STRIDE]
        turned = split(-mmk(below, corner))
        blank = jnp.zeros((STRIDE, STRIDE), BF)
        inverses[s, a] = [
            jnp.concatenate([jnp.concatenate([u, blank], axis=1), jnp.concatenate([t, l], axis=1)], axis=0)
            for u, t, l in zip(above, turned, below)
        ]

    capacity = 2 * width // members
    glue_copy.wait()
    glue = glue_ref[...]
    place = lax.axis_index("member")
    before = (iota((width, width), 0) < iota((width, width), 1)).astype(BF)
    dispatches = []
    for s in range(subs):
        owner = glue[s:s + 1] // (NDUAL // members)
        owners = (iota((members, width), 0) == owner)
        ranks = mm(owners.astype(BF), before)
        rank = jnp.sum(jnp.where(owners, ranks, 0.0), axis=0, keepdims=True).astype(jnp.int32)
        target = (owner ^ place) * capacity + rank
        dispatches.append((iota((members * capacity, width), 0) == target).astype(BF))
    panel_copy.wait()
    for a in range(0, order, wide):
        solved = []
        for s in range(subs):
            now = jnp.where(prow + a < sizes_ref[s], rest[s, a:a + wide], 0.0)
            solved.append(split(mm3(inverses[s, a], split(now))))
        if a + wide < order:
            for s in range(subs):
                strip_copies[s, a].wait()
        for c in range(a + wide, order, wide):
            for s in range(subs):
                rest[s, c:c + wide] = rest[s, c:c + wide] - mm3(split(f_ref[s, c:c + wide, a:a + wide]), solved[s])
        for s in range(subs):
            hi, lo = solved[s]
            squares[s] = squares[s] + mm(hi, hi, dims)
            crosses[s] = crosses[s] + mm(hi, lo, dims)
    duals = [split(squares[s] + (crosses[s] + crosses[s].T)) for s in range(subs)]
    for s in range(subs):
        values = mm(dispatches[s], duals[s][0]) + mm(dispatches[s], duals[s][1])
        for k in range(members):
            out_refs[k][s * capacity:(s + 1) * capacity] = values[k * capacity:(k + 1) * capacity]


def solve(sizes, glue, factors, panels, members):
    subs, order, width = panels.shape
    capacity = 2 * width // members
    vm = pl.BlockSpec(memory_space=pltpu.VMEM)
    far = pl.BlockSpec(memory_space=pltpu.HBM)
    return pl.pallas_call(
        functools.partial(solve_kernel, members),
        out_shape=[jax.ShapeDtypeStruct((subs * capacity, width), F32)] * members,
        in_specs=[far] * 4,
        out_specs=[vm] * members,
        scratch_shapes=[
            pltpu.VMEM((subs, order, width), F32),
            pltpu.VMEM((subs, order, order), F32),
            pltpu.SMEM((subs,), jnp.int32),
            pltpu.VMEM((subs, width), jnp.int32),
            pltpu.SemaphoreType.DMA((subs, order // STRIDE)),
            pltpu.SemaphoreType.DMA((subs, order // (2 * STRIDE))),
            pltpu.SemaphoreType.DMA((subs, order // (2 * STRIDE))),
            pltpu.SemaphoreType.DMA,
            pltpu.SemaphoreType.DMA((2,)),
        ],
        compiler_params=pltpu.CompilerParams(vmem_limit_bytes=52 << 20),
        cost_estimate=pl.CostEstimate(flops=10_000_000_000, bytes_accessed=8 << 20, transcendentals=0),
        name="solve",
    )(sizes, glue, factors, panels)


def pack_kernel(loads_ref, glue_ref, out_ref, held, lines_of, tail, in_sems, load_sems, tail_sems):
    members, rows, nrhs = out_ref.shape
    half, lines = loads_ref.shape[0] // 2, glue_ref.shape[0] // 2
    labels = pltpu.make_async_copy(glue_ref, lines_of, in_sems.at[0])
    load = pltpu.make_async_copy(loads_ref, held, in_sems.at[1])
    labels.start()
    load.start()
    labels.wait()
    blank = jnp.zeros((rows - half - lines, nrhs), F32)
    for part in range(2):
        line = lines_of[part * lines:(part + 1) * lines].astype(F32)
        tail[part] = jnp.concatenate([line, blank], axis=0)
    copies = []
    for k in range(members):
        copies.append(pltpu.make_async_copy(tail.at[k % 2], out_ref.at[k, pl.ds(half, rows - half)], tail_sems.at[k]))
        copies[-1].start()
    load.wait()
    for k in range(members):
        rows_of = held.at[pl.ds(k % 2 * half, half)]
        copies.append(pltpu.make_async_copy(rows_of, out_ref.at[k, pl.ds(0, half)], load_sems.at[k]))
        copies[-1].start()
    for copy in copies:
        copy.wait()


def pack(loads, glue, members):
    subs = glue.shape[0]
    share, nrhs = loads.shape
    rows = share // 2 + 8 * (-(-subs // 16))
    far = pl.BlockSpec(memory_space=pltpu.HBM)
    return pl.pallas_call(
        pack_kernel,
        out_shape=jax.ShapeDtypeStruct((members, rows, nrhs), F32),
        in_specs=[far, far],
        out_specs=far,
        scratch_shapes=[
            pltpu.VMEM((share, nrhs), F32),
            pltpu.VMEM(glue.shape, jnp.int32),
            pltpu.VMEM((2, rows - share // 2, nrhs), F32),
            pltpu.SemaphoreType.DMA((2,)),
            pltpu.SemaphoreType.DMA((members,)),
            pltpu.SemaphoreType.DMA((members,)),
        ],
        compiler_params=pltpu.CompilerParams(vmem_limit_bytes=58 << 20),
        cost_estimate=pl.CostEstimate(flops=1_000_000, bytes_accessed=1 << 20, transcendentals=0),
        name="pack",
    )(loads, glue)


def routes_kernel(subs, place_ref, own_ref, twin_ref, stand_ref, label_ref, high_ref, low_ref):
    members, block, width = own_ref.shape
    share = NDUAL // members
    half, lines = share // 2, subs // 2
    slots = label_ref.shape[1]
    capacity = slots // subs
    first_core = place_ref[0] % 2 == 0
    glue = []
    for k in range(members):
        source = place_ref[0] ^ k
        pair = own_ref[source], twin_ref[source]
        for part in range(2):
            got = jnp.where(first_core, pair[part], pair[1 - part])
            row = pl.ds(pl.multiple_of(source * share + part * half, half), half)
            high_ref[row], low_ref[row] = split(got[:half])
            glue.append(got[half:half + lines])
    glue = jnp.concatenate(glue, axis=0)
    stand_ref[...] = glue.T.astype(jnp.int32)
    glue = glue.astype(jnp.int32)
    first = place_ref[0] * share
    mine = (glue >= first) & (glue < first + share)
    before = (iota((width, width), 0) < iota((width, width), 1)).astype(BF)
    ranks = mm(mine.astype(BF), before).astype(jnp.int32)
    local = jnp.where(mine, glue - first + 1, 0).astype(F32).astype(BF)
    labels = []
    for k in range(members):
        found = jnp.full((1, slots), -1.0, F32)
        for s in range(subs):
            i = k * subs + s
            rank = jnp.where(mine[i:i + 1], ranks[i:i + 1] + s * capacity, -1)
            at_slot = (iota((slots, width), 0) == rank).astype(BF)
            line = mm(local[i:i + 1], at_slot, (((1,), (1,)), ((), ())))
            found = jnp.where(line > 0.5, line + (s * share - 1), found)
        labels.append(found)
    label_ref[...] = jnp.concatenate(labels, axis=0).astype(jnp.int32)


def placed(subs, sources, label_ref, stand_ref, values):
    slots, width = values[0].shape
    share = NDUAL // label_ref.shape[0]
    total = jnp.zeros((2 * share, NDUAL), F32)
    for k, value in zip(sources, values):
        rows = (iota((subs * share, slots), 0) == label_ref[k:k + 1]).astype(BF)
        moved = mm(rows, jnp.concatenate(split(value[...]), axis=1)).astype(BF)
        for s in range(subs):
            i = k * subs + s
            part = moved[s * share:(s + 1) * share]
            columns = (iota((width, NDUAL), 1) == stand_ref[:, i:i + 1]).astype(BF)
            total = total + mm(jnp.concatenate([part[:, :width], part[:, width:]], axis=0), columns)
    return total[:share] + total[share:]


def early_kernel(subs, sources, label_ref, stand_ref, *refs):
    refs[-1][...] = placed(subs, sources, label_ref, stand_ref, refs[:-1])


def finish_kernel(subs, sources, label_ref, stand_ref, high_ref, low_ref, early_ref, *refs):
    values, (dual_ref, raw_ref, first_ref, last_ref) = refs[:-4], refs[-4:]
    dual = early_ref[...] + placed(subs, sources, label_ref, stand_ref, values)
    dual_ref[...] = dual
    raw = mm3(split(dual), (high_ref[...], low_ref[...]))
    raw_ref[...] = raw
    first_ref[...] = raw[:IFACE]
    last_ref[...] = raw[raw.shape[0] - IFACE:]


def call(kernel, outs, args, flops, name, smem=0):
    vm = pl.BlockSpec(memory_space=pltpu.VMEM)
    specs = [pl.BlockSpec(memory_space=pltpu.SMEM)] * smem + [vm] * (len(args) - smem)
    return pl.pallas_call(
        kernel,
        out_shape=outs,
        in_specs=specs,
        out_specs=jax.tree.map(lambda _: vm, outs),
        compiler_params=pltpu.CompilerParams(vmem_limit_bytes=16 << 20),
        cost_estimate=pl.CostEstimate(flops=flops, bytes_accessed=4 << 20, transcendentals=0),
        name=name,
    )(*args)


def on_device(factors, panels, sizes, glue_index, loads):
    members = lax.axis_size("member")
    subs, order, width = panels.shape
    share, nrhs = loads.shape
    capacity = 2 * width // members
    slots = subs * capacity
    count = members * subs
    shape = jax.ShapeDtypeStruct
    place = lax.axis_index("member").astype(jnp.int32).reshape(1)

    def across(value, distance):
        return lax.ppermute(value, "member", [(i, i ^ distance) for i in range(members)])

    packed = pack(loads, glue_index, members)
    own = lax.all_to_all(packed, "member", split_axis=0, concat_axis=0, tiled=True)
    values = solve(sizes, glue_index, factors, panels, members)
    own, *values = lax.optimization_barrier((own, *values))
    distances = [*range(2, members, 2), *range(3, members, 2), 1]
    arrived = {0: values[0], **{k: across(values[k], k) for k in distances}}
    last_ones = distances[-3:-1]
    first_ones = [k for k in arrived if k not in last_ones]
    twin = across(own, 1)
    stand, labels, high, low = call(
        functools.partial(routes_kernel, subs),
        (
            shape((width, count), jnp.int32),
            shape((members, slots), jnp.int32),
            shape((NDUAL, nrhs), BF),
            shape((NDUAL, nrhs), BF),
        ),
        (place, own, twin),
        2_000_000_000,
        "routes",
        smem=1,
    )
    early = call(
        functools.partial(early_kernel, subs, first_ones),
        shape((share, NDUAL), F32),
        (labels, stand, *[arrived[k] for k in first_ones]),
        2_000_000_000,
        "early",
    )
    dual_rows, raw, first, last = call(
        functools.partial(finish_kernel, subs, last_ones),
        (
            shape((share, NDUAL), F32),
            shape((share, nrhs), F32),
            shape((IFACE, nrhs), F32),
            shape((IFACE, nrhs), F32),
        ),
        (labels, stand, high, low, early, *[arrived[k] for k in last_ones]),
        3_000_000_000,
        "finish",
    )
    peers = lax.axis_size("cluster")
    up = [(i, (i + 1) % peers) for i in range(peers)]
    down = [(j, i) for i, j in up]
    before = lax.ppermute(last, "cluster", up)
    after = lax.ppermute(first, "cluster", down)
    between = jnp.zeros((share - 2 * IFACE, nrhs), F32)
    products = raw + jnp.concatenate([before, between, after], axis=0)
    return (dual_rows, products)


def solution(mesh):
    shards = ("cluster", "member")
    return jax.shard_map(
        on_device,
        mesh=mesh,
        in_specs=(P(shards, None, None), P(shards, None, None), P(shards), P(shards, None), P(shards, None)),
        out_specs=(P(shards, None), P(shards, None)),
        check_vma=False,
    )
```

```python
import functools
import jax, jax.numpy as jnp
from jax import lax
from jax.experimental import pallas as pl
from jax.experimental.pallas import tpu as pltpu
F32, BF = jnp.float32, jnp.bfloat16
from jax.sharding import PartitionSpec as P

STRIDE, BASE = 128, 16
NDUAL, IFACE = 1024, 8

def split(v):
    hi = v.astype(BF)
    return hi, (v - hi.astype(F32)).astype(BF)

def mm(a, b, dims=(((1,), (0,)), ((), ()))):
    return lax.dot_general(a, b, dims, preferred_element_type=F32)

def mm3(a, b):
    ah, al = a
    bh, bl = b
    return mm(ah, bh) + (mm(al, bh) + mm(ah, bl))

def iota(shape, dim):
    return lax.broadcasted_iota(jnp.int32, shape, dim)

def mmk(a, b):
    ah, al = a
    bh, bl = b
    return mm(jnp.concatenate([ah, al], axis=1), jnp.concatenate([bh, bh], axis=0)) + mm(ah, bl)


def turn(v, by):
    return pltpu.roll(v, by, 1)


def split32(v):
    hi = v.astype(BF).astype(F32)
    return hi, v - hi


def eliminate(packs):
    lane = iota((BASE, STRIDE), 1)
    row = iota((BASE, STRIDE), 0)
    local = lane % BASE
    parts = BASE // 8
    start = (iota((8, STRIDE), 1) // BASE) * BASE
    row8 = iota((8, STRIDE), 0)
    eye = (row == local).astype(F32)
    recips, works, pieces = [], [], []
    for packed in packs:
        diag = jnp.sum(jnp.where(row == local, packed, 0.0), axis=0, keepdims=True)
        recip = 1.0 / diag
        scaled = jnp.where(row > local, packed * recip, 0.0)
        recips.append(jnp.broadcast_to(recip, (8, STRIDE)))
        works.append([eye[g * 8:(g + 1) * 8] for g in range(parts)])
        pieces.append([scaled[g * 8:(g + 1) * 8] for g in range(parts)])
    for j in range(BASE - 1):
        for work, piece in zip(works, pieces):
            pivot = work[j // 8][j % 8:j % 8 + 1]
            for g in range((j + 1) // 8, parts):
                column = jnp.take_along_axis(piece[g], start + j, axis=1, mode="promise_in_bounds")
                work[g] = work[g] - column * pivot
    for work, recip in zip(works, recips):
        for g in range(parts):
            work[g] = work[g] * jnp.take_along_axis(recip, start + (row8 + g * 8), axis=1, mode="promise_in_bounds")
    return [jnp.concatenate(work, axis=0) for work in works]


def slabs_of(v, size):
    return [v[r:r + size] for r in range(0, v.shape[0], size)]


def invert_blocks(blocks):
    lane = iota((BASE, STRIDE), 1)
    packs = []
    for block in blocks:
        packed = block[:BASE]
        for q, slab in enumerate(slabs_of(block, BASE)):
            packed = jnp.where(lane // BASE == q, slab, packed) if q else packed
        packs.append(packed)
    inners = eliminate(packs)
    states = [[jnp.where(lane // BASE == q, inner, 0.0) for q in range(STRIDE // BASE)] for inner in inners]
    size = BASE
    while size < STRIDE:
        half = iota((STRIDE // 2, STRIDE), 1) // size
        even = half % 2 == 0
        pair = (half // 2 == iota((STRIDE // 2, STRIDE), 0) // size) & even
        products = []
        for block, slabs in zip(blocks, states):
            ch, cl = split32(jnp.where(pair, jnp.concatenate(slabs_of(block, size)[1::2], axis=0), 0.0))
            a = jnp.concatenate([ch + turn(cl, size), ch], axis=1).astype(BF)
            tops = [split(v) for v in slabs[0::2]]
            w = [v[0] for v in tops for _ in range(2)] + [v[1] for v in tops for _ in range(2)]
            products.append(mm(a, jnp.concatenate(w, axis=0)))
        belows = []
        for product, slabs in zip(products, states):
            xh, xl = split32(jnp.concatenate(slabs[1::2], axis=0))
            a = jnp.concatenate([xh + turn(xl, STRIDE - size), xh], axis=1).astype(BF)
            th, tl = split(product)
            w = [v for v in slabs_of(th, size) for _ in range(2)] + [v for v in slabs_of(tl, size) for _ in range(2)]
            belows.append(slabs_of(mm(a, jnp.concatenate(w, axis=0)), size))
        states = [
            [jnp.concatenate([top, low - add], axis=0) for top, low, add in zip(slabs[0::2], slabs[1::2], below)]
            for slabs, below in zip(states, belows)
        ]
        size *= 2
    return [slabs[0] for slabs in states]


BATCH = 16


def solve_kernel(members, packed_ref, far_ref, p_ref, *refs):
    out_refs = refs[:members]
    rest, f_ref, tails, square_sems, corner_sems, strip_sems, panel_sem, small_sem = refs[members:]
    extra = tails.shape[1]
    ends = packed_ref.at[pl.ds(0, 2), pl.ds(packed_ref.shape[1] - extra, extra)]
    small_copy = pltpu.make_async_copy(ends, tails, small_sem)
    small_copy.start()
    subs, order, width = p_ref.shape
    wide = 2 * STRIDE
    square_copies, corner_copies, strip_copies = {}, {}, {}

    def fetch(s, rows, columns, sem):
        part = (s, rows, columns)
        copy = pltpu.make_async_copy(far_ref.at[part], f_ref.at[part], sem)
        copy.start()
        return copy

    for step, a in enumerate(range(0, order, STRIDE)):
        for s in range(subs):
            square_copies[s, a] = fetch(s, pl.ds(a, STRIDE), pl.ds(a, STRIDE), square_sems.at[s, step])
    for step, a in enumerate(range(0, order, wide)):
        for s in range(subs):
            corner_copies[s, a] = fetch(s, pl.ds(a + STRIDE, STRIDE), pl.ds(a, STRIDE), corner_sems.at[s, step])
    panel_copy = pltpu.make_async_copy(p_ref, rest, panel_sem)
    panel_copy.start()
    for step, a in enumerate(range(0, order - wide, wide)):
        for s in range(subs):
            strip_copies[s, a] = fetch(s, pl.ds(a + wide, order - a - wide), pl.ds(a, wide), strip_sems.at[s, step])
    small_copy.wait()
    lines = subs // 2
    lives = [tails[0, lines + s:lines + s + 1].astype(jnp.int32) for s in range(subs)]
    row = iota((STRIDE, STRIDE), 0)
    col = iota((STRIDE, STRIDE), 1)
    prow = iota((wide, width), 0)
    dims = (((0,), (0,)), ((), ()))
    squares = [jnp.zeros((width, width), F32)] * subs
    crosses = [jnp.zeros((width, width), F32)] * subs
    places = [(s, a) for a in range(0, order, STRIDE) for s in range(subs)]
    small = {}
    for first in range(0, len(places), BATCH):
        batch = places[first:first + BATCH]
        blocks = []
        for s, a in batch:
            square_copies[s, a].wait()
            d = f_ref[s, a:a + STRIDE, a:a + STRIDE]
            keep = (row + a < lives[s][:, :STRIDE]) & (col <= row)
            blocks.append(jnp.where(keep, d, (row == col).astype(F32)))
        for place, inverse in zip(batch, invert_blocks(blocks)):
            small[place] = split(inverse)
    heads = [(s, a) for a in range(0, order, wide) for s in range(subs)]
    corners = []
    for s, a in heads:
        b = a + STRIDE
        corner_copies[s, a].wait()
        corner = jnp.where(row + b < lives[s][:, :STRIDE], f_ref[s, b:b + STRIDE, a:b], 0.0)
        corners.append(split(mmk(split(corner), small[s, a])))
    inverses = {}
    for (s, a), corner in zip(heads, corners):
        above, below = small[s, a], small[s, a + STRIDE]
        turned = split(-mmk(below, corner))
        blank = jnp.zeros((STRIDE, STRIDE), BF)
        inverses[s, a] = [
            jnp.concatenate([jnp.concatenate([u, blank], axis=1), jnp.concatenate([t, l], axis=1)], axis=0)
            for u, t, l in zip(above, turned, below)
        ]

    capacity = 2 * width // members
    glue = jnp.concatenate([tails[0, :lines], tails[1, :lines]], axis=0).astype(jnp.int32)
    place = lax.axis_index("member")
    before = (iota((width, width), 0) < iota((width, width), 1)).astype(BF)
    dispatches = []
    for s in range(subs):
        owner = glue[s:s + 1] // (NDUAL // members)
        owners = (iota((members, width), 0) == owner)
        ranks = mm(owners.astype(BF), before)
        rank = jnp.sum(jnp.where(owners, ranks, 0.0), axis=0, keepdims=True).astype(jnp.int32)
        target = (owner ^ place) * capacity + rank
        dispatches.append((iota((members * capacity, width), 0) == target).astype(BF))
    panel_copy.wait()
    for a in range(0, order, wide):
        solved = []
        for s in range(subs):
            now = jnp.where(prow + a < lives[s], rest[s, a:a + wide], 0.0)
            solved.append(split(mm3(inverses[s, a], split(now))))
        if a + wide < order:
            for s in range(subs):
                strip_copies[s, a].wait()
        for c in range(a + wide, order, wide):
            for s in range(subs):
                rest[s, c:c + wide] = rest[s, c:c + wide] - mm3(split(f_ref[s, c:c + wide, a:a + wide]), solved[s])
        for s in range(subs):
            hi, lo = solved[s]
            squares[s] = squares[s] + mm(hi, hi, dims)
            crosses[s] = crosses[s] + mm(hi, lo, dims)
    duals = [split(squares[s] + (crosses[s] + crosses[s].T)) for s in range(subs)]
    for s in range(subs):
        values = mm(dispatches[s], duals[s][0]) + mm(dispatches[s], duals[s][1])
        for k in range(members):
            out_refs[k][s * capacity:(s + 1) * capacity] = values[k * capacity:(k + 1) * capacity]


def solve(packed, factors, panels, members):
    subs, order, width = panels.shape
    capacity = 2 * width // members
    vm = pl.BlockSpec(memory_space=pltpu.VMEM)
    far = pl.BlockSpec(memory_space=pltpu.HBM)
    return pl.pallas_call(
        functools.partial(solve_kernel, members),
        out_shape=[jax.ShapeDtypeStruct((subs * capacity, width), F32)] * members,
        in_specs=[far] * 3,
        out_specs=[vm] * members,
        scratch_shapes=[
            pltpu.VMEM((subs, order, width), F32),
            pltpu.VMEM((subs, order, order), F32),
            pltpu.VMEM((2, tail_rows(subs), width), F32),
            pltpu.SemaphoreType.DMA((subs, order // STRIDE)),
            pltpu.SemaphoreType.DMA((subs, order // (2 * STRIDE))),
            pltpu.SemaphoreType.DMA((subs, order // (2 * STRIDE))),
            pltpu.SemaphoreType.DMA,
            pltpu.SemaphoreType.DMA,
        ],
        compiler_params=pltpu.CompilerParams(vmem_limit_bytes=52 << 20),
        cost_estimate=pl.CostEstimate(flops=10_000_000_000, bytes_accessed=8 << 20, transcendentals=0),
        name="solve",
    )(packed, factors, panels)


def tail_rows(subs):
    return 8 * (-(-(subs // 2 + subs) // 8))


def pack_kernel(loads_ref, glue_ref, sizes_ref, out_ref, held, lines_of, sizes_of, tail, in_sems, load_sems, tail_sems):
    members, rows, nrhs = out_ref.shape
    subs = glue_ref.shape[0]
    half, lines = loads_ref.shape[0] // 2, subs // 2
    labels = pltpu.make_async_copy(glue_ref, lines_of, in_sems.at[0])
    load = pltpu.make_async_copy(loads_ref, held, in_sems.at[1])
    sizes = pltpu.make_async_copy(sizes_ref, sizes_of, in_sems.at[2])
    labels.start()
    sizes.start()
    load.start()
    labels.wait()
    sizes.wait()
    lives = [jnp.full((1, nrhs), sizes_of[s], jnp.int32).astype(F32) for s in range(subs)]
    blank = [jnp.zeros((rows - half - lines - subs, nrhs), F32)]
    for part in range(2):
        line = lines_of[part * lines:(part + 1) * lines].astype(F32)
        tail[part] = jnp.concatenate([line, *lives, *blank], axis=0)
    copies = []
    for k in range(members):
        copies.append(pltpu.make_async_copy(tail.at[k % 2], out_ref.at[k, pl.ds(half, rows - half)], tail_sems.at[k]))
        copies[-1].start()
    load.wait()
    for k in range(members):
        rows_of = held.at[pl.ds(k % 2 * half, half)]
        copies.append(pltpu.make_async_copy(rows_of, out_ref.at[k, pl.ds(0, half)], load_sems.at[k]))
        copies[-1].start()
    for copy in copies:
        copy.wait()


def pack(loads, glue, sizes, members):
    subs = glue.shape[0]
    share, nrhs = loads.shape
    rows = share // 2 + tail_rows(subs)
    far = pl.BlockSpec(memory_space=pltpu.HBM)
    return pl.pallas_call(
        pack_kernel,
        out_shape=jax.ShapeDtypeStruct((members, rows, nrhs), F32),
        in_specs=[far] * 3,
        out_specs=far,
        scratch_shapes=[
            pltpu.VMEM((share, nrhs), F32),
            pltpu.VMEM(glue.shape, jnp.int32),
            pltpu.SMEM(sizes.shape, jnp.int32),
            pltpu.VMEM((2, rows - share // 2, nrhs), F32),
            pltpu.SemaphoreType.DMA((3,)),
            pltpu.SemaphoreType.DMA((members,)),
            pltpu.SemaphoreType.DMA((members,)),
        ],
        compiler_params=pltpu.CompilerParams(vmem_limit_bytes=58 << 20),
        cost_estimate=pl.CostEstimate(flops=1_000_000, bytes_accessed=1 << 20, transcendentals=0),
        name="pack",
    )(loads, glue, sizes)


def routes_kernel(subs, place_ref, own_ref, twin_ref, stand_ref, label_ref, high_ref, low_ref):
    members, block, width = own_ref.shape
    share = NDUAL // members
    half, lines = share // 2, subs // 2
    slots = label_ref.shape[1]
    capacity = slots // subs
    first_core = place_ref[0] % 2 == 0
    glue = []
    for k in range(members):
        source = place_ref[0] ^ k
        pair = own_ref[source], twin_ref[source]
        for part in range(2):
            got = jnp.where(first_core, pair[part], pair[1 - part])
            row = pl.ds(pl.multiple_of(source * share + part * half, half), half)
            high_ref[row], low_ref[row] = split(got[:half])
            glue.append(got[half:half + lines])
    glue = jnp.concatenate(glue, axis=0)
    stand_ref[...] = glue.T.astype(jnp.int32)
    glue = glue.astype(jnp.int32)
    first = place_ref[0] * share
    mine = (glue >= first) & (glue < first + share)
    before = (iota((width, width), 0) < iota((width, width), 1)).astype(BF)
    ranks = mm(mine.astype(BF), before).astype(jnp.int32)
    local = jnp.where(mine, glue - first + 1, 0).astype(F32).astype(BF)
    labels = []
    for k in range(members):
        found = jnp.full((1, slots), -1.0, F32)
        for s in range(subs):
            i = k * subs + s
            rank = jnp.where(mine[i:i + 1], ranks[i:i + 1] + s * capacity, -1)
            at_slot = (iota((slots, width), 0) == rank).astype(BF)
            line = mm(local[i:i + 1], at_slot, (((1,), (1,)), ((), ())))
            found = jnp.where(line > 0.5, line + (s * share - 1), found)
        labels.append(found)
    label_ref[...] = jnp.concatenate(labels, axis=0).astype(jnp.int32)


def placed(subs, sources, label_ref, stand_ref, values):
    slots, width = values[0].shape
    share = NDUAL // label_ref.shape[0]
    total = jnp.zeros((2 * share, NDUAL), F32)
    for k, value in zip(sources, values):
        rows = (iota((subs * share, slots), 0) == label_ref[k:k + 1]).astype(BF)
        moved = mm(rows, jnp.concatenate(split(value[...]), axis=1)).astype(BF)
        for s in range(subs):
            i = k * subs + s
            part = moved[s * share:(s + 1) * share]
            columns = (iota((width, NDUAL), 1) == stand_ref[:, i:i + 1]).astype(BF)
            total = total + mm(jnp.concatenate([part[:, :width], part[:, width:]], axis=0), columns)
    return total[:share] + total[share:]


def early_kernel(subs, sources, label_ref, stand_ref, *refs):
    refs[-1][...] = placed(subs, sources, label_ref, stand_ref, refs[:-1])


def finish_kernel(subs, sources, label_ref, stand_ref, high_ref, low_ref, early_ref, *refs):
    values, (dual_ref, raw_ref, first_ref, last_ref) = refs[:-4], refs[-4:]
    dual = early_ref[...] + placed(subs, sources, label_ref, stand_ref, values)
    dual_ref[...] = dual
    raw = mm3(split(dual), (high_ref[...], low_ref[...]))
    raw_ref[...] = raw
    first_ref[...] = raw[:IFACE]
    last_ref[...] = raw[raw.shape[0] - IFACE:]


def call(kernel, outs, args, flops, name, smem=0):
    vm = pl.BlockSpec(memory_space=pltpu.VMEM)
    specs = [pl.BlockSpec(memory_space=pltpu.SMEM)] * smem + [vm] * (len(args) - smem)
    return pl.pallas_call(
        kernel,
        out_shape=outs,
        in_specs=specs,
        out_specs=jax.tree.map(lambda _: vm, outs),
        compiler_params=pltpu.CompilerParams(vmem_limit_bytes=16 << 20),
        cost_estimate=pl.CostEstimate(flops=flops, bytes_accessed=4 << 20, transcendentals=0),
        name=name,
    )(*args)


def on_device(factors, panels, sizes, glue_index, loads):
    members = lax.axis_size("member")
    subs, order, width = panels.shape
    share, nrhs = loads.shape
    capacity = 2 * width // members
    slots = subs * capacity
    count = members * subs
    shape = jax.ShapeDtypeStruct
    place = lax.axis_index("member").astype(jnp.int32).reshape(1)

    def across(value, distance):
        return lax.ppermute(value, "member", [(i, i ^ distance) for i in range(members)])

    packed = pack(loads, glue_index, sizes, members)
    own = lax.all_to_all(packed, "member", split_axis=0, concat_axis=0, tiled=True)
    values = solve(packed, factors, panels, members)
    own, *values = lax.optimization_barrier((own, *values))
    distances = [*range(2, members, 2), *range(3, members, 2), 1]
    arrived = {0: values[0], **{k: across(values[k], k) for k in distances}}
    last_ones = distances[-3:-1]
    first_ones = [k for k in arrived if k not in last_ones]
    twin = across(own, 1)
    stand, labels, high, low = call(
        functools.partial(routes_kernel, subs),
        (
            shape((width, count), jnp.int32),
            shape((members, slots), jnp.int32),
            shape((NDUAL, nrhs), BF),
            shape((NDUAL, nrhs), BF),
        ),
        (place, own, twin),
        2_000_000_000,
        "routes",
        smem=1,
    )
    early = call(
        functools.partial(early_kernel, subs, first_ones),
        shape((share, NDUAL), F32),
        (labels, stand, *[arrived[k] for k in first_ones]),
        2_000_000_000,
        "early",
    )
    dual_rows, raw, first, last = call(
        functools.partial(finish_kernel, subs, last_ones),
        (
            shape((share, NDUAL), F32),
            shape((share, nrhs), F32),
            shape((IFACE, nrhs), F32),
            shape((IFACE, nrhs), F32),
        ),
        (labels, stand, high, low, early, *[arrived[k] for k in last_ones]),
        3_000_000_000,
        "finish",
    )
    peers = lax.axis_size("cluster")
    up = [(i, (i + 1) % peers) for i in range(peers)]
    down = [(j, i) for i, j in up]
    before = lax.ppermute(last, "cluster", up)
    after = lax.ppermute(first, "cluster", down)
    between = jnp.zeros((share - 2 * IFACE, nrhs), F32)
    products = raw + jnp.concatenate([before, between, after], axis=0)
    return (dual_rows, products)


def solution(mesh):
    shards = ("cluster", "member")
    return jax.shard_map(
        on_device,
        mesh=mesh,
        in_specs=(P(shards, None, None), P(shards, None, None), P(shards), P(shards, None), P(shards, None)),
        out_specs=(P(shards, None), P(shards, None)),
        check_vma=False,
    )
```

```python
import functools
import jax, jax.numpy as jnp
from jax import lax
from jax.experimental import pallas as pl
from jax.experimental.pallas import tpu as pltpu
F32, BF = jnp.float32, jnp.bfloat16
from jax.sharding import PartitionSpec as P

STRIDE, BASE = 128, 16
NDUAL, IFACE = 1024, 8

def split(v):
    hi = v.astype(BF)
    return hi, (v - hi.astype(F32)).astype(BF)

def mm(a, b, dims=(((1,), (0,)), ((), ()))):
    return lax.dot_general(a, b, dims, preferred_element_type=F32)

def mm3(a, b):
    ah, al = a
    bh, bl = b
    return mm(ah, bh) + (mm(al, bh) + mm(ah, bl))

def iota(shape, dim):
    return lax.broadcasted_iota(jnp.int32, shape, dim)

def mmk(a, b):
    ah, al = a
    bh, bl = b
    return mm(jnp.concatenate([ah, al], axis=1), jnp.concatenate([bh, bh], axis=0)) + mm(ah, bl)


def turn(v, by):
    return pltpu.roll(v, by, 1)


def split32(v):
    hi = v.astype(BF).astype(F32)
    return hi, v - hi


def eliminate(packs):
    lane = iota((BASE, STRIDE), 1)
    row = iota((BASE, STRIDE), 0)
    local = lane % BASE
    parts = BASE // 8
    start = (iota((8, STRIDE), 1) // BASE) * BASE
    row8 = iota((8, STRIDE), 0)
    eye = (row == local).astype(F32)
    recips, works, pieces = [], [], []
    for packed in packs:
        diag = jnp.sum(jnp.where(row == local, packed, 0.0), axis=0, keepdims=True)
        recip = 1.0 / diag
        scaled = jnp.where(row > local, packed * recip, 0.0)
        recips.append(jnp.broadcast_to(recip, (8, STRIDE)))
        works.append([eye[g * 8:(g + 1) * 8] for g in range(parts)])
        pieces.append([scaled[g * 8:(g + 1) * 8] for g in range(parts)])
    for j in range(BASE - 1):
        for work, piece in zip(works, pieces):
            pivot = work[j // 8][j % 8:j % 8 + 1]
            for g in range((j + 1) // 8, parts):
                column = jnp.take_along_axis(piece[g], start + j, axis=1, mode="promise_in_bounds")
                work[g] = work[g] - column * pivot
    for work, recip in zip(works, recips):
        for g in range(parts):
            work[g] = work[g] * jnp.take_along_axis(recip, start + (row8 + g * 8), axis=1, mode="promise_in_bounds")
    return [jnp.concatenate(work, axis=0) for work in works]


def slabs_of(v, size):
    return [v[r:r + size] for r in range(0, v.shape[0], size)]


def invert_blocks(blocks):
    lane = iota((BASE, STRIDE), 1)
    packs = []
    for block in blocks:
        packed = block[:BASE]
        for q, slab in enumerate(slabs_of(block, BASE)):
            packed = jnp.where(lane // BASE == q, slab, packed) if q else packed
        packs.append(packed)
    inners = eliminate(packs)
    states = [[jnp.where(lane // BASE == q, inner, 0.0) for q in range(STRIDE // BASE)] for inner in inners]
    size = BASE
    while size < STRIDE:
        half = iota((STRIDE // 2, STRIDE), 1) // size
        even = half % 2 == 0
        pair = (half // 2 == iota((STRIDE // 2, STRIDE), 0) // size) & even
        products = []
        for block, slabs in zip(blocks, states):
            ch, cl = split32(jnp.where(pair, jnp.concatenate(slabs_of(block, size)[1::2], axis=0), 0.0))
            a = jnp.concatenate([ch + turn(cl, size), ch], axis=1).astype(BF)
            tops = [split(v) for v in slabs[0::2]]
            w = [v[0] for v in tops for _ in range(2)] + [v[1] for v in tops for _ in range(2)]
            products.append(mm(a, jnp.concatenate(w, axis=0)))
        belows = []
        for product, slabs in zip(products, states):
            xh, xl = split32(jnp.concatenate(slabs[1::2], axis=0))
            a = jnp.concatenate([xh + turn(xl, STRIDE - size), xh], axis=1).astype(BF)
            th, tl = split(product)
            w = [v for v in slabs_of(th, size) for _ in range(2)] + [v for v in slabs_of(tl, size) for _ in range(2)]
            belows.append(slabs_of(mm(a, jnp.concatenate(w, axis=0)), size))
        states = [
            [jnp.concatenate([top, low - add], axis=0) for top, low, add in zip(slabs[0::2], slabs[1::2], below)]
            for slabs, below in zip(states, belows)
        ]
        size *= 2
    return [slabs[0] for slabs in states]


BATCH = 16


def solve_kernel(members, packed_ref, far_ref, p_ref, *refs):
    out_refs = refs[:members]
    rest, f_ref, tails, square_sems, corner_sems, strip_sems, panel_sem, small_sem = refs[members:]
    extra = tails.shape[1]
    ends = packed_ref.at[pl.ds(0, 2), pl.ds(packed_ref.shape[1] - extra, extra)]
    small_copy = pltpu.make_async_copy(ends, tails, small_sem)
    small_copy.start()
    subs, order, width = p_ref.shape
    wide = 2 * STRIDE
    square_copies, corner_copies, strip_copies = {}, {}, {}

    def fetch(s, rows, columns, sem):
        part = (s, rows, columns)
        copy = pltpu.make_async_copy(far_ref.at[part], f_ref.at[part], sem)
        copy.start()
        return copy

    for step, a in enumerate(range(0, order, STRIDE)):
        for s in range(subs):
            square_copies[s, a] = fetch(s, pl.ds(a, STRIDE), pl.ds(a, STRIDE), square_sems.at[s, step])
    for step, a in enumerate(range(0, order, wide)):
        for s in range(subs):
            corner_copies[s, a] = fetch(s, pl.ds(a + STRIDE, STRIDE), pl.ds(a, STRIDE), corner_sems.at[s, step])
    panel_copy = pltpu.make_async_copy(p_ref, rest, panel_sem)
    panel_copy.start()
    for step, a in enumerate(range(0, order - wide, wide)):
        for s in range(subs):
            strip_copies[s, a] = fetch(s, pl.ds(a + wide, order - a - wide), pl.ds(a, wide), strip_sems.at[s, step])
    small_copy.wait()
    lines = subs // 2
    lives = [tails[0, lines + s:lines + s + 1].astype(jnp.int32) for s in range(subs)]
    row = iota((STRIDE, STRIDE), 0)
    col = iota((STRIDE, STRIDE), 1)
    prow = iota((wide, width), 0)
    dims = (((0,), (0,)), ((), ()))
    squares = [jnp.zeros((width, width), F32)] * subs
    crosses = [jnp.zeros((width, width), F32)] * subs
    places = [(s, a) for a in range(0, order, STRIDE) for s in range(subs)]
    small = {}
    for first in range(0, len(places), BATCH):
        batch = places[first:first + BATCH]
        blocks = []
        for s, a in batch:
            square_copies[s, a].wait()
            d = f_ref[s, a:a + STRIDE, a:a + STRIDE]
            keep = (row + a < lives[s][:, :STRIDE]) & (col <= row)
            blocks.append(jnp.where(keep, d, (row == col).astype(F32)))
        for place, inverse in zip(batch, invert_blocks(blocks)):
            small[place] = split(inverse)
    heads = [(s, a) for a in range(0, order, wide) for s in range(subs)]
    corners = []
    for s, a in heads:
        b = a + STRIDE
        corner_copies[s, a].wait()
        corner = jnp.where(row + b < lives[s][:, :STRIDE], f_ref[s, b:b + STRIDE, a:b], 0.0)
        corners.append(split(mmk(split(corner), small[s, a])))
    inverses = {}
    for (s, a), corner in zip(heads, corners):
        above, below = small[s, a], small[s, a + STRIDE]
        turned = split(-mmk(below, corner))
        blank = jnp.zeros((STRIDE, STRIDE), BF)
        inverses[s, a] = [
            jnp.concatenate([jnp.concatenate([u, blank], axis=1), jnp.concatenate([t, l], axis=1)], axis=0)
            for u, t, l in zip(above, turned, below)
        ]

    capacity = 2 * width // members
    glue = jnp.concatenate([tails[0, :lines], tails[1, :lines]], axis=0).astype(jnp.int32)
    place = lax.axis_index("member")
    before = (iota((width, width), 0) < iota((width, width), 1)).astype(BF)
    dispatches = []
    for s in range(subs):
        owner = glue[s:s + 1] // (NDUAL // members)
        owners = (iota((members, width), 0) == owner)
        ranks = mm(owners.astype(BF), before)
        rank = jnp.sum(jnp.where(owners, ranks, 0.0), axis=0, keepdims=True).astype(jnp.int32)
        target = (owner ^ place) * capacity + rank
        dispatches.append((iota((members * capacity, width), 0) == target).astype(BF))
    panel_copy.wait()
    for a in range(0, order, wide):
        solved = []
        for s in range(subs):
            now = jnp.where(prow + a < lives[s], rest[s, a:a + wide], 0.0)
            solved.append(split(mm3(inverses[s, a], split(now))))
        if a + wide < order:
            for s in range(subs):
                strip_copies[s, a].wait()
        for c in range(a + wide, order, wide):
            for s in range(subs):
                rest[s, c:c + wide] = rest[s, c:c + wide] - mm3(split(f_ref[s, c:c + wide, a:a + wide]), solved[s])
        for s in range(subs):
            hi, lo = solved[s]
            squares[s] = squares[s] + mm(hi, hi, dims)
            crosses[s] = crosses[s] + mm(hi, lo, dims)
    duals = [split(squares[s] + (crosses[s] + crosses[s].T)) for s in range(subs)]
    for s in range(subs):
        values = mm(dispatches[s], duals[s][0]) + mm(dispatches[s], duals[s][1])
        for k in range(members):
            out_refs[k][s * capacity:(s + 1) * capacity] = values[k * capacity:(k + 1) * capacity]


def solve(packed, factors, panels, members):
    subs, order, width = panels.shape
    capacity = 2 * width // members
    vm = pl.BlockSpec(memory_space=pltpu.VMEM)
    far = pl.BlockSpec(memory_space=pltpu.HBM)
    return pl.pallas_call(
        functools.partial(solve_kernel, members),
        out_shape=[jax.ShapeDtypeStruct((subs * capacity, width), F32)] * members,
        in_specs=[far] * 3,
        out_specs=[vm] * members,
        scratch_shapes=[
            pltpu.VMEM((subs, order, width), F32),
            pltpu.VMEM((subs, order, order), F32),
            pltpu.VMEM((2, tail_rows(subs), width), F32),
            pltpu.SemaphoreType.DMA((subs, order // STRIDE)),
            pltpu.SemaphoreType.DMA((subs, order // (2 * STRIDE))),
            pltpu.SemaphoreType.DMA((subs, order // (2 * STRIDE))),
            pltpu.SemaphoreType.DMA,
            pltpu.SemaphoreType.DMA,
        ],
        compiler_params=pltpu.CompilerParams(vmem_limit_bytes=53760 << 10),
        cost_estimate=pl.CostEstimate(flops=10_000_000_000, bytes_accessed=8 << 20, transcendentals=0),
        name="solve",
    )(packed, factors, panels)


def tail_rows(subs):
    return 8 * (-(-(subs // 2 + subs) // 8))


def pack_kernel(loads_ref, glue_ref, sizes_ref, out_ref, held, lines_of, sizes_of, tail, in_sems, load_sems, tail_sems):
    members, rows, nrhs = out_ref.shape
    subs = glue_ref.shape[0]
    half, lines = loads_ref.shape[0] // 2, subs // 2
    labels = pltpu.make_async_copy(glue_ref, lines_of, in_sems.at[0])
    load = pltpu.make_async_copy(loads_ref, held, in_sems.at[1])
    sizes = pltpu.make_async_copy(sizes_ref, sizes_of, in_sems.at[2])
    labels.start()
    sizes.start()
    load.start()
    labels.wait()
    sizes.wait()
    lives = [jnp.full((1, nrhs), sizes_of[s], jnp.int32).astype(F32) for s in range(subs)]
    blank = [jnp.zeros((rows - half - lines - subs, nrhs), F32)]
    for part in range(2):
        line = lines_of[part * lines:(part + 1) * lines].astype(F32)
        tail[part] = jnp.concatenate([line, *lives, *blank], axis=0)
    copies = []
    for k in range(members):
        copies.append(pltpu.make_async_copy(tail.at[k % 2], out_ref.at[k, pl.ds(half, rows - half)], tail_sems.at[k]))
        copies[-1].start()
    load.wait()
    for k in range(members):
        rows_of = held.at[pl.ds(k % 2 * half, half)]
        copies.append(pltpu.make_async_copy(rows_of, out_ref.at[k, pl.ds(0, half)], load_sems.at[k]))
        copies[-1].start()
    for copy in copies:
        copy.wait()


def pack(loads, glue, sizes, members):
    subs = glue.shape[0]
    share, nrhs = loads.shape
    rows = share // 2 + tail_rows(subs)
    far = pl.BlockSpec(memory_space=pltpu.HBM)
    return pl.pallas_call(
        pack_kernel,
        out_shape=jax.ShapeDtypeStruct((members, rows, nrhs), F32),
        in_specs=[far] * 3,
        out_specs=far,
        scratch_shapes=[
            pltpu.VMEM((share, nrhs), F32),
            pltpu.VMEM(glue.shape, jnp.int32),
            pltpu.SMEM(sizes.shape, jnp.int32),
            pltpu.VMEM((2, rows - share // 2, nrhs), F32),
            pltpu.SemaphoreType.DMA((3,)),
            pltpu.SemaphoreType.DMA((members,)),
            pltpu.SemaphoreType.DMA((members,)),
        ],
        compiler_params=pltpu.CompilerParams(vmem_limit_bytes=58 << 20),
        cost_estimate=pl.CostEstimate(flops=1_000_000, bytes_accessed=1 << 20, transcendentals=0),
        name="pack",
    )(loads, glue, sizes)


def routes_kernel(subs, place_ref, own_ref, twin_ref, stand_ref, label_ref, high_ref, low_ref):
    members, block, width = own_ref.shape
    share = NDUAL // members
    half, lines = share // 2, subs // 2
    slots = label_ref.shape[1]
    capacity = slots // subs
    first_core = place_ref[0] % 2 == 0
    glue = []
    for k in range(members):
        source = place_ref[0] ^ k
        pair = own_ref[source], twin_ref[source]
        for part in range(2):
            got = jnp.where(first_core, pair[part], pair[1 - part])
            row = pl.ds(pl.multiple_of(source * share + part * half, half), half)
            high_ref[row], low_ref[row] = split(got[:half])
            glue.append(got[half:half + lines])
    glue = jnp.concatenate(glue, axis=0)
    stand_ref[...] = glue.T.astype(jnp.int32)
    glue = glue.astype(jnp.int32)
    first = place_ref[0] * share
    mine = (glue >= first) & (glue < first + share)
    before = (iota((width, width), 0) < iota((width, width), 1)).astype(BF)
    ranks = mm(mine.astype(BF), before).astype(jnp.int32)
    local = jnp.where(mine, glue - first + 1, 0).astype(F32).astype(BF)
    labels = []
    for k in range(members):
        found = jnp.full((1, slots), -1.0, F32)
        for s in range(subs):
            i = k * subs + s
            rank = jnp.where(mine[i:i + 1], ranks[i:i + 1] + s * capacity, -1)
            at_slot = (iota((slots, width), 0) == rank).astype(BF)
            line = mm(local[i:i + 1], at_slot, (((1,), (1,)), ((), ())))
            found = jnp.where(line > 0.5, line + (s * share - 1), found)
        labels.append(found)
    label_ref[...] = jnp.concatenate(labels, axis=0).astype(jnp.int32)


def placed(subs, sources, label_ref, stand_ref, values):
    slots, width = values[0].shape
    share = NDUAL // label_ref.shape[0]
    total = jnp.zeros((2 * share, NDUAL), F32)
    for k, value in zip(sources, values):
        rows = (iota((subs * share, slots), 0) == label_ref[k:k + 1]).astype(BF)
        moved = mm(rows, jnp.concatenate(split(value[...]), axis=1)).astype(BF)
        for s in range(subs):
            i = k * subs + s
            part = moved[s * share:(s + 1) * share]
            columns = (iota((width, NDUAL), 1) == stand_ref[:, i:i + 1]).astype(BF)
            total = total + mm(jnp.concatenate([part[:, :width], part[:, width:]], axis=0), columns)
    return total[:share] + total[share:]


def early_kernel(subs, sources, label_ref, stand_ref, *refs):
    refs[-1][...] = placed(subs, sources, label_ref, stand_ref, refs[:-1])


def finish_kernel(subs, sources, label_ref, stand_ref, high_ref, low_ref, early_ref, *refs):
    values, (dual_ref, raw_ref, first_ref, last_ref) = refs[:-4], refs[-4:]
    dual = early_ref[...] + placed(subs, sources, label_ref, stand_ref, values)
    dual_ref[...] = dual
    raw = mm3(split(dual), (high_ref[...], low_ref[...]))
    raw_ref[...] = raw
    first_ref[...] = raw[:IFACE]
    last_ref[...] = raw[raw.shape[0] - IFACE:]


def call(kernel, outs, args, flops, name, smem=0):
    vm = pl.BlockSpec(memory_space=pltpu.VMEM)
    specs = [pl.BlockSpec(memory_space=pltpu.SMEM)] * smem + [vm] * (len(args) - smem)
    return pl.pallas_call(
        kernel,
        out_shape=outs,
        in_specs=specs,
        out_specs=jax.tree.map(lambda _: vm, outs),
        compiler_params=pltpu.CompilerParams(vmem_limit_bytes=16 << 20),
        cost_estimate=pl.CostEstimate(flops=flops, bytes_accessed=4 << 20, transcendentals=0),
        name=name,
    )(*args)


def on_device(factors, panels, sizes, glue_index, loads):
    members = lax.axis_size("member")
    subs, order, width = panels.shape
    share, nrhs = loads.shape
    capacity = 2 * width // members
    slots = subs * capacity
    count = members * subs
    shape = jax.ShapeDtypeStruct
    place = lax.axis_index("member").astype(jnp.int32).reshape(1)

    def across(value, distance):
        return lax.ppermute(value, "member", [(i, i ^ distance) for i in range(members)])

    packed = pack(loads, glue_index, sizes, members)
    own = lax.all_to_all(packed, "member", split_axis=0, concat_axis=0, tiled=True)
    values = solve(packed, factors, panels, members)
    own, *values = lax.optimization_barrier((own, *values))
    distances = [*range(2, members, 2), *range(3, members, 2), 1]
    arrived = {0: values[0], **{k: across(values[k], k) for k in distances}}
    last_ones = distances[-3:-1]
    first_ones = [k for k in arrived if k not in last_ones]
    twin = across(own, 1)
    stand, labels, high, low = call(
        functools.partial(routes_kernel, subs),
        (
            shape((width, count), jnp.int32),
            shape((members, slots), jnp.int32),
            shape((NDUAL, nrhs), BF),
            shape((NDUAL, nrhs), BF),
        ),
        (place, own, twin),
        2_000_000_000,
        "routes",
        smem=1,
    )
    early = call(
        functools.partial(early_kernel, subs, first_ones),
        shape((share, NDUAL), F32),
        (labels, stand, *[arrived[k] for k in first_ones]),
        2_000_000_000,
        "early",
    )
    dual_rows, raw, first, last = call(
        functools.partial(finish_kernel, subs, last_ones),
        (
            shape((share, NDUAL), F32),
            shape((share, nrhs), F32),
            shape((IFACE, nrhs), F32),
            shape((IFACE, nrhs), F32),
        ),
        (labels, stand, high, low, early, *[arrived[k] for k in last_ones]),
        3_000_000_000,
        "finish",
    )
    peers = lax.axis_size("cluster")
    up = [(i, (i + 1) % peers) for i in range(peers)]
    down = [(j, i) for i, j in up]
    before = lax.ppermute(last, "cluster", up)
    after = lax.ppermute(first, "cluster", down)
    between = jnp.zeros((share - 2 * IFACE, nrhs), F32)
    products = raw + jnp.concatenate([before, between, after], axis=0)
    return (dual_rows, products)


def solution(mesh):
    shards = ("cluster", "member")
    return jax.shard_map(
        on_device,
        mesh=mesh,
        in_specs=(P(shards, None, None), P(shards, None, None), P(shards), P(shards, None), P(shards, None)),
        out_specs=(P(shards, None), P(shards, None)),
        check_vma=False,
    )
```

```python
import functools
import jax, jax.numpy as jnp
from jax import lax
from jax.experimental import pallas as pl
from jax.experimental.pallas import tpu as pltpu
F32, BF = jnp.float32, jnp.bfloat16
from jax.sharding import PartitionSpec as P

STRIDE, BASE = 128, 16
NDUAL, IFACE = 1024, 8

def split(v):
    hi = v.astype(BF)
    return hi, (v - hi.astype(F32)).astype(BF)

def mm(a, b, dims=(((1,), (0,)), ((), ()))):
    return lax.dot_general(a, b, dims, preferred_element_type=F32)

def mm3(a, b):
    ah, al = a
    bh, bl = b
    return mm(ah, bh) + (mm(al, bh) + mm(ah, bl))

def iota(shape, dim):
    return lax.broadcasted_iota(jnp.int32, shape, dim)

def mmk(a, b):
    ah, al = a
    bh, bl = b
    return mm(jnp.concatenate([ah, al], axis=1), jnp.concatenate([bh, bh], axis=0)) + mm(ah, bl)


def turn(v, by):
    return pltpu.roll(v, by, 1)


def split32(v):
    hi = v.astype(BF).astype(F32)
    return hi, v - hi


def eliminate(packs):
    lane = iota((BASE, STRIDE), 1)
    row = iota((BASE, STRIDE), 0)
    local = lane % BASE
    parts = BASE // 8
    start = (iota((8, STRIDE), 1) // BASE) * BASE
    row8 = iota((8, STRIDE), 0)
    eye = (row == local).astype(F32)
    recips, works, pieces = [], [], []
    for packed in packs:
        diag = jnp.sum(jnp.where(row == local, packed, 0.0), axis=0, keepdims=True)
        recip = 1.0 / diag
        scaled = jnp.where(row > local, packed * recip, 0.0)
        recips.append(jnp.broadcast_to(recip, (8, STRIDE)))
        works.append([eye[g * 8:(g + 1) * 8] for g in range(parts)])
        pieces.append([scaled[g * 8:(g + 1) * 8] for g in range(parts)])
    for j in range(BASE - 1):
        for work, piece in zip(works, pieces):
            pivot = work[j // 8][j % 8:j % 8 + 1]
            for g in range((j + 1) // 8, parts):
                column = jnp.take_along_axis(piece[g], start + j, axis=1, mode="promise_in_bounds")
                work[g] = work[g] - column * pivot
    for work, recip in zip(works, recips):
        for g in range(parts):
            work[g] = work[g] * jnp.take_along_axis(recip, start + (row8 + g * 8), axis=1, mode="promise_in_bounds")
    return [jnp.concatenate(work, axis=0) for work in works]


def slabs_of(v, size):
    return [v[r:r + size] for r in range(0, v.shape[0], size)]


def invert_blocks(blocks):
    lane = iota((BASE, STRIDE), 1)
    packs = []
    for block in blocks:
        packed = block[:BASE]
        for q, slab in enumerate(slabs_of(block, BASE)):
            packed = jnp.where(lane // BASE == q, slab, packed) if q else packed
        packs.append(packed)
    inners = eliminate(packs)
    states = [[jnp.where(lane // BASE == q, inner, 0.0) for q in range(STRIDE // BASE)] for inner in inners]
    size = BASE
    while size < STRIDE:
        half = iota((STRIDE // 2, STRIDE), 1) // size
        even = half % 2 == 0
        pair = (half // 2 == iota((STRIDE // 2, STRIDE), 0) // size) & even
        products = []
        for block, slabs in zip(blocks, states):
            ch, cl = split32(jnp.where(pair, jnp.concatenate(slabs_of(block, size)[1::2], axis=0), 0.0))
            a = jnp.concatenate([ch + turn(cl, size), ch], axis=1).astype(BF)
            tops = [split(v) for v in slabs[0::2]]
            w = [v[0] for v in tops for _ in range(2)] + [v[1] for v in tops for _ in range(2)]
            products.append(mm(a, jnp.concatenate(w, axis=0)))
        belows = []
        for product, slabs in zip(products, states):
            xh, xl = split32(jnp.concatenate(slabs[1::2], axis=0))
            a = jnp.concatenate([xh + turn(xl, STRIDE - size), xh], axis=1).astype(BF)
            th, tl = split(product)
            w = [v for v in slabs_of(th, size) for _ in range(2)] + [v for v in slabs_of(tl, size) for _ in range(2)]
            belows.append(slabs_of(mm(a, jnp.concatenate(w, axis=0)), size))
        states = [
            [jnp.concatenate([top, low - add], axis=0) for top, low, add in zip(slabs[0::2], slabs[1::2], below)]
            for slabs, below in zip(states, belows)
        ]
        size *= 2
    return [slabs[0] for slabs in states]


BATCH = 16


def solve_kernel(members, packed_ref, far_ref, p_ref, *refs):
    out_refs = refs[:members]
    rest, f_ref, tails, square_sems, corner_sems, strip_sems, panel_sem, small_sem = refs[members:]
    extra = tails.shape[1]
    ends = packed_ref.at[pl.ds(0, 2), pl.ds(packed_ref.shape[1] - extra, extra)]
    small_copy = pltpu.make_async_copy(ends, tails, small_sem)
    subs, order, width = p_ref.shape
    wide = 2 * STRIDE
    square_copies, corner_copies, strip_copies = {}, {}, {}

    def fetch(s, rows, columns, sem):
        part = (s, rows, columns)
        copy = pltpu.make_async_copy(far_ref.at[part], f_ref.at[part], sem)
        copy.start()
        return copy

    for step, a in enumerate(range(0, order, STRIDE)):
        for s in range(subs):
            square_copies[s, a] = fetch(s, pl.ds(a, STRIDE), pl.ds(a, STRIDE), square_sems.at[s, step])
    small_copy.start()
    for step, a in enumerate(range(0, order, wide)):
        for s in range(subs):
            corner_copies[s, a] = fetch(s, pl.ds(a + STRIDE, STRIDE), pl.ds(a, STRIDE), corner_sems.at[s, step])
    panel_copy = pltpu.make_async_copy(p_ref, rest, panel_sem)
    panel_copy.start()
    for step, a in enumerate(range(0, order - wide, wide)):
        for s in range(subs):
            strip_copies[s, a] = fetch(s, pl.ds(a + wide, order - a - wide), pl.ds(a, wide), strip_sems.at[s, step])
    small_copy.wait()
    lines = subs // 2
    lives = [tails[0, lines + s:lines + s + 1].astype(jnp.int32) for s in range(subs)]
    row = iota((STRIDE, STRIDE), 0)
    col = iota((STRIDE, STRIDE), 1)
    prow = iota((wide, width), 0)
    dims = (((0,), (0,)), ((), ()))
    squares = [jnp.zeros((width, width), F32)] * subs
    crosses = [jnp.zeros((width, width), F32)] * subs
    places = [(s, a) for a in range(0, order, STRIDE) for s in range(subs)]
    small = {}
    for first in range(0, len(places), BATCH):
        batch = places[first:first + BATCH]
        blocks = []
        for s, a in batch:
            square_copies[s, a].wait()
            d = f_ref[s, a:a + STRIDE, a:a + STRIDE]
            keep = (row + a < lives[s][:, :STRIDE]) & (col <= row)
            blocks.append(jnp.where(keep, d, (row == col).astype(F32)))
        for place, inverse in zip(batch, invert_blocks(blocks)):
            small[place] = split(inverse)
    heads = [(s, a) for a in range(0, order, wide) for s in range(subs)]
    corners = []
    for s, a in heads:
        b = a + STRIDE
        corner_copies[s, a].wait()
        corner = jnp.where(row + b < lives[s][:, :STRIDE], f_ref[s, b:b + STRIDE, a:b], 0.0)
        corners.append(split(mmk(split(corner), small[s, a])))
    inverses = {}
    for (s, a), corner in zip(heads, corners):
        above, below = small[s, a], small[s, a + STRIDE]
        turned = split(-mmk(below, corner))
        blank = jnp.zeros((STRIDE, STRIDE), BF)
        inverses[s, a] = [
            jnp.concatenate([jnp.concatenate([u, blank], axis=1), jnp.concatenate([t, l], axis=1)], axis=0)
            for u, t, l in zip(above, turned, below)
        ]

    capacity = 2 * width // members
    glue = jnp.concatenate([tails[0, :lines], tails[1, :lines]], axis=0).astype(jnp.int32)
    place = lax.axis_index("member")
    before = (iota((width, width), 0) < iota((width, width), 1)).astype(BF)
    dispatches = []
    for s in range(subs):
        owner = glue[s:s + 1] // (NDUAL // members)
        owners = (iota((members, width), 0) == owner)
        ranks = mm(owners.astype(BF), before)
        rank = jnp.sum(jnp.where(owners, ranks, 0.0), axis=0, keepdims=True).astype(jnp.int32)
        target = (owner ^ place) * capacity + rank
        dispatches.append((iota((members * capacity, width), 0) == target).astype(BF))
    panel_copy.wait()
    for a in range(0, order, wide):
        solved = []
        for s in range(subs):
            now = jnp.where(prow + a < lives[s], rest[s, a:a + wide], 0.0)
            solved.append(split(mm3(inverses[s, a], split(now))))
        if a + wide < order:
            for s in range(subs):
                strip_copies[s, a].wait()
        for c in range(a + wide, order, wide):
            for s in range(subs):
                rest[s, c:c + wide] = rest[s, c:c + wide] - mm3(split(f_ref[s, c:c + wide, a:a + wide]), solved[s])
        for s in range(subs):
            hi, lo = solved[s]
            squares[s] = squares[s] + mm(hi, hi, dims)
            crosses[s] = crosses[s] + mm(hi, lo, dims)
    duals = [split(squares[s] + (crosses[s] + crosses[s].T)) for s in range(subs)]
    for s in range(subs):
        values = mm(dispatches[s], duals[s][0]) + mm(dispatches[s], duals[s][1])
        for k in range(members):
            out_refs[k][s * capacity:(s + 1) * capacity] = values[k * capacity:(k + 1) * capacity]


def solve(packed, factors, panels, members):
    subs, order, width = panels.shape
    capacity = 2 * width // members
    vm = pl.BlockSpec(memory_space=pltpu.VMEM)
    far = pl.BlockSpec(memory_space=pltpu.HBM)
    return pl.pallas_call(
        functools.partial(solve_kernel, members),
        out_shape=[jax.ShapeDtypeStruct((subs * capacity, width), F32)] * members,
        in_specs=[far] * 3,
        out_specs=[vm] * members,
        scratch_shapes=[
            pltpu.VMEM((subs, order, width), F32),
            pltpu.VMEM((subs, order, order), F32),
            pltpu.VMEM((2, tail_rows(subs), width), F32),
            pltpu.SemaphoreType.DMA((subs, order // STRIDE)),
            pltpu.SemaphoreType.DMA((subs, order // (2 * STRIDE))),
            pltpu.SemaphoreType.DMA((subs, order // (2 * STRIDE))),
            pltpu.SemaphoreType.DMA,
            pltpu.SemaphoreType.DMA,
        ],
        compiler_params=pltpu.CompilerParams(vmem_limit_bytes=53760 << 10),
        cost_estimate=pl.CostEstimate(flops=10_000_000_000, bytes_accessed=8 << 20, transcendentals=0),
        name="solve",
    )(packed, factors, panels)


def tail_rows(subs):
    return 8 * (-(-(subs // 2 + subs) // 8))


def pack_kernel(loads_ref, glue_ref, sizes_ref, out_ref, held, lines_of, sizes_of, tail, in_sems, load_sems, tail_sems):
    members, rows, nrhs = out_ref.shape
    subs = glue_ref.shape[0]
    half, lines = loads_ref.shape[0] // 2, subs // 2
    labels = pltpu.make_async_copy(glue_ref, lines_of, in_sems.at[0])
    load = pltpu.make_async_copy(loads_ref, held, in_sems.at[1])
    sizes = pltpu.make_async_copy(sizes_ref, sizes_of, in_sems.at[2])
    labels.start()
    sizes.start()
    load.start()
    labels.wait()
    sizes.wait()
    lives = [jnp.full((1, nrhs), sizes_of[s], jnp.int32).astype(F32) for s in range(subs)]
    blank = [jnp.zeros((rows - half - lines - subs, nrhs), F32)]
    for part in range(2):
        line = lines_of[part * lines:(part + 1) * lines].astype(F32)
        tail[part] = jnp.concatenate([line, *lives, *blank], axis=0)
    copies = []
    for k in range(members):
        copies.append(pltpu.make_async_copy(tail.at[k % 2], out_ref.at[k, pl.ds(half, rows - half)], tail_sems.at[k]))
        copies[-1].start()
    load.wait()
    for k in range(members):
        rows_of = held.at[pl.ds(k % 2 * half, half)]
        copies.append(pltpu.make_async_copy(rows_of, out_ref.at[k, pl.ds(0, half)], load_sems.at[k]))
        copies[-1].start()
    for copy in copies:
        copy.wait()


def pack(loads, glue, sizes, members):
    subs = glue.shape[0]
    share, nrhs = loads.shape
    rows = share // 2 + tail_rows(subs)
    far = pl.BlockSpec(memory_space=pltpu.HBM)
    return pl.pallas_call(
        pack_kernel,
        out_shape=jax.ShapeDtypeStruct((members, rows, nrhs), F32),
        in_specs=[far] * 3,
        out_specs=far,
        scratch_shapes=[
            pltpu.VMEM((share, nrhs), F32),
            pltpu.VMEM(glue.shape, jnp.int32),
            pltpu.SMEM(sizes.shape, jnp.int32),
            pltpu.VMEM((2, rows - share // 2, nrhs), F32),
            pltpu.SemaphoreType.DMA((3,)),
            pltpu.SemaphoreType.DMA((members,)),
            pltpu.SemaphoreType.DMA((members,)),
        ],
        compiler_params=pltpu.CompilerParams(vmem_limit_bytes=58 << 20),
        cost_estimate=pl.CostEstimate(flops=1_000_000, bytes_accessed=1 << 20, transcendentals=0),
        name="pack",
    )(loads, glue, sizes)


def routes_kernel(subs, place_ref, own_ref, twin_ref, stand_ref, label_ref, high_ref, low_ref):
    members, block, width = own_ref.shape
    share = NDUAL // members
    half, lines = share // 2, subs // 2
    slots = label_ref.shape[1]
    capacity = slots // subs
    first_core = place_ref[0] % 2 == 0
    glue = []
    for k in range(members):
        source = place_ref[0] ^ k
        pair = own_ref[source], twin_ref[source]
        for part in range(2):
            got = jnp.where(first_core, pair[part], pair[1 - part])
            row = pl.ds(pl.multiple_of(source * share + part * half, half), half)
            high_ref[row], low_ref[row] = split(got[:half])
            glue.append(got[half:half + lines])
    glue = jnp.concatenate(glue, axis=0)
    stand_ref[...] = glue.T.astype(jnp.int32)
    glue = glue.astype(jnp.int32)
    first = place_ref[0] * share
    mine = (glue >= first) & (glue < first + share)
    before = (iota((width, width), 0) < iota((width, width), 1)).astype(BF)
    ranks = mm(mine.astype(BF), before).astype(jnp.int32)
    local = jnp.where(mine, glue - first + 1, 0).astype(F32).astype(BF)
    labels = []
    for k in range(members):
        found = jnp.full((1, slots), -1.0, F32)
        for s in range(subs):
            i = k * subs + s
            rank = jnp.where(mine[i:i + 1], ranks[i:i + 1] + s * capacity, -1)
            at_slot = (iota((slots, width), 0) == rank).astype(BF)
            line = mm(local[i:i + 1], at_slot, (((1,), (1,)), ((), ())))
            found = jnp.where(line > 0.5, line + (s * share - 1), found)
        labels.append(found)
    label_ref[...] = jnp.concatenate(labels, axis=0).astype(jnp.int32)


def placed(subs, sources, label_ref, stand_ref, values):
    slots, width = values[0].shape
    share = NDUAL // label_ref.shape[0]
    total = jnp.zeros((2 * share, NDUAL), F32)
    for k, value in zip(sources, values):
        rows = (iota((subs * share, slots), 0) == label_ref[k:k + 1]).astype(BF)
        moved = mm(rows, jnp.concatenate(split(value[...]), axis=1)).astype(BF)
        for s in range(subs):
            i = k * subs + s
            part = moved[s * share:(s + 1) * share]
            columns = (iota((width, NDUAL), 1) == stand_ref[:, i:i + 1]).astype(BF)
            total = total + mm(jnp.concatenate([part[:, :width], part[:, width:]], axis=0), columns)
    return total[:share] + total[share:]


def early_kernel(subs, sources, label_ref, stand_ref, *refs):
    refs[-1][...] = placed(subs, sources, label_ref, stand_ref, refs[:-1])


def finish_kernel(subs, sources, label_ref, stand_ref, high_ref, low_ref, early_ref, *refs):
    values, (dual_ref, raw_ref, first_ref, last_ref) = refs[:-4], refs[-4:]
    dual = early_ref[...] + placed(subs, sources, label_ref, stand_ref, values)
    dual_ref[...] = dual
    raw = mm3(split(dual), (high_ref[...], low_ref[...]))
    raw_ref[...] = raw
    first_ref[...] = raw[:IFACE]
    last_ref[...] = raw[raw.shape[0] - IFACE:]


def call(kernel, outs, args, flops, name, smem=0):
    vm = pl.BlockSpec(memory_space=pltpu.VMEM)
    specs = [pl.BlockSpec(memory_space=pltpu.SMEM)] * smem + [vm] * (len(args) - smem)
    return pl.pallas_call(
        kernel,
        out_shape=outs,
        in_specs=specs,
        out_specs=jax.tree.map(lambda _: vm, outs),
        compiler_params=pltpu.CompilerParams(vmem_limit_bytes=16 << 20),
        cost_estimate=pl.CostEstimate(flops=flops, bytes_accessed=4 << 20, transcendentals=0),
        name=name,
    )(*args)


def on_device(factors, panels, sizes, glue_index, loads):
    members = lax.axis_size("member")
    subs, order, width = panels.shape
    share, nrhs = loads.shape
    capacity = 2 * width // members
    slots = subs * capacity
    count = members * subs
    shape = jax.ShapeDtypeStruct
    place = lax.axis_index("member").astype(jnp.int32).reshape(1)

    def across(value, distance):
        return lax.ppermute(value, "member", [(i, i ^ distance) for i in range(members)])

    packed = pack(loads, glue_index, sizes, members)
    own = lax.all_to_all(packed, "member", split_axis=0, concat_axis=0, tiled=True)
    values = solve(packed, factors, panels, members)
    own, *values = lax.optimization_barrier((own, *values))
    distances = [*range(2, members, 2), *range(3, members, 2), 1]
    arrived = {0: values[0], **{k: across(values[k], k) for k in distances}}
    last_ones = distances[-3:-1]
    first_ones = [k for k in arrived if k not in last_ones]
    twin = across(own, 1)
    stand, labels, high, low = call(
        functools.partial(routes_kernel, subs),
        (
            shape((width, count), jnp.int32),
            shape((members, slots), jnp.int32),
            shape((NDUAL, nrhs), BF),
            shape((NDUAL, nrhs), BF),
        ),
        (place, own, twin),
        2_000_000_000,
        "routes",
        smem=1,
    )
    early = call(
        functools.partial(early_kernel, subs, first_ones),
        shape((share, NDUAL), F32),
        (labels, stand, *[arrived[k] for k in first_ones]),
        2_000_000_000,
        "early",
    )
    dual_rows, raw, first, last = call(
        functools.partial(finish_kernel, subs, last_ones),
        (
            shape((share, NDUAL), F32),
            shape((share, nrhs), F32),
            shape((IFACE, nrhs), F32),
            shape((IFACE, nrhs), F32),
        ),
        (labels, stand, high, low, early, *[arrived[k] for k in last_ones]),
        3_000_000_000,
        "finish",
    )
    peers = lax.axis_size("cluster")
    up = [(i, (i + 1) % peers) for i in range(peers)]
    down = [(j, i) for i, j in up]
    before = lax.ppermute(last, "cluster", up)
    after = lax.ppermute(first, "cluster", down)
    between = jnp.zeros((share - 2 * IFACE, nrhs), F32)
    products = raw + jnp.concatenate([before, between, after], axis=0)
    return (dual_rows, products)


def solution(mesh):
    shards = ("cluster", "member")
    return jax.shard_map(
        on_device,
        mesh=mesh,
        in_specs=(P(shards, None, None), P(shards, None, None), P(shards), P(shards, None), P(shards, None)),
        out_specs=(P(shards, None), P(shards, None)),
        check_vma=False,
    )
```

```python
import functools
import jax, jax.numpy as jnp
from jax import lax
from jax.experimental import pallas as pl
from jax.experimental.pallas import tpu as pltpu
F32, BF = jnp.float32, jnp.bfloat16
from jax.sharding import PartitionSpec as P

STRIDE, BASE = 128, 16
NDUAL, IFACE = 1024, 8

def split(v):
    hi = v.astype(BF)
    return hi, (v - hi.astype(F32)).astype(BF)

def mm(a, b, dims=(((1,), (0,)), ((), ()))):
    return lax.dot_general(a, b, dims, preferred_element_type=F32)

def mm3(a, b):
    ah, al = a
    bh, bl = b
    return mm(ah, bh) + (mm(al, bh) + mm(ah, bl))

def iota(shape, dim):
    return lax.broadcasted_iota(jnp.int32, shape, dim)

def mmk(a, b):
    ah, al = a
    bh, bl = b
    return mm(jnp.concatenate([ah, al], axis=1), jnp.concatenate([bh, bh], axis=0)) + mm(ah, bl)


def turn(v, by):
    return pltpu.roll(v, by, 1)


def split32(v):
    hi = v.astype(BF).astype(F32)
    return hi, v - hi


def eliminate(packs):
    lane = iota((BASE, STRIDE), 1)
    row = iota((BASE, STRIDE), 0)
    local = lane % BASE
    parts = BASE // 8
    start = (iota((8, STRIDE), 1) // BASE) * BASE
    row8 = iota((8, STRIDE), 0)
    eye = (row == local).astype(F32)
    recips, works, pieces = [], [], []
    for packed in packs:
        diag = jnp.sum(jnp.where(row == local, packed, 0.0), axis=0, keepdims=True)
        recip = 1.0 / diag
        scaled = jnp.where(row > local, packed * recip, 0.0)
        recips.append(jnp.broadcast_to(recip, (8, STRIDE)))
        works.append([eye[g * 8:(g + 1) * 8] for g in range(parts)])
        pieces.append([scaled[g * 8:(g + 1) * 8] for g in range(parts)])
    for j in range(BASE - 1):
        for work, piece in zip(works, pieces):
            pivot = work[j // 8][j % 8:j % 8 + 1]
            for g in range((j + 1) // 8, parts):
                column = jnp.take_along_axis(piece[g], start + j, axis=1, mode="promise_in_bounds")
                work[g] = work[g] - column * pivot
    for work, recip in zip(works, recips):
        for g in range(parts):
            work[g] = work[g] * jnp.take_along_axis(recip, start + (row8 + g * 8), axis=1, mode="promise_in_bounds")
    return [jnp.concatenate(work, axis=0) for work in works]


def slabs_of(v, size):
    return [v[r:r + size] for r in range(0, v.shape[0], size)]


def invert_blocks(blocks):
    lane = iota((BASE, STRIDE), 1)
    packs = []
    for block in blocks:
        packed = block[:BASE]
        for q, slab in enumerate(slabs_of(block, BASE)):
            packed = jnp.where(lane // BASE == q, slab, packed) if q else packed
        packs.append(packed)
    inners = eliminate(packs)
    states = [[jnp.where(lane // BASE == q, inner, 0.0) for q in range(STRIDE // BASE)] for inner in inners]
    size = BASE
    while size < STRIDE:
        half = iota((STRIDE // 2, STRIDE), 1) // size
        even = half % 2 == 0
        pair = (half // 2 == iota((STRIDE // 2, STRIDE), 0) // size) & even
        products = []
        for block, slabs in zip(blocks, states):
            ch, cl = split32(jnp.where(pair, jnp.concatenate(slabs_of(block, size)[1::2], axis=0), 0.0))
            a = jnp.concatenate([ch + turn(cl, size), ch], axis=1).astype(BF)
            tops = [split(v) for v in slabs[0::2]]
            w = [v[0] for v in tops for _ in range(2)] + [v[1] for v in tops for _ in range(2)]
            products.append(mm(a, jnp.concatenate(w, axis=0)))
        belows = []
        for product, slabs in zip(products, states):
            xh, xl = split32(jnp.concatenate(slabs[1::2], axis=0))
            a = jnp.concatenate([xh + turn(xl, STRIDE - size), xh], axis=1).astype(BF)
            th, tl = split(product)
            w = [v for v in slabs_of(th, size) for _ in range(2)] + [v for v in slabs_of(tl, size) for _ in range(2)]
            belows.append(slabs_of(mm(a, jnp.concatenate(w, axis=0)), size))
        states = [
            [jnp.concatenate([top, low - add], axis=0) for top, low, add in zip(slabs[0::2], slabs[1::2], below)]
            for slabs, below in zip(states, belows)
        ]
        size *= 2
    return [slabs[0] for slabs in states]


BATCH = 16


def solve_kernel(members, packed_ref, far_ref, p_ref, *refs):
    out_refs = refs[:members]
    rest, f_ref, tails, square_sems, corner_sems, strip_sems, panel_sem, small_sem = refs[members:]
    extra = tails.shape[1]
    ends = packed_ref.at[pl.ds(0, 2), pl.ds(packed_ref.shape[1] - extra, extra)]
    small_copy = pltpu.make_async_copy(ends, tails, small_sem)
    small_copy.start()
    subs, order, width = p_ref.shape
    wide = 2 * STRIDE
    square_copies, corner_copies, strip_copies = {}, {}, {}

    def fetch(s, rows, columns, sem):
        part = (s, rows, columns)
        copy = pltpu.make_async_copy(far_ref.at[part], f_ref.at[part], sem)
        copy.start()
        return copy

    for step, a in enumerate(range(0, order, STRIDE)):
        for s in range(subs):
            square_copies[s, a] = fetch(s, pl.ds(a, STRIDE), pl.ds(a, STRIDE), square_sems.at[s, step])
    for step, a in enumerate(range(0, order, wide)):
        for s in range(subs):
            corner_copies[s, a] = fetch(s, pl.ds(a + STRIDE, STRIDE), pl.ds(a, STRIDE), corner_sems.at[s, step])
    panel_copy = pltpu.make_async_copy(p_ref, rest, panel_sem)
    panel_copy.start()
    for step, a in enumerate(range(0, order - wide, wide)):
        for s in range(subs):
            strip_copies[s, a] = fetch(s, pl.ds(a + wide, order - a - wide), pl.ds(a, wide), strip_sems.at[s, step])
    small_copy.wait()
    lines = subs // 2
    lives = [tails[0, lines + s:lines + s + 1].astype(jnp.int32) for s in range(subs)]
    row = iota((STRIDE, STRIDE), 0)
    col = iota((STRIDE, STRIDE), 1)
    prow = iota((wide, width), 0)
    dims = (((0,), (0,)), ((), ()))
    squares = [jnp.zeros((width, width), F32)] * subs
    crosses = [jnp.zeros((width, width), F32)] * subs
    places = [(s, a) for a in range(0, order, STRIDE) for s in range(subs)]
    small = {}
    for first in range(0, len(places), BATCH):
        batch = places[first:first + BATCH]
        blocks = []
        for s, a in batch:
            square_copies[s, a].wait()
            d = f_ref[s, a:a + STRIDE, a:a + STRIDE]
            keep = (row + a < lives[s][:, :STRIDE]) & (col <= row)
            blocks.append(jnp.where(keep, d, (row == col).astype(F32)))
        for place, inverse in zip(batch, invert_blocks(blocks)):
            small[place] = split(inverse)
    heads = [(s, a) for a in range(0, order, wide) for s in range(subs)]
    corners = []
    for s, a in heads:
        b = a + STRIDE
        corner_copies[s, a].wait()
        corner = jnp.where(row + b < lives[s][:, :STRIDE], f_ref[s, b:b + STRIDE, a:b], 0.0)
        corners.append(split(mmk(split(corner), small[s, a])))
    inverses = {}
    for (s, a), corner in zip(heads, corners):
        above, below = small[s, a], small[s, a + STRIDE]
        turned = split(-mmk(below, corner))
        blank = jnp.zeros((STRIDE, STRIDE), BF)
        inverses[s, a] = [
            jnp.concatenate([jnp.concatenate([u, blank], axis=1), jnp.concatenate([t, l], axis=1)], axis=0)
            for u, t, l in zip(above, turned, below)
        ]

    capacity = 2 * width // members
    glue = jnp.concatenate([tails[0, :lines], tails[1, :lines]], axis=0).astype(jnp.int32)
    place = lax.axis_index("member")
    before = (iota((width, width), 0) < iota((width, width), 1)).astype(BF)
    dispatches = []
    for s in range(subs):
        owner = glue[s:s + 1] // (NDUAL // members)
        owners = (iota((members, width), 0) == owner)
        ranks = mm(owners.astype(BF), before)
        rank = jnp.sum(jnp.where(owners, ranks, 0.0), axis=0, keepdims=True).astype(jnp.int32)
        target = (owner ^ place) * capacity + rank
        dispatches.append((iota((members * capacity, width), 0) == target).astype(BF))
    panel_copy.wait()
    for a in range(0, order, wide):
        solved = []
        for s in range(subs):
            now = jnp.where(prow + a < lives[s], rest[s, a:a + wide], 0.0)
            solved.append(split(mm3(inverses[s, a], split(now))))
        if a + wide < order:
            for s in range(subs):
                strip_copies[s, a].wait()
        for c in range(a + wide, order, wide):
            for s in range(subs):
                rest[s, c:c + wide] = rest[s, c:c + wide] - mm3(split(f_ref[s, c:c + wide, a:a + wide]), solved[s])
        for s in range(subs):
            hi, lo = solved[s]
            squares[s] = squares[s] + mm(hi, hi, dims)
            crosses[s] = crosses[s] + mm(hi, lo, dims)
    duals = [split(squares[s] + (crosses[s] + crosses[s].T)) for s in range(subs)]
    for s in range(subs):
        values = mm(dispatches[s], duals[s][0]) + mm(dispatches[s], duals[s][1])
        for k in range(members):
            out_refs[k][s * capacity:(s + 1) * capacity] = values[k * capacity:(k + 1) * capacity]


def solve(packed, factors, panels, members):
    subs, order, width = panels.shape
    capacity = 2 * width // members
    vm = pl.BlockSpec(memory_space=pltpu.VMEM)
    far = pl.BlockSpec(memory_space=pltpu.HBM)
    return pl.pallas_call(
        functools.partial(solve_kernel, members),
        out_shape=[jax.ShapeDtypeStruct((subs * capacity, width), F32)] * members,
        in_specs=[far] * 3,
        out_specs=[vm] * members,
        scratch_shapes=[
            pltpu.VMEM((subs, order, width), F32),
            pltpu.VMEM((subs, order, order), F32),
            pltpu.VMEM((2, tail_rows(subs), width), F32),
            pltpu.SemaphoreType.DMA((subs, order // STRIDE)),
            pltpu.SemaphoreType.DMA((subs, order // (2 * STRIDE))),
            pltpu.SemaphoreType.DMA((subs, order // (2 * STRIDE))),
            pltpu.SemaphoreType.DMA,
            pltpu.SemaphoreType.DMA,
        ],
        compiler_params=pltpu.CompilerParams(vmem_limit_bytes=52 << 20),
        cost_estimate=pl.CostEstimate(flops=10_000_000_000, bytes_accessed=8 << 20, transcendentals=0),
        name="solve",
    )(packed, factors, panels)


def tail_rows(subs):
    return 8 * (-(-(subs // 2 + subs) // 8))


def pack_kernel(loads_ref, glue_ref, sizes_ref, out_ref, held, lines_of, sizes_of, tail, in_sems, load_sems, tail_sems):
    members, rows, nrhs = out_ref.shape
    subs = glue_ref.shape[0]
    half, lines = loads_ref.shape[0] // 2, subs // 2
    labels = pltpu.make_async_copy(glue_ref, lines_of, in_sems.at[0])
    load = pltpu.make_async_copy(loads_ref, held, in_sems.at[1])
    sizes = pltpu.make_async_copy(sizes_ref, sizes_of, in_sems.at[2])
    labels.start()
    sizes.start()
    load.start()
    labels.wait()
    sizes.wait()
    lives = [jnp.full((1, nrhs), sizes_of[s], jnp.int32).astype(F32) for s in range(subs)]
    blank = [jnp.zeros((rows - half - lines - subs, nrhs), F32)]
    for part in range(2):
        line = lines_of[part * lines:(part + 1) * lines].astype(F32)
        tail[part] = jnp.concatenate([line, *lives, *blank], axis=0)
    copies = []
    for k in range(members):
        copies.append(pltpu.make_async_copy(tail.at[k % 2], out_ref.at[k, pl.ds(half, rows - half)], tail_sems.at[k]))
        copies[-1].start()
    load.wait()
    for k in range(members):
        rows_of = held.at[pl.ds(k % 2 * half, half)]
        copies.append(pltpu.make_async_copy(rows_of, out_ref.at[k, pl.ds(0, half)], load_sems.at[k]))
        copies[-1].start()
    for copy in copies:
        copy.wait()


def pack(loads, glue, sizes, members):
    subs = glue.shape[0]
    share, nrhs = loads.shape
    rows = share // 2 + tail_rows(subs)
    far = pl.BlockSpec(memory_space=pltpu.HBM)
    return pl.pallas_call(
        pack_kernel,
        out_shape=jax.ShapeDtypeStruct((members, rows, nrhs), F32),
        in_specs=[far] * 3,
        out_specs=far,
        scratch_shapes=[
            pltpu.VMEM((share, nrhs), F32),
            pltpu.VMEM(glue.shape, jnp.int32),
            pltpu.SMEM(sizes.shape, jnp.int32),
            pltpu.VMEM((2, rows - share // 2, nrhs), F32),
            pltpu.SemaphoreType.DMA((3,)),
            pltpu.SemaphoreType.DMA((members,)),
            pltpu.SemaphoreType.DMA((members,)),
        ],
        compiler_params=pltpu.CompilerParams(vmem_limit_bytes=58 << 20),
        cost_estimate=pl.CostEstimate(flops=1_000_000, bytes_accessed=1 << 20, transcendentals=0),
        name="pack",
    )(loads, glue, sizes)


def routes_kernel(subs, place_ref, own_ref, twin_ref, stand_ref, label_ref, high_ref, low_ref):
    members, block, width = own_ref.shape
    share = NDUAL // members
    half, lines = share // 2, subs // 2
    slots = label_ref.shape[1]
    capacity = slots // subs
    first_core = place_ref[0] % 2 == 0
    glue = []
    for k in range(members):
        source = place_ref[0] ^ k
        pair = own_ref[source], twin_ref[source]
        for part in range(2):
            got = jnp.where(first_core, pair[part], pair[1 - part])
            row = pl.ds(pl.multiple_of(source * share + part * half, half), half)
            high_ref[row], low_ref[row] = split(got[:half])
            glue.append(got[half:half + lines])
    glue = jnp.concatenate(glue, axis=0)
    stand_ref[...] = glue.T.astype(jnp.int32)
    glue = glue.astype(jnp.int32)
    first = place_ref[0] * share
    mine = (glue >= first) & (glue < first + share)
    before = (iota((width, width), 0) < iota((width, width), 1)).astype(BF)
    ranks = mm(mine.astype(BF), before).astype(jnp.int32)
    local = jnp.where(mine, glue - first + 1, 0).astype(F32).astype(BF)
    labels = []
    for k in range(members):
        found = jnp.full((1, slots), -1.0, F32)
        for s in range(subs):
            i = k * subs + s
            rank = jnp.where(mine[i:i + 1], ranks[i:i + 1] + s * capacity, -1)
            at_slot = (iota((slots, width), 0) == rank).astype(BF)
            line = mm(local[i:i + 1], at_slot, (((1,), (1,)), ((), ())))
            found = jnp.where(line > 0.5, line + (s * share - 1), found)
        labels.append(found)
    label_ref[...] = jnp.concatenate(labels, axis=0).astype(jnp.int32)


def placed(subs, sources, label_ref, stand_ref, values):
    slots, width = values[0].shape
    share = NDUAL // label_ref.shape[0]
    total = jnp.zeros((2 * share, NDUAL), F32)
    for k, value in zip(sources, values):
        rows = (iota((subs * share, slots), 0) == label_ref[k:k + 1]).astype(BF)
        moved = mm(rows, jnp.concatenate(split(value[...]), axis=1)).astype(BF)
        for s in range(subs):
            i = k * subs + s
            part = moved[s * share:(s + 1) * share]
            columns = (iota((width, NDUAL), 1) == stand_ref[:, i:i + 1]).astype(BF)
            total = total + mm(jnp.concatenate([part[:, :width], part[:, width:]], axis=0), columns)
    return total[:share] + total[share:]


def early_kernel(subs, sources, label_ref, stand_ref, *refs):
    refs[-1][...] = placed(subs, sources, label_ref, stand_ref, refs[:-1])


def finish_kernel(subs, sources, label_ref, stand_ref, high_ref, low_ref, early_ref, *refs):
    values, (dual_ref, raw_ref, first_ref, last_ref) = refs[:-4], refs[-4:]
    dual = early_ref[...] + placed(subs, sources, label_ref, stand_ref, values)
    dual_ref[...] = dual
    raw = mm3(split(dual), (high_ref[...], low_ref[...]))
    raw_ref[...] = raw
    first_ref[...] = raw[:IFACE]
    last_ref[...] = raw[raw.shape[0] - IFACE:]


def call(kernel, outs, args, flops, name, smem=0):
    vm = pl.BlockSpec(memory_space=pltpu.VMEM)
    specs = [pl.BlockSpec(memory_space=pltpu.SMEM)] * smem + [vm] * (len(args) - smem)
    return pl.pallas_call(
        kernel,
        out_shape=outs,
        in_specs=specs,
        out_specs=jax.tree.map(lambda _: vm, outs),
        compiler_params=pltpu.CompilerParams(vmem_limit_bytes=16 << 20),
        cost_estimate=pl.CostEstimate(flops=flops, bytes_accessed=4 << 20, transcendentals=0),
        name=name,
    )(*args)


def on_device(factors, panels, sizes, glue_index, loads):
    members = lax.axis_size("member")
    subs, order, width = panels.shape
    share, nrhs = loads.shape
    capacity = 2 * width // members
    slots = subs * capacity
    count = members * subs
    shape = jax.ShapeDtypeStruct
    place = lax.axis_index("member").astype(jnp.int32).reshape(1)

    def across(value, distance):
        return lax.ppermute(value, "member", [(i, i ^ distance) for i in range(members)])

    packed = pack(loads, glue_index, sizes, members)
    own = lax.all_to_all(packed, "member", split_axis=0, concat_axis=0, tiled=True)
    values = solve(packed, factors, panels, members)
    own, *values = lax.optimization_barrier((own, *values))
    distances = [*range(2, members, 2), members - 1, *range(3, members - 1, 2), 1]
    arrived = {0: values[0], **{k: across(values[k], k) for k in distances}}
    last_ones = distances[-3:-1]
    first_ones = [k for k in arrived if k not in last_ones]
    twin = across(own, 1)
    stand, labels, high, low = call(
        functools.partial(routes_kernel, subs),
        (
            shape((width, count), jnp.int32),
            shape((members, slots), jnp.int32),
            shape((NDUAL, nrhs), BF),
            shape((NDUAL, nrhs), BF),
        ),
        (place, own, twin),
        2_000_000_000,
        "routes",
        smem=1,
    )
    early = call(
        functools.partial(early_kernel, subs, first_ones),
        shape((share, NDUAL), F32),
        (labels, stand, *[arrived[k] for k in first_ones]),
        2_000_000_000,
        "early",
    )
    dual_rows, raw, first, last = call(
        functools.partial(finish_kernel, subs, last_ones),
        (
            shape((share, NDUAL), F32),
            shape((share, nrhs), F32),
            shape((IFACE, nrhs), F32),
            shape((IFACE, nrhs), F32),
        ),
        (labels, stand, high, low, early, *[arrived[k] for k in last_ones]),
        3_000_000_000,
        "finish",
    )
    peers = lax.axis_size("cluster")
    up = [(i, (i + 1) % peers) for i in range(peers)]
    down = [(j, i) for i, j in up]
    before = lax.ppermute(last, "cluster", up)
    after = lax.ppermute(first, "cluster", down)
    between = jnp.zeros((share - 2 * IFACE, nrhs), F32)
    products = raw + jnp.concatenate([before, between, after], axis=0)
    return (dual_rows, products)


def solution(mesh):
    shards = ("cluster", "member")
    return jax.shard_map(
        on_device,
        mesh=mesh,
        in_specs=(P(shards, None, None), P(shards, None, None), P(shards), P(shards, None), P(shards, None)),
        out_specs=(P(shards, None), P(shards, None)),
        check_vma=False,
    )
```

```python
import functools
import jax, jax.numpy as jnp
from jax import lax
from jax.experimental import pallas as pl
from jax.experimental.pallas import tpu as pltpu
F32, BF = jnp.float32, jnp.bfloat16
from jax.sharding import PartitionSpec as P

STRIDE, BASE = 128, 16
NDUAL, IFACE = 1024, 8

def split(v):
    hi = v.astype(BF)
    return hi, (v - hi.astype(F32)).astype(BF)

def mm(a, b, dims=(((1,), (0,)), ((), ()))):
    return lax.dot_general(a, b, dims, preferred_element_type=F32)

def mm3(a, b):
    ah, al = a
    bh, bl = b
    return mm(ah, bh) + (mm(al, bh) + mm(ah, bl))

def iota(shape, dim):
    return lax.broadcasted_iota(jnp.int32, shape, dim)

def mmk(a, b):
    ah, al = a
    bh, bl = b
    return mm(jnp.concatenate([ah, al], axis=1), jnp.concatenate([bh, bh], axis=0)) + mm(ah, bl)


def turn(v, by):
    return pltpu.roll(v, by, 1)


def split32(v):
    hi = v.astype(BF).astype(F32)
    return hi, v - hi


def eliminate(packs):
    lane = iota((BASE, STRIDE), 1)
    row = iota((BASE, STRIDE), 0)
    local = lane % BASE
    parts = BASE // 8
    start = (iota((8, STRIDE), 1) // BASE) * BASE
    row8 = iota((8, STRIDE), 0)
    eye = (row == local).astype(F32)
    recips, works, pieces = [], [], []
    for packed in packs:
        diag = jnp.sum(jnp.where(row == local, packed, 0.0), axis=0, keepdims=True)
        recip = 1.0 / diag
        scaled = jnp.where(row > local, packed * recip, 0.0)
        recips.append(jnp.broadcast_to(recip, (8, STRIDE)))
        works.append([eye[g * 8:(g + 1) * 8] for g in range(parts)])
        pieces.append([scaled[g * 8:(g + 1) * 8] for g in range(parts)])
    for j in range(BASE - 1):
        for work, piece in zip(works, pieces):
            pivot = work[j // 8][j % 8:j % 8 + 1]
            for g in range((j + 1) // 8, parts):
                column = jnp.take_along_axis(piece[g], start + j, axis=1, mode="promise_in_bounds")
                work[g] = work[g] - column * pivot
    for work, recip in zip(works, recips):
        for g in range(parts):
            work[g] = work[g] * jnp.take_along_axis(recip, start + (row8 + g * 8), axis=1, mode="promise_in_bounds")
    return [jnp.concatenate(work, axis=0) for work in works]


def slabs_of(v, size):
    return [v[r:r + size] for r in range(0, v.shape[0], size)]


def invert_blocks(blocks):
    lane = iota((BASE, STRIDE), 1)
    packs = []
    for block in blocks:
        packed = block[:BASE]
        for q, slab in enumerate(slabs_of(block, BASE)):
            packed = jnp.where(lane // BASE == q, slab, packed) if q else packed
        packs.append(packed)
    inners = eliminate(packs)
    states = [[jnp.where(lane // BASE == q, inner, 0.0) for q in range(STRIDE // BASE)] for inner in inners]
    size = BASE
    while size < STRIDE:
        half = iota((STRIDE // 2, STRIDE), 1) // size
        even = half % 2 == 0
        pair = (half // 2 == iota((STRIDE // 2, STRIDE), 0) // size) & even
        products = []
        for block, slabs in zip(blocks, states):
            ch, cl = split32(jnp.where(pair, jnp.concatenate(slabs_of(block, size)[1::2], axis=0), 0.0))
            a = jnp.concatenate([ch + turn(cl, size), ch], axis=1).astype(BF)
            tops = [split(v) for v in slabs[0::2]]
            w = [v[0] for v in tops for _ in range(2)] + [v[1] for v in tops for _ in range(2)]
            products.append(mm(a, jnp.concatenate(w, axis=0)))
        belows = []
        for product, slabs in zip(products, states):
            xh, xl = split32(jnp.concatenate(slabs[1::2], axis=0))
            a = jnp.concatenate([xh + turn(xl, STRIDE - size), xh], axis=1).astype(BF)
            th, tl = split(product)
            w = [v for v in slabs_of(th, size) for _ in range(2)] + [v for v in slabs_of(tl, size) for _ in range(2)]
            belows.append(slabs_of(mm(a, jnp.concatenate(w, axis=0)), size))
        states = [
            [jnp.concatenate([top, low - add], axis=0) for top, low, add in zip(slabs[0::2], slabs[1::2], below)]
            for slabs, below in zip(states, belows)
        ]
        size *= 2
    return [slabs[0] for slabs in states]


BATCH = 16


def solve_kernel(members, packed_ref, far_ref, p_ref, *refs):
    out_refs = refs[:members]
    rest, f_ref, tails, square_sems, corner_sems, strip_sems, panel_sem, small_sem = refs[members:]
    extra = tails.shape[1]
    ends = packed_ref.at[pl.ds(0, 2), pl.ds(packed_ref.shape[1] - extra, extra)]
    small_copy = pltpu.make_async_copy(ends, tails, small_sem)
    small_copy.start()
    subs, order, width = p_ref.shape
    wide = 2 * STRIDE
    square_copies, corner_copies, strip_copies = {}, {}, {}

    def fetch(s, rows, columns, sem):
        part = (s, rows, columns)
        copy = pltpu.make_async_copy(far_ref.at[part], f_ref.at[part], sem)
        copy.start()
        return copy

    for step, a in enumerate(range(0, order, STRIDE)):
        for s in range(subs):
            square_copies[s, a] = fetch(s, pl.ds(a, STRIDE), pl.ds(a, STRIDE), square_sems.at[s, step])
    for step, a in enumerate(range(0, order, wide)):
        for s in range(subs):
            corner_copies[s, a] = fetch(s, pl.ds(a + STRIDE, STRIDE), pl.ds(a, STRIDE), corner_sems.at[s, step])
    panel_copy = pltpu.make_async_copy(p_ref, rest, panel_sem)
    panel_copy.start()
    for step, a in enumerate(range(0, order - wide, wide)):
        for s in range(subs):
            strip_copies[s, a] = fetch(s, pl.ds(a + wide, order - a - wide), pl.ds(a, wide), strip_sems.at[s, step])
    small_copy.wait()
    lines = subs // 2
    lives = [tails[0, lines + s:lines + s + 1].astype(jnp.int32) for s in range(subs)]
    row = iota((STRIDE, STRIDE), 0)
    col = iota((STRIDE, STRIDE), 1)
    prow = iota((wide, width), 0)
    dims = (((0,), (0,)), ((), ()))
    squares = [jnp.zeros((width, width), F32)] * subs
    crosses = [jnp.zeros((width, width), F32)] * subs
    places = [(s, a) for a in range(0, order, STRIDE) for s in range(subs)]
    small = {}
    for first in range(0, len(places), BATCH):
        batch = places[first:first + BATCH]
        blocks = []
        for s, a in batch:
            square_copies[s, a].wait()
            d = f_ref[s, a:a + STRIDE, a:a + STRIDE]
            keep = (row + a < lives[s][:, :STRIDE]) & (col <= row)
            blocks.append(jnp.where(keep, d, (row == col).astype(F32)))
        for place, inverse in zip(batch, invert_blocks(blocks)):
            small[place] = split(inverse)
    heads = [(s, a) for a in range(0, order, wide) for s in range(subs)]
    corners = []
    for s, a in heads:
        b = a + STRIDE
        corner_copies[s, a].wait()
        corner = jnp.where(row + b < lives[s][:, :STRIDE], f_ref[s, b:b + STRIDE, a:b], 0.0)
        corners.append(split(mmk(split(corner), small[s, a])))
    inverses = {}
    for (s, a), corner in zip(heads, corners):
        above, below = small[s, a], small[s, a + STRIDE]
        turned = split(-mmk(below, corner))
        blank = jnp.zeros((STRIDE, STRIDE), BF)
        inverses[s, a] = [
            jnp.concatenate([jnp.concatenate([u, blank], axis=1), jnp.concatenate([t, l], axis=1)], axis=0)
            for u, t, l in zip(above, turned, below)
        ]

    capacity = 2 * width // members
    glue = jnp.concatenate([tails[0, :lines], tails[1, :lines]], axis=0).astype(jnp.int32)
    place = lax.axis_index("member")
    before = (iota((width, width), 0) < iota((width, width), 1)).astype(BF)
    dispatches = []
    for s in range(subs):
        owner = glue[s:s + 1] // (NDUAL // members)
        owners = (iota((members, width), 0) == owner)
        ranks = mm(owners.astype(BF), before)
        rank = jnp.sum(jnp.where(owners, ranks, 0.0), axis=0, keepdims=True).astype(jnp.int32)
        target = (owner ^ place) * capacity + rank
        dispatches.append((iota((members * capacity, width), 0) == target).astype(BF))
    panel_copy.wait()
    for a in range(0, order, wide):
        solved = []
        for s in range(subs):
            now = jnp.where(prow + a < lives[s], rest[s, a:a + wide], 0.0)
            solved.append(split(mm3(inverses[s, a], split(now))))
        if a + wide < order:
            for s in range(subs):
                strip_copies[s, a].wait()
        for c in range(a + wide, order, wide):
            for s in range(subs):
                rest[s, c:c + wide] = rest[s, c:c + wide] - mm3(split(f_ref[s, c:c + wide, a:a + wide]), solved[s])
        for s in range(subs):
            hi, lo = solved[s]
            squares[s] = squares[s] + mm(hi, hi, dims)
            crosses[s] = crosses[s] + mm(hi, lo, dims)
    duals = [split(squares[s] + (crosses[s] + crosses[s].T)) for s in range(subs)]
    for s in range(subs):
        values = mm(dispatches[s], duals[s][0]) + mm(dispatches[s], duals[s][1])
        for k in range(members):
            out_refs[k][s * capacity:(s + 1) * capacity] = values[k * capacity:(k + 1) * capacity]


def solve(packed, factors, panels, members):
    subs, order, width = panels.shape
    capacity = 2 * width // members
    vm = pl.BlockSpec(memory_space=pltpu.VMEM)
    far = pl.BlockSpec(memory_space=pltpu.HBM)
    return pl.pallas_call(
        functools.partial(solve_kernel, members),
        out_shape=[jax.ShapeDtypeStruct((subs * capacity, width), F32)] * members,
        in_specs=[far] * 3,
        out_specs=[vm] * members,
        scratch_shapes=[
            pltpu.VMEM((subs, order, width), F32),
            pltpu.VMEM((subs, order, order), F32),
            pltpu.VMEM((2, tail_rows(subs), width), F32),
            pltpu.SemaphoreType.DMA((subs, order // STRIDE)),
            pltpu.SemaphoreType.DMA((subs, order // (2 * STRIDE))),
            pltpu.SemaphoreType.DMA((subs, order // (2 * STRIDE))),
            pltpu.SemaphoreType.DMA,
            pltpu.SemaphoreType.DMA,
        ],
        compiler_params=pltpu.CompilerParams(vmem_limit_bytes=52 << 20),
        cost_estimate=pl.CostEstimate(flops=10_000_000_000, bytes_accessed=8 << 20, transcendentals=0),
        name="solve",
    )(packed, factors, panels)


def tail_rows(subs):
    return 8 * (-(-(subs // 2 + subs) // 8))


def pack_kernel(loads_ref, glue_ref, sizes_ref, out_ref, held, lines_of, sizes_of, tail, in_sems, load_sems, tail_sems):
    members, rows, nrhs = out_ref.shape
    subs = glue_ref.shape[0]
    half, lines = loads_ref.shape[0] // 2, subs // 2
    labels = pltpu.make_async_copy(glue_ref, lines_of, in_sems.at[0])
    load = pltpu.make_async_copy(loads_ref, held, in_sems.at[1])
    sizes = pltpu.make_async_copy(sizes_ref, sizes_of, in_sems.at[2])
    labels.start()
    sizes.start()
    load.start()
    labels.wait()
    sizes.wait()
    lives = [jnp.full((1, nrhs), sizes_of[s], jnp.int32).astype(F32) for s in range(subs)]
    blank = [jnp.zeros((rows - half - lines - subs, nrhs), F32)]
    for part in range(2):
        line = lines_of[part * lines:(part + 1) * lines].astype(F32)
        tail[part] = jnp.concatenate([line, *lives, *blank], axis=0)
    copies = []
    for k in range(members):
        copies.append(pltpu.make_async_copy(tail.at[k % 2], out_ref.at[k, pl.ds(half, rows - half)], tail_sems.at[k]))
        copies[-1].start()
    load.wait()
    for k in range(members):
        rows_of = held.at[pl.ds(k % 2 * half, half)]
        copies.append(pltpu.make_async_copy(rows_of, out_ref.at[k, pl.ds(0, half)], load_sems.at[k]))
        copies[-1].start()
    for copy in copies:
        copy.wait()


def pack(loads, glue, sizes, members):
    subs = glue.shape[0]
    share, nrhs = loads.shape
    rows = share // 2 + tail_rows(subs)
    far = pl.BlockSpec(memory_space=pltpu.HBM)
    return pl.pallas_call(
        pack_kernel,
        out_shape=jax.ShapeDtypeStruct((members, rows, nrhs), F32),
        in_specs=[far] * 3,
        out_specs=far,
        scratch_shapes=[
            pltpu.VMEM((share, nrhs), F32),
            pltpu.VMEM(glue.shape, jnp.int32),
            pltpu.SMEM(sizes.shape, jnp.int32),
            pltpu.VMEM((2, rows - share // 2, nrhs), F32),
            pltpu.SemaphoreType.DMA((3,)),
            pltpu.SemaphoreType.DMA((members,)),
            pltpu.SemaphoreType.DMA((members,)),
        ],
        compiler_params=pltpu.CompilerParams(vmem_limit_bytes=58 << 20),
        cost_estimate=pl.CostEstimate(flops=1_000_000, bytes_accessed=1 << 20, transcendentals=0),
        name="pack",
    )(loads, glue, sizes)


def routes_kernel(subs, place_ref, own_ref, twin_ref, stand_ref, label_ref, high_ref, low_ref):
    members, block, width = own_ref.shape
    share = NDUAL // members
    half, lines = share // 2, subs // 2
    slots = label_ref.shape[1]
    capacity = slots // subs
    first_core = place_ref[0] % 2 == 0
    glue = []
    for k in range(members):
        source = place_ref[0] ^ k
        pair = own_ref[source], twin_ref[source]
        for part in range(2):
            got = jnp.where(first_core, pair[part], pair[1 - part])
            row = pl.ds(pl.multiple_of(source * share + part * half, half), half)
            high_ref[row], low_ref[row] = split(got[:half])
            glue.append(got[half:half + lines])
    glue = jnp.concatenate(glue, axis=0)
    stand_ref[...] = glue.T.astype(jnp.int32)
    glue = glue.astype(jnp.int32)
    first = place_ref[0] * share
    mine = (glue >= first) & (glue < first + share)
    before = (iota((width, width), 0) < iota((width, width), 1)).astype(BF)
    ranks = mm(mine.astype(BF), before).astype(jnp.int32)
    local = jnp.where(mine, glue - first + 1, 0).astype(F32).astype(BF)
    labels = []
    for k in range(members):
        found = jnp.full((1, slots), -1.0, F32)
        for s in range(subs):
            i = k * subs + s
            rank = jnp.where(mine[i:i + 1], ranks[i:i + 1] + s * capacity, -1)
            at_slot = (iota((slots, width), 0) == rank).astype(BF)
            line = mm(local[i:i + 1], at_slot, (((1,), (1,)), ((), ())))
            found = jnp.where(line > 0.5, line + (s * share - 1), found)
        labels.append(found)
    label_ref[...] = jnp.concatenate(labels, axis=0).astype(jnp.int32)


def placed(subs, sources, label_ref, stand_ref, values):
    slots, width = values[0].shape
    share = NDUAL // label_ref.shape[0]
    total = jnp.zeros((2 * share, NDUAL), F32)
    for k, value in zip(sources, values):
        rows = (iota((subs * share, slots), 0) == label_ref[k:k + 1]).astype(BF)
        moved = mm(rows, jnp.concatenate(split(value[...]), axis=1)).astype(BF)
        for s in range(subs):
            i = k * subs + s
            part = moved[s * share:(s + 1) * share]
            columns = (iota((width, NDUAL), 1) == stand_ref[:, i:i + 1]).astype(BF)
            total = total + mm(jnp.concatenate([part[:, :width], part[:, width:]], axis=0), columns)
    return total[:share] + total[share:]


def early_kernel(subs, sources, label_ref, stand_ref, *refs):
    refs[-1][...] = placed(subs, sources, label_ref, stand_ref, refs[:-1])


def finish_kernel(subs, sources, label_ref, stand_ref, high_ref, low_ref, early_ref, *refs):
    values, (dual_ref, raw_ref, first_ref, last_ref) = refs[:-4], refs[-4:]
    dual = early_ref[...] + placed(subs, sources, label_ref, stand_ref, values)
    dual_ref[...] = dual
    raw = mm3(split(dual), (high_ref[...], low_ref[...]))
    raw_ref[...] = raw
    first_ref[...] = raw[:IFACE]
    last_ref[...] = raw[raw.shape[0] - IFACE:]


def call(kernel, outs, args, flops, name, smem=0):
    vm = pl.BlockSpec(memory_space=pltpu.VMEM)
    specs = [pl.BlockSpec(memory_space=pltpu.SMEM)] * smem + [vm] * (len(args) - smem)
    return pl.pallas_call(
        kernel,
        out_shape=outs,
        in_specs=specs,
        out_specs=jax.tree.map(lambda _: vm, outs),
        compiler_params=pltpu.CompilerParams(vmem_limit_bytes=16 << 20),
        cost_estimate=pl.CostEstimate(flops=flops, bytes_accessed=4 << 20, transcendentals=0),
        name=name,
    )(*args)


def on_device(factors, panels, sizes, glue_index, loads):
    members = lax.axis_size("member")
    subs, order, width = panels.shape
    share, nrhs = loads.shape
    capacity = 2 * width // members
    slots = subs * capacity
    count = members * subs
    shape = jax.ShapeDtypeStruct
    place = lax.axis_index("member").astype(jnp.int32).reshape(1)

    def across(value, distance):
        return lax.ppermute(value, "member", [(i, i ^ distance) for i in range(members)])

    packed = pack(loads, glue_index, sizes, members)
    own = lax.all_to_all(packed, "member", split_axis=0, concat_axis=0, tiled=True)
    values = solve(packed, factors, panels, members)
    own, *values = lax.optimization_barrier((own, *values))
    distances = [*range(2, members, 2), *range(3, members, 2), 1]
    arrived = {0: values[0], **{k: across(values[k], k) for k in distances}}
    last_ones = distances[-2:-1]
    first_ones = [k for k in arrived if k not in last_ones]
    twin = across(own, 1)
    stand, labels, high, low = call(
        functools.partial(routes_kernel, subs),
        (
            shape((width, count), jnp.int32),
            shape((members, slots), jnp.int32),
            shape((NDUAL, nrhs), BF),
            shape((NDUAL, nrhs), BF),
        ),
        (place, own, twin),
        2_000_000_000,
        "routes",
        smem=1,
    )
    early = call(
        functools.partial(early_kernel, subs, first_ones),
        shape((share, NDUAL), F32),
        (labels, stand, *[arrived[k] for k in first_ones]),
        2_000_000_000,
        "early",
    )
    dual_rows, raw, first, last = call(
        functools.partial(finish_kernel, subs, last_ones),
        (
            shape((share, NDUAL), F32),
            shape((share, nrhs), F32),
            shape((IFACE, nrhs), F32),
            shape((IFACE, nrhs), F32),
        ),
        (labels, stand, high, low, early, *[arrived[k] for k in last_ones]),
        3_000_000_000,
        "finish",
    )
    peers = lax.axis_size("cluster")
    up = [(i, (i + 1) % peers) for i in range(peers)]
    down = [(j, i) for i, j in up]
    before = lax.ppermute(last, "cluster", up)
    after = lax.ppermute(first, "cluster", down)
    between = jnp.zeros((share - 2 * IFACE, nrhs), F32)
    products = raw + jnp.concatenate([before, between, after], axis=0)
    return (dual_rows, products)


def solution(mesh):
    shards = ("cluster", "member")
    return jax.shard_map(
        on_device,
        mesh=mesh,
        in_specs=(P(shards, None, None), P(shards, None, None), P(shards), P(shards, None), P(shards, None)),
        out_specs=(P(shards, None), P(shards, None)),
        check_vma=False,
    )
```
